32 devices in a mesh: beam: 8 (over z, x), head: 4 (over y, core).
Axes of the slice: x: 2, y: 2, z: 4, core: 2. Of those that a mesh axis runs over, the one named last changes fastest.
Arguments:
- hidden: bfloat16 [4, 16, 8, 8192], P(None, 'beam'), may hold values from -6 to 6
- w_qkv: bfloat16 [8192, 10240], P('beam', 'head'), may hold values from -0.0625 to 0.0625
- qkv_bias: float32 [10240], P('head'), may hold values from -3 to 3
- prompt_keys: bfloat16 [8, 8, 16384, 128], P('beam', 'head'), may hold values from -16.125 to 16.125
- prompt_values: bfloat16 [8, 8, 16384, 128], P('beam', 'head'), may hold values from -12 to 12
- suffix_keys: bfloat16 [16, 8, 8, 512, 128], P('beam', None, 'head'), may hold values from -10 to 10
- suffix_values: bfloat16 [16, 8, 8, 512, 128], P('beam', None, 'head'), may hold values from -12 to 12
- w_out: bfloat16 [8192, 8192], P('head', 'beam'), may hold values from -0.0625 to 0.0625
- parents: int32 [4, 16, 8], replicated, may hold values from 0 to 15
- lengths: int32 [16, 8], replicated, may hold values from 1 to 508
Outputs:
- attended: bfloat16 [4, 16, 8, 8192], P(None, None, 'head', 'beam')
The draws below stay inside these ranges and needn't reach their ends.
All inputs are finite; a program needn't handle non-finite values.
Results may differ from the reference program's by a relative error of at most 0.03.
Values may be sent and summed in bfloat16 or wider, within the bound.
No kernel may reach another device: no remote copies, remote signals or barrier semaphores. Data moves between devices by JAX's collectives and lax.ppermute only.
A program may use at most 320 MiB of HBM per device.

```python
import math
import jax
import jax.numpy as jnp
import numpy as np
from jax import lax

D = 8192
HQ = 64
KVH = 8
HD = 128
GROUP = 8
WIDTH = 16
PROMPTS = 8
PLEN = 16384
SUF = 512
STEPS = 4


def shared_pattern(key):
    return jax.random.randint(key, (KVH, HD), 0, 2).astype(jnp.float32) * 2.0 - 1.0


def draw_qkv_bias(key, part):
    pattern = shared_pattern(key)
    key = jax.random.fold_in(key, 11)
    key_one, key_two, key_three, key_four = jax.random.split(key, 4)
    rough = jnp.clip(0.25 * jax.random.normal(key_one, (KVH, GROUP + 1, HD), jnp.float32), -1.0, 1.0)
    query_strength = jax.random.uniform(key_two, (KVH, GROUP, 1), jnp.float32, 0.8, 1.2)
    key_strength = jax.random.uniform(key_three, (KVH, 1, 1), jnp.float32, 0.9, 1.3)
    value_bias = jnp.clip(0.5 * jax.random.normal(key_four, (KVH, 1, HD), jnp.float32), -2.0, 2.0)
    query_bias = query_strength * pattern[:, None, :] + rough[:, :GROUP, :]
    key_bias = key_strength * pattern[:, None, :] + rough[:, GROUP:, :]
    combined = jnp.concatenate([query_bias, key_bias, value_bias], axis=1)
    return combined.reshape(-1)


def draw_prompt_keys(key, part):
    key = jax.random.fold_in(key, 23)
    key_one = jax.random.fold_in(key, 0)
    draw_base = jnp.clip(1.5 * jax.random.normal(key_one, (PROMPTS, KVH, PLEN, HD), jnp.float32), -6.0, 6.0)
    return draw_base.astype(jnp.bfloat16)


def draw_lengths(key, part):
    key = jax.random.fold_in(key, 37)
    key_one, key_two, key_three = jax.random.split(key, 3)
    drawn = jax.random.randint(key_one, (WIDTH, PROMPTS), 1, SUF - STEPS + 1)
    chosen_row = jax.random.randint(key_two, (), 0, WIDTH)
    chosen_col = jax.random.randint(key_three, (), 0, PROMPTS)
    chosen_cell = (jnp.arange(WIDTH)[:, None] == chosen_row) & (jnp.arange(PROMPTS)[None, :] == chosen_col)
    return jnp.where(chosen_cell, SUF - STEPS, drawn).astype(jnp.int32)


def place_ends(array, stream_key, smallest, largest):
    spot = [jax.random.randint(jax.random.fold_in(stream_key, axis), (), 0, length) for axis, length in enumerate(array.shape)]
    longest = array.shape.index(max(array.shape))
    next_to = spot[:longest] + [(spot[longest] + 1) % array.shape[longest]] + spot[longest + 1:]
    return array.at[tuple(spot)].set(smallest).at[tuple(next_to)].set(largest)


def block_levels(own_key, dims, pieces, smallest, high):
    level = 1.0
    for dim, parts in pieces:
        steps = jax.random.uniform(jax.random.fold_in(jax.random.fold_in(own_key, 6), dim), (parts,), jnp.float32, smallest / len(pieces), high / len(pieces))
        level = level * jnp.repeat(jnp.exp(steps), dims[dim] // parts).reshape((-1,) + (1,) * (len(dims) - 1 - dim))
    return level


def rank_table(count, skew):
    weights = [(1 << 20) // math.isqrt(rank ** skew) + 1 for rank in range(1, count + 1)]
    scale = 1 + sum(weights) // (1 << 30)
    return np.cumsum(np.array([max(1, weight // scale) for weight in weights]))


def skewed_ids(key, dims, count, skew):
    listing = rank_table(count, skew)
    ticket = jax.random.randint(jax.random.fold_in(key, 1), dims, 0, int(listing[count - 1]))
    rank = jnp.searchsorted(jnp.asarray(listing, jnp.int32), ticket, side="right")
    return jax.random.permutation(jax.random.fold_in(key, 2), count)[rank].astype(jnp.int32)


def normal_values(key, extent, spread, bound, pieces=(), kind=jnp.bfloat16):
    result = jax.random.normal(key, extent, jnp.float32) * spread
    if len(pieces) > 0:
        result = block_levels(key, extent, pieces, -0.22, 0.18) * result
    return jnp.clip(result, min=-bound, max=bound).astype(kind)


def setup_inputs(seed: int = 0) -> dict:
    key_list = jax.random.split(jax.random.key(seed), 11)
    hidden = normal_values(key_list[0], (STEPS, WIDTH, PROMPTS, D), 1.0, 6.0, ((1, 8),))
    w_qkv = normal_values(key_list[1], (D, KVH * (GROUP + 2) * HD), D ** -0.5, 0.0625, ((0, 8), (1, 4)))
    qkv_bias = draw_qkv_bias(jax.random.fold_in(key_list[10], 71), 0)
    prompt_keys = draw_prompt_keys(jax.random.fold_in(key_list[10], 71), 0)
    prompt_values = normal_values(key_list[4], (PROMPTS, KVH, PLEN, HD), 3.0, 12.0, ((0, 8), (1, 4)))
    suffix_keys = normal_values(key_list[5], (WIDTH, PROMPTS, KVH, SUF, HD), 2.5, 10.0, ((0, 8), (2, 4)))
    suffix_values = normal_values(key_list[6], (WIDTH, PROMPTS, KVH, SUF, HD), 3.0, 12.0, ((0, 8), (2, 4)))
    w_out = normal_values(key_list[7], (HQ * HD, D), (HQ * HD) ** -0.5, 0.0625, ((0, 4), (1, 8)))
    parents = place_ends(skewed_ids(key_list[8], (STEPS, WIDTH, PROMPTS), WIDTH, 2), jax.random.fold_in(key_list[8], 3), 0, WIDTH - 1).astype(jnp.int32)
    lengths = draw_lengths(jax.random.fold_in(key_list[10], 71), 0)
    return dict(hidden=hidden, w_qkv=w_qkv, qkv_bias=qkv_bias, prompt_keys=prompt_keys, prompt_values=prompt_values, suffix_keys=suffix_keys, suffix_values=suffix_values, w_out=w_out, parents=parents, lengths=lengths)


rope_base = 1000000.0
masked_score = -1e30


def rotate(vectors, positions):
    half_size = vectors.shape[-1] // 2
    frequency = rope_base ** (-(jnp.arange(half_size, dtype=jnp.float32) * 2.0 / vectors.shape[-1]))
    angles = positions.astype(jnp.float32)[..., None] * frequency
    cosine = jnp.cos(angles)
    sine_part = jnp.sin(angles)
    lower_half = vectors[..., :half_size]
    upper_half = vectors[..., half_size:]
    return jnp.concatenate([lower_half * cosine - upper_half * sine_part, upper_half * cosine + lower_half * sine_part], axis=-1)


def lineage(parents):
    step_count = parents.shape[0]
    slot_ids = jnp.broadcast_to(jnp.arange(parents.shape[1], dtype=jnp.int32)[:, None], parents.shape[1:])
    chain_list = []
    root_list = []
    for current_step in range(step_count):
        chain_links = [slot_ids] * step_count
        current = slot_ids
        for later_step in range(current_step, 0, -1):
            current = jnp.take_along_axis(parents[later_step], current, axis=0)
            chain_links[later_step - 1] = current
        root_list.append(jnp.take_along_axis(parents[0], current, axis=0))
        chain_list.append(jnp.stack(chain_links))
    return jnp.stack(chain_list), jnp.stack(root_list)


def base_lengths(lengths, roots):
    return jax.vmap(lambda chosen: jnp.take_along_axis(lengths, chosen, axis=0))(roots)


def reference(hidden, w_qkv, qkv_bias, prompt_keys, prompt_values, suffix_keys, suffix_values, w_out, parents, lengths):
    projected = jnp.dot(hidden.reshape(-1, D), w_qkv, preferred_element_type=jnp.float32) + qkv_bias
    projected = projected.reshape(STEPS, WIDTH, PROMPTS, KVH, GROUP + 2, HD)
    chains, roots = lineage(parents)
    starts = base_lengths(lengths, roots)
    positions = PLEN + starts + jnp.arange(STEPS, dtype=jnp.int32)[:, None, None]
    queries = rotate(projected[..., :GROUP, :], jnp.broadcast_to(positions[..., None, None], (STEPS, WIDTH, PROMPTS, KVH, GROUP))).astype(jnp.bfloat16)
    fresh_keys = rotate(projected[..., GROUP, :], jnp.broadcast_to(positions[..., None], (STEPS, WIDTH, PROMPTS, KVH))).astype(jnp.bfloat16)
    fresh_values = projected[..., GROUP + 1, :].astype(jnp.bfloat16)
    score_scale = HD ** -0.5
    section_ids = jnp.arange(STEPS, dtype=jnp.int32)
    fresh_ok = (section_ids[None, :] <= section_ids[:, None])[:, None, None, None, :]
    suffix_ids = jnp.arange(SUF, dtype=jnp.int32)

    def one_prompt(prompt):
        query_rows = queries[:, :, prompt].astype(jnp.float32)
        own_roots = roots[:, :, prompt]
        prompt_scores = jnp.einsum('swngh,nlh->swngl', query_rows, prompt_keys[prompt].astype(jnp.float32)) * score_scale
        picked_keys = suffix_keys[:, prompt][own_roots]
        picked_values = suffix_values[:, prompt][own_roots]
        suffix_scores = jnp.einsum('swngh,swnjh->swngj', query_rows, picked_keys.astype(jnp.float32)) * score_scale
        suffix_ok = (suffix_ids[None, None, :] < starts[:, :, prompt][..., None])[:, :, None, None, :]
        lineage_ids = chains[:, :, :, prompt]
        newest_keys = fresh_keys[:, :, prompt][section_ids[None, :, None], lineage_ids]
        newest_values = fresh_values[:, :, prompt][section_ids[None, :, None], lineage_ids]
        fresh_scores = jnp.einsum('swngh,stwnh->swngt', query_rows, newest_keys.astype(jnp.float32)) * score_scale
        joined = jnp.concatenate([prompt_scores, jnp.where(suffix_ok, suffix_scores, masked_score), jnp.where(fresh_ok, fresh_scores, masked_score)], axis=-1)
        row_peak = jnp.max(joined, axis=-1, keepdims=True)
        weights = jnp.exp(joined - row_peak)
        weight_sum = jnp.sum(weights, axis=-1)
        rounded = lax.optimization_barrier(weights.astype(jnp.bfloat16)).astype(jnp.float32)
        mixture = jnp.einsum('swngl,nlh->swngh', rounded[..., :PLEN], prompt_values[prompt].astype(jnp.float32))
        mixture = mixture + jnp.einsum('swngj,swnjh->swngh', rounded[..., PLEN:PLEN + SUF], picked_values.astype(jnp.float32))
        mixture = mixture + jnp.einsum('swngt,stwnh->swngh', rounded[..., PLEN + SUF:], newest_values.astype(jnp.float32))
        return (mixture / weight_sum[..., None]).astype(jnp.bfloat16)

    contexts = lax.map(one_prompt, jnp.arange(PROMPTS, dtype=jnp.int32))
    flattened = jnp.transpose(contexts, (1, 2, 0, 3, 4, 5)).reshape(STEPS * WIDTH * PROMPTS, HQ * HD)
    attended = jnp.dot(flattened, w_out, preferred_element_type=jnp.float32)
    return attended.reshape(STEPS, WIDTH, PROMPTS, D).astype(jnp.bfloat16)
```

```python
import functools

import jax
import jax.numpy as jnp
from jax import lax
from jax.experimental import pallas as pl
from jax.experimental.pallas import tpu as pltpu
from jax.sharding import PartitionSpec as P

rope_base = 1000000.0
masked_score = -1e30
log2e = 1.4426950408889634
group = 8
bf16 = jnp.bfloat16
f32 = jnp.float32
key_block = 2048
pieces = 4
tile_units = 16


def params(vmem_mib=48):
    return pltpu.CompilerParams(vmem_limit_bytes=vmem_mib << 20)


def whole(shape):
    return pl.BlockSpec(shape, lambda *_: (0,) * len(shape))


def ring_order(count):
    return list(range(0, count, 2)) + list(range(count - 1, 0, -2))


def ring_pairs(count):
    order = ring_order(count)
    forward = [(order[i], order[(i + 1) % count]) for i in range(count)]
    return forward, [(b, a) for a, b in forward]


def ring_place(index, count):
    return jnp.where(index % 2 == 0, index // 2, count - 1 - index // 2)


def ring_member(place, count):
    return jnp.where(place < count // 2, 2 * place, 2 * (count - 1 - place) + 1)


def gather_ring(block, count):
    forward, backward = ring_pairs(count)
    middle = count // 2
    half = block.shape[0] // 2
    found = [None] * count
    found[0] = block
    ahead = behind = block
    for step in range(1, middle):
        ahead = lax.ppermute(ahead, "beam", forward)
        behind = lax.ppermute(behind, "beam", backward)
        found[count - step] = ahead
        found[step] = behind
    found[middle] = (
        lax.ppermute(ahead[:half], "beam", forward),
        lax.ppermute(behind[half:], "beam", backward),
    )
    return found


def scatter_ring(blocks, count):
    forward, backward = ring_pairs(count)
    middle = count // 2
    ahead, behind = blocks[middle]
    half = ahead.shape[0]
    for step in range(middle - 1, -1, -1):
        ahead = lax.ppermute(ahead, "beam", forward)
        behind = lax.ppermute(behind, "beam", backward)
        if step == 0:
            break
        front = blocks[step].astype(f32)
        back = blocks[count - step].astype(f32)
        ahead = ahead.astype(f32)
        behind = behind.astype(f32)
        if step == middle - 1:
            ahead = jnp.concatenate([ahead + front[:half], front[half:]])
            behind = jnp.concatenate([back[:half], behind + back[half:]])
        else:
            ahead = ahead + front
            behind = behind + back
        ahead = ahead.astype(bf16)
        behind = behind.astype(bf16)
    return ahead, behind


def flat(found):
    listed = []
    for block in found:
        listed.extend(block if isinstance(block, tuple) else (block,))
    return listed


def lineage_kernel(parents_ref, lengths_ref, roots_ref, starts_ref, chain_ref):
    steps, width, prompts = parents_ref.shape

    def take(table, chosen):
        out = jnp.zeros_like(chosen)
        for j in range(width):
            out = jnp.where(chosen == j, table[j : j + 1, :], out)
        return out

    own = lax.broadcasted_iota(jnp.int32, (width, prompts), 0)
    lengths = lengths_ref[...]
    for s in range(steps):
        current = own
        for t in range(steps - 1, s, -1):
            chain_ref[s, t] = own - width
        chain_ref[s, s] = own
        for t in range(s, 0, -1):
            current = take(parents_ref[t], current)
            chain_ref[s, t - 1] = current
        root = take(parents_ref[0], current)
        roots_ref[s] = root
        starts_ref[s] = take(lengths, root)


def lineage_tables(parents, lengths):
    steps, width, prompts = parents.shape
    return pl.pallas_call(
        lineage_kernel,
        out_shape=(
            jax.ShapeDtypeStruct((steps, width, prompts), jnp.int32),
            jax.ShapeDtypeStruct((steps, width, prompts), jnp.int32),
            jax.ShapeDtypeStruct((steps, steps, width, prompts), jnp.int32),
        ),
        compiler_params=params(),
        name="lineage",
    )(parents, lengths)


def split_kernel(core_ref, x_ref, o_ref):
    o_ref[0] = x_ref[...]


def split_hidden(hidden, core, count):
    rows, width = hidden.shape
    half, part = rows // 2, width // count
    return pl.pallas_call(
        split_kernel,
        grid_spec=pltpu.PrefetchScalarGridSpec(
            num_scalar_prefetch=1,
            grid=(count,),
            in_specs=[pl.BlockSpec((half, part), lambda i, core: (core[0], i))],
            out_specs=pl.BlockSpec((1, half, part), lambda i, core: (i, 0, 0)),
        ),
        out_shape=jax.ShapeDtypeStruct((count, half, part), bf16),
        compiler_params=params(),
        name="split_hidden",
    )(core, hidden)


def project_kernel(count, prompts, local, info_ref, mine_ref, other_ref, w_ref, *refs):
    outs, x_ref = refs[:-1], refs[-1]
    half = mine_ref.shape[1]
    units = 2 * half * count // prompts
    total = 2 * half * count

    @pl.when(pl.program_id(0) == 0)
    def _():
        part = mine_ref.shape[2]
        x = jnp.concatenate(
            [mine_ref[...].reshape(count * half, part), other_ref[...].reshape(count * half, part)]
        )
        i = lax.broadcasted_iota(jnp.int32, (total, total), 1)
        t = lax.broadcasted_iota(jnp.int32, (total, total), 0)
        core = info_ref[0]
        place = info_ref[1]
        second = i // (count * half)
        source = (i // half) % count
        row = i % half + half * jnp.where(second == 0, core, 1 - core)
        prompt = row % prompts
        unit = source * (2 * half // prompts) + row // prompts
        target = ((ring_place(prompt, count) - place + count) % count) * units + unit
        perm = jnp.where(t == target, 1.0, 0.0).astype(bf16)
        x_ref[...] = jnp.dot(perm, x, preferred_element_type=f32).astype(bf16)

    y = jnp.dot(x_ref[...], w_ref[...], preferred_element_type=f32)
    at = 0
    for j in range(count):
        block = y[j * units : (j + 1) * units]
        if j == count // 2:
            outs[at][...] = block[: units // 2].astype(bf16)
            outs[at + 1][...] = block[units // 2 :].astype(bf16)
            at += 2
        else:
            outs[at][...] = block
            at += 1


def project(info, mine, other, w, head, local, prompts):
    count, half, part = mine.shape
    columns = w.shape[1] // local
    step = 256
    units = 2 * half * count // prompts
    middle = count // 2
    shapes, specs = [], []
    for j in range(count):
        if j == middle:
            shapes += [jax.ShapeDtypeStruct((units // 2, columns), bf16)] * 2
            specs += [pl.BlockSpec((units // 2, step), lambda i, info: (0, i))] * 2
        else:
            shapes.append(jax.ShapeDtypeStruct((units, columns), f32))
            specs.append(pl.BlockSpec((units, step), lambda i, info: (0, i)))
    outs = pl.pallas_call(
        functools.partial(project_kernel, count, prompts, local),
        grid_spec=pltpu.PrefetchScalarGridSpec(
            num_scalar_prefetch=1,
            grid=(columns // step,),
            in_specs=[
                whole(mine.shape),
                whole(other.shape),
                pl.BlockSpec((part, step), lambda i, info: (0, head * (columns // step) + i)),
            ],
            out_specs=specs,
            scratch_shapes=[pltpu.VMEM((2 * half * count, part), bf16)],
        ),
        out_shape=shapes,
        compiler_params=params(),
        cost_estimate=pl.CostEstimate(
            flops=2 * units * count * part * columns, bytes_accessed=6 << 20, transcendentals=0
        ),
        name="project",
    )(info, mine, other, w)
    blocks = list(outs[:middle]) + [(outs[middle], outs[middle + 1])] + list(outs[middle + 2 :])
    return blocks


def rotate_kernel(own_ref, front_ref, back_ref, bias_ref, cos_ref, sin_ref, q_ref, k_ref, v_ref):
    x = own_ref[...] + front_ref[...].astype(f32) + back_ref[...].astype(f32) + bias_ref[...]
    cosine, sine = cos_ref[...], sin_ref[...]
    scale = log2e * 128**-0.5
    for g in range(group + 1):
        part = x[:, g * 128 : (g + 1) * 128]
        turned = part * cosine + pltpu.roll(part, 64, 1) * sine
        if g < group:
            q_ref[:, g * 128 : (g + 1) * 128] = (turned * scale).astype(bf16)
        else:
            k_ref[...] = turned.astype(bf16)
    v_ref[...] = x[:, (group + 1) * 128 :].astype(bf16)


def rotate(own, front, back, bias, cosine, sine):
    units = own.shape[0]
    return pl.pallas_call(
        rotate_kernel,
        out_shape=(
            jax.ShapeDtypeStruct((units, group * 128), bf16),
            jax.ShapeDtypeStruct((units, 128), bf16),
            jax.ShapeDtypeStruct((units, 128), bf16),
        ),
        compiler_params=params(),
        name="rotate",
    )(own, front, back, bias, cosine, sine)


def dot_nt(a, b):
    return lax.dot_general(a, b, (((1,), (1,)), ((), ())), preferred_element_type=f32)


def prompt_kernel(local, first, *refs):
    q_refs = refs[:local]
    refs = refs[local:]
    if first:
        kf_refs, vf_refs, bias_ref = refs[:local], refs[local : 2 * local], refs[2 * local]
        refs = refs[2 * local + 1 :]
    else:
        old_acc, old_peak = refs[:2]
        refs = refs[2:]
    k_ref, v_ref, acc, peak, rows_ref = refs
    units = q_refs[0].shape[0]
    rows = group * units
    block = k_ref.shape[2]

    @pl.when(pl.program_id(0) == 0)
    def _():
        for n in range(local):
            for g in range(group):
                rows_ref[n, g * units : (g + 1) * units] = q_refs[n][:, g * 128 : (g + 1) * 128]
            if first:
                bias = jnp.concatenate([bias_ref[...]] * group)
                s = dot_nt(rows_ref[n], kf_refs[n][...]) + bias
                top = jnp.max(s, axis=1, keepdims=True)
                p = jnp.exp2(s - top).astype(bf16)
                v = jnp.concatenate([vf_refs[n][...], jnp.ones((units, 128), bf16)], axis=1)
                acc[n] = jnp.dot(p, v, preferred_element_type=f32)
                peak[n] = jnp.broadcast_to(top, (rows, 128))
            else:
                acc[n] = old_acc[n]
                peak[n] = old_peak[n]

    ones = jnp.ones((block, 128), bf16)
    cut = rows // 4
    for r in range(4):
        for n in range(local):
            at = slice(r * cut, (r + 1) * cut)
            s = dot_nt(rows_ref[n, at], k_ref[0, n])
            before = peak[n, at]
            now = jnp.maximum(before, jnp.max(s, axis=1, keepdims=True))
            peak[n, at] = now
            p = jnp.exp2(s - jnp.concatenate([now] * (block // 128), axis=1)).astype(bf16)
            fade = jnp.exp2(before - now)
            values = jnp.concatenate([v_ref[0, n], ones], axis=1)
            acc[n, at] = acc[n, at] * jnp.concatenate([fade, fade], axis=1) + jnp.dot(
                p, values, preferred_element_type=f32
            )


def prompt_piece(queries, fresh, bias, state, keys, values, piece):
    local = len(queries)
    units = queries[0].shape[0]
    rows = group * units
    first = state is None
    length = keys.shape[2] // pieces
    steps = length // key_block
    cache = pl.BlockSpec((1, local, key_block, 128), lambda i: (0, 0, piece * steps + i, 0))
    acc_shape, peak_shape = (local, rows, 256), (local, rows, 128)
    if first:
        given = [*fresh[0], *fresh[1], bias]
    else:
        given = list(state)
    given = [*queries, *given]
    return pl.pallas_call(
        functools.partial(prompt_kernel, local, first),
        grid=(steps,),
        in_specs=[whole(a.shape) for a in given] + [cache, cache],
        out_specs=(whole(acc_shape), whole(peak_shape)),
        out_shape=(
            jax.ShapeDtypeStruct(acc_shape, f32),
            jax.ShapeDtypeStruct(peak_shape, f32),
        ),
        scratch_shapes=[pltpu.VMEM((local, rows, 128), bf16)],
        compiler_params=params(),
        cost_estimate=pl.CostEstimate(
            flops=local * rows * length * 1024,
            bytes_accessed=local * length * 512,
            transcendentals=local * rows * length,
        ),
        name="prompt_attention",
    )(*given, keys, values)


def suffix_kernel(count, tiles_ref, lens_ref, ids_ref, *refs):
    q_refs = refs[: count + 1]
    code_ref, k_ref, v_ref = refs[count + 1 : count + 4]
    outs = refs[count + 4 : 2 * count + 5]
    qs, acc = refs[2 * count + 5 :]
    j = pl.program_id(0)
    middle = count // 2
    units = q_refs[0].shape[0]
    slots = k_ref.shape[0]
    keys = k_ref.shape[3]
    tile = tile_units

    @pl.when(j == 0)
    def _():
        at = 0
        for i in range(count):
            if i == middle:
                qs[i, : units // 2] = q_refs[at][...]
                qs[i, units // 2 :] = q_refs[at + 1][...]
                at += 2
            else:
                qs[i] = q_refs[at][...]
                at += 1

    prompt = ids_ref[j]
    acc[...] = jnp.zeros_like(acc)

    def body(t, _):
        q = qs[j]
        spot = lax.broadcasted_iota(jnp.int32, (tile, units), 0) + t * tile
        lane = lax.broadcasted_iota(jnp.int32, (tile, 128), 1)
        picks, results = [], []
        for w in range(slots):
            pick = jnp.where(code_ref[prompt, w : w + 1, :] == spot, 1.0, 0.0)
            chosen = jnp.dot(pick.astype(bf16), q, preferred_element_type=f32).astype(bf16)
            rows = jnp.concatenate(
                [chosen[:, g * 128 : (g + 1) * 128] for g in range(group)], axis=0
            )
            s = dot_nt(rows, k_ref[w, 0, 0])
            key = lax.broadcasted_iota(jnp.int32, s.shape, 1)
            s = jnp.where(key < lens_ref[w, prompt], s, masked_score)
            top = jnp.max(s, axis=1, keepdims=True)
            p = jnp.exp2(s - top)
            total = jnp.sum(p, axis=1, keepdims=True)
            o = jnp.dot(p.astype(bf16), v_ref[w, 0, 0], preferred_element_type=f32)
            o = (o / total).astype(bf16)
            level = top + jnp.log2(total)
            spread = jnp.zeros((tile, 128), f32)
            for g in range(group):
                spread = jnp.where(
                    lane % group == g, level[g * tile : (g + 1) * tile], spread
                )
            high = spread.astype(bf16)
            rest = spread - high.astype(f32)
            mid = rest.astype(bf16)
            low = (rest - mid.astype(f32)).astype(bf16)
            packed = jnp.where(
                lane < group,
                high.astype(f32),
                jnp.where(
                    lane < 2 * group,
                    mid.astype(f32),
                    jnp.where(lane < 3 * group, low.astype(f32), 0.0),
                ),
            ).astype(bf16)
            results.append(
                jnp.concatenate(
                    [o[g * tile : (g + 1) * tile] for g in range(group)] + [packed], axis=1
                )
            )
            picks.append(pick)
        pick = jnp.concatenate(picks, axis=0).astype(bf16)
        result = jnp.concatenate(results, axis=0)
        acc[...] += lax.dot_general(
            pick, result, (((0,), (0,)), ((), ())), preferred_element_type=f32
        )
        return 0

    lax.fori_loop(0, tiles_ref[prompt], body, 0)
    at = 0
    for i in range(count):
        if i == middle:

            @pl.when(j == i)
            def _(at=at):
                outs[at][...] = acc[: units // 2].astype(bf16)
                outs[at + 1][...] = acc[units // 2 :].astype(bf16)

            at += 2
        else:

            @pl.when(j == i)
            def _(at=at):
                outs[at][...] = acc[...].astype(bf16)

            at += 1


def suffix_attention(tiles, lens, ids, queries, code, keys, values, head):
    count = len(queries)
    middle = count // 2
    units = queries[0].shape[0]
    width = group * 128 + 128
    slots, _, _, span, _ = keys.shape
    cache = pl.BlockSpec(
        (slots, 1, 1, span, 128), lambda j, tiles, lens, ids: (0, ids[j], head, 0, 0)
    )
    listed = flat(queries)
    shapes = [
        (units // 2, width) if i in (middle, middle + 1) else (units, width)
        for i in range(count + 1)
    ]
    outs = pl.pallas_call(
        functools.partial(suffix_kernel, count),
        grid_spec=pltpu.PrefetchScalarGridSpec(
            num_scalar_prefetch=3,
            grid=(count,),
            in_specs=[whole(a.shape) for a in listed] + [whole(code.shape), cache, cache],
            out_specs=[whole(s) for s in shapes],
            scratch_shapes=[
                pltpu.VMEM((count, units, group * 128), bf16),
                pltpu.VMEM((units, width), f32),
            ],
        ),
        out_shape=[jax.ShapeDtypeStruct(s, bf16) for s in shapes],
        compiler_params=params(),
        cost_estimate=pl.CostEstimate(
            flops=2 << 30, bytes_accessed=6 << 20, transcendentals=2 << 20
        ),
        name="suffix_attention",
    )(tiles, lens, ids, *listed, code, keys, values)
    return list(outs[:middle]) + [(outs[middle], outs[middle + 1])] + list(outs[middle + 2 :])


def merge_kernel(acc_ref, peak_ref, own_ref, front_ref, back_ref, o_ref):
    units = own_ref.shape[0]
    part = own_ref[...].astype(f32) + front_ref[...].astype(f32) + back_ref[...].astype(f32)
    levels = part[:, group * 128 :]
    for g in range(group):
        at = slice(g * units, (g + 1) * units)
        level = (
            levels[:, g : g + 1]
            + levels[:, group + g : group + g + 1]
            + levels[:, 2 * group + g : 2 * group + g + 1]
        )
        peak = peak_ref[0, at]
        top = jnp.maximum(peak, level)
        one = jnp.exp2(peak - top)
        two = jnp.exp2(level - top)
        mixed = acc_ref[0, at, :128] * one + part[:, g * 128 : (g + 1) * 128] * two
        o_ref[:, g * 128 : (g + 1) * 128] = (
            mixed / (acc_ref[0, at, 128:] * one + two)
        ).astype(bf16)


def merge(state, own, front, back, head):
    acc, peak = state
    units = own.shape[0]
    return pl.pallas_call(
        merge_kernel,
        grid=(1,),
        in_specs=[
            pl.BlockSpec((1,) + acc.shape[1:], lambda i: (head, 0, 0)),
            pl.BlockSpec((1,) + peak.shape[1:], lambda i: (head, 0, 0)),
            whole(own.shape),
            whole(front.shape),
            whole(back.shape),
        ],
        out_specs=whole((units, group * 128)),
        out_shape=jax.ShapeDtypeStruct((units, group * 128), bf16),
        compiler_params=params(),
        name="merge",
    )(acc, peak, own, front, back)


def output_kernel(count, local, heads, per, info_ref, *refs):
    contexts = refs[: local * (count + 1)]
    w_ref = refs[local * (count + 1)]
    outs = refs[local * (count + 1) + 1 : -1]
    x_ref = refs[-1]
    middle = count // 2
    units = contexts[0].shape[0]

    @pl.when(pl.program_id(0) == 0)
    def _():
        for n in range(local):
            row = 0
            for i in range(count + 1):
                ref = contexts[n * (count + 1) + i]
                size = ref.shape[0]
                x_ref[row : row + size, n * group * 128 : (n + 1) * group * 128] = ref[...]
                row += size

    y = jnp.dot(x_ref[...], w_ref[...], preferred_element_type=f32).astype(bf16)
    for j in range(count):
        for r in range(heads):

            @pl.when(info_ref[j] == r)
            def _(j=j, r=r):
                outs[r][pl.ds(pl.multiple_of(info_ref[count + j] * units, units), units)] = y[
                    j * units : (j + 1) * units
                ]


def output(info, contexts, w, heads, per):
    local = len(contexts)
    count = len(contexts[0])
    units = contexts[0][0].shape[0]
    listed = [block for found in contexts for block in flat(found)]
    step = 256
    return pl.pallas_call(
        functools.partial(output_kernel, count, local, heads, per),
        grid_spec=pltpu.PrefetchScalarGridSpec(
            num_scalar_prefetch=1,
            grid=(w.shape[1] // step,),
            in_specs=[whole(a.shape) for a in listed]
            + [pl.BlockSpec((w.shape[0], step), lambda i, info: (0, i))],
            out_specs=[pl.BlockSpec((per * units, step), lambda i, info: (0, i))] * heads,
            scratch_shapes=[pltpu.VMEM((count * units, w.shape[0]), bf16)],
        ),
        out_shape=[jax.ShapeDtypeStruct((per * units, w.shape[1]), bf16)] * heads,
        compiler_params=params(),
        name="output_projection",
    )(info, *listed, w)


def finish_kernel(steps, local, count, *refs):
    terms, o_ref = refs[:-1], refs[-1]
    rows = o_ref.shape[0]
    per = rows // (steps * local * count)
    width = local * count
    total = terms[0][...].astype(f32)
    for term in terms[1:]:
        total = total + term[...].astype(f32)
    i = lax.broadcasted_iota(jnp.int32, (rows, rows), 1)
    t = lax.broadcasted_iota(jnp.int32, (rows, rows), 0)
    slot = i // (steps * width)
    source = (i // (steps * local)) % count
    step = (i // local) % steps
    target = (step * width + source * local + i % local) * per + slot
    perm = jnp.where(t == target, 1.0, 0.0).astype(bf16)
    o_ref[...] = jnp.dot(perm, total.astype(bf16), preferred_element_type=f32).astype(bf16)


def finish(terms, steps, local, count):
    return pl.pallas_call(
        functools.partial(finish_kernel, steps, local, count),
        out_shape=jax.ShapeDtypeStruct(terms[0].shape, bf16),
        compiler_params=params(),
        name="finish",
    )(*terms)


def shards(
    hidden,
    w_qkv,
    qkv_bias,
    prompt_keys,
    prompt_values,
    suffix_keys,
    suffix_values,
    w_out,
    parents,
    lengths,
):
    count = lax.axis_size("beam")
    heads = lax.axis_size("head")
    beam = lax.axis_index("beam").astype(jnp.int32)
    head = lax.axis_index("head").astype(jnp.int32)
    steps, local_slots, prompts, _ = hidden.shape
    local = prompt_keys.shape[1]
    prompt_len = prompt_keys.shape[2]
    width = local_slots * count
    units = steps * width
    place = ring_place(beam, count)
    core = head % 2
    partner = [(j, j ^ 1) for j in range(heads)]

    rows = hidden.reshape(steps * local_slots * prompts, hidden.shape[3])
    mine = lax.all_to_all(
        split_hidden(rows, core.reshape(1), count), "beam", split_axis=0, concat_axis=0, tiled=True
    )
    other = lax.ppermute(mine, "head", partner)

    roots, starts, chain = lineage_tables(parents, lengths)

    def by_unit(table):
        table = table.reshape(steps, count, local_slots, prompts)
        return jnp.transpose(table, (3, 1, 0, 2)).reshape(prompts, units)

    unit_roots = by_unit(roots)
    unit_steps = jnp.broadcast_to(
        jnp.arange(steps, dtype=jnp.int32)[None, :, None], (count, steps, local_slots)
    ).reshape(units)
    positions = prompt_len + lax.dynamic_index_in_dim(by_unit(starts), beam, 0, False) + unit_steps
    frequency = rope_base ** (-(jnp.arange(64, dtype=f32) * 2.0 / 128))
    angles = positions.astype(f32)[:, None] * frequency
    cosine, sine = jnp.cos(angles), jnp.sin(angles)
    cosine = jnp.concatenate([cosine, cosine], axis=1)
    sine = jnp.concatenate([-sine, sine], axis=1)
    slot_ids = beam * local_slots + jnp.arange(local_slots, dtype=jnp.int32)
    owned = unit_roots[:, None, :] == slot_ids[:, None]
    upto = jnp.arange(units)[:, None] <= jnp.arange(units)[None, :]
    ranks = jnp.einsum(
        "pwu,uv->pwv", owned.astype(f32), upto.astype(f32), preferred_element_type=f32
    ).astype(jnp.int32)
    code = jnp.where(owned, ranks - 1, -1)
    tiles = (jnp.max(ranks[:, :, -1], axis=1) + tile_units - 1) // tile_units
    lens = lax.dynamic_slice_in_dim(lengths, beam * local_slots, local_slots, 0)
    places = (place + jnp.arange(count, dtype=jnp.int32)) % count
    ids = ring_member(places, count)
    own_chain = lax.dynamic_index_in_dim(chain, beam, 3, False)
    linked = own_chain[..., None] == jnp.arange(width, dtype=jnp.int32)
    linked = linked.reshape(steps, steps, count, local_slots, count, local_slots)
    linked = jnp.transpose(linked, (2, 0, 3, 4, 1, 5)).reshape(units, units)
    fresh_bias = jnp.where(linked, 0.0, masked_score).astype(f32)

    info = jnp.stack([core, place])
    queries, fresh_keys, fresh_values = [], [], []
    for n in range(local):
        blocks = project(info, mine, other, w_qkv, n, local, prompts)
        front, back = scatter_ring(blocks, count)
        columns = blocks[0].shape[1]
        bias = qkv_bias[n * columns : (n + 1) * columns].reshape(1, columns)
        q, k, v = rotate(blocks[0], front, back, bias, cosine, sine)
        queries.append(q)
        fresh_keys.append(k)
        fresh_values.append(v)

    gathered = [gather_ring(q, count) for q in queries]
    state = None
    for piece in range(pieces):
        state = prompt_piece(
            queries,
            (fresh_keys, fresh_values),
            fresh_bias,
            state,
            prompt_keys,
            prompt_values,
            piece,
        )
    contexts = []
    for n in range(local):
        parts = suffix_attention(
            tiles, lens, ids, gathered[n], code, suffix_keys, suffix_values, n
        )
        front, back = scatter_ring(parts, count)
        contexts.append(gather_ring(merge(state, parts[0], front, back, n), count))

    per = prompts // heads
    targets = ids // per
    if heads == 4:
        info = jnp.concatenate([targets ^ head, ids % per])
        outs = output(info, contexts, w_out, heads, per)
        near, far = (lax.ppermute(outs[i], "head", partner) for i in (1, 3))
        far = (outs[2].astype(f32) + far.astype(f32)).astype(bf16)
        far = lax.ppermute(far, "head", [(j, j ^ 2) for j in range(heads)])
        result = finish([outs[0], near, far], steps, local_slots, count)
    else:
        info = jnp.concatenate([targets, ids % per])
        outs = jnp.stack(output(info, contexts, w_out, heads, per))
        summed = lax.psum_scatter(outs, "head", scatter_dimension=0, tiled=True)
        result = finish([summed[0]], steps, local_slots, count)
    return result.reshape(steps, width, per, result.shape[1])


def solution(mesh):
    return jax.shard_map(
        shards,
        mesh=mesh,
        in_specs=(
            P(None, "beam", None, None),
            P("beam", "head"),
            P("head"),
            P("beam", "head", None, None),
            P("beam", "head", None, None),
            P("beam", None, "head", None, None),
            P("beam", None, "head", None, None),
            P("head", "beam"),
            P(),
            P(),
        ),
        out_specs=P(None, None, "head", "beam"),
        check_vma=False,
    )
```

```python
import functools

import jax
import jax.numpy as jnp
from jax import lax
from jax.experimental import pallas as pl
from jax.experimental.pallas import tpu as pltpu
from jax.sharding import PartitionSpec as P

rope_base = 1000000.0
masked_score = -1e30
log2e = 1.4426950408889634
group = 8
bf16 = jnp.bfloat16
f32 = jnp.float32
key_block = 2048
pieces = 4
tile_units = 32
project_step = 1280


def params(vmem_mib=24):
    return pltpu.CompilerParams(vmem_limit_bytes=vmem_mib << 20)


def whole(_):
    return pl.BlockSpec(memory_space=pltpu.VMEM)


def ring_order(count):
    return list(range(0, count, 2)) + list(range(count - 1, 0, -2))


def ring_pairs(count):
    order = ring_order(count)
    forward = [(order[i], order[(i + 1) % count]) for i in range(count)]
    return forward, [(b, a) for a, b in forward]


def ring_place(index, count):
    return jnp.where(index % 2 == 0, index // 2, count - 1 - index // 2)


def ring_member(place, count):
    return jnp.where(place < count // 2, 2 * place, 2 * (count - 1 - place) + 1)


def gather_ring(block, count):
    forward, backward = ring_pairs(count)
    middle = count // 2
    half = block.shape[0] // 2
    found = [None] * count
    found[0] = block
    ahead = behind = block
    for step in range(1, middle):
        ahead = lax.ppermute(ahead, "beam", forward)
        behind = lax.ppermute(behind, "beam", backward)
        found[count - step] = ahead
        found[step] = behind
    found[middle] = (
        lax.ppermute(ahead[:half], "beam", forward),
        lax.ppermute(behind[half:], "beam", backward),
    )
    return found


def scatter_ring(blocks, count):
    forward, backward = ring_pairs(count)
    middle = count // 2
    ahead, behind = blocks[middle]
    half = ahead.shape[0]
    for step in range(middle - 1, -1, -1):
        ahead = lax.ppermute(ahead, "beam", forward)
        behind = lax.ppermute(behind, "beam", backward)
        if step == 0:
            break
        front = blocks[step].astype(f32)
        back = blocks[count - step].astype(f32)
        ahead = ahead.astype(f32)
        behind = behind.astype(f32)
        if step == middle - 1:
            ahead = jnp.concatenate([ahead + front[:half], front[half:]])
            behind = jnp.concatenate([back[:half], behind + back[half:]])
        else:
            ahead = ahead + front
            behind = behind + back
        ahead = ahead.astype(bf16)
        behind = behind.astype(bf16)
    return ahead, behind


def flat(found):
    listed = []
    for block in found:
        listed.extend(block if isinstance(block, tuple) else (block,))
    return listed


def lineage_kernel(parents_ref, lengths_ref, roots_ref, starts_ref, chain_ref):
    steps, width, prompts = parents_ref.shape

    def take(table, chosen):
        out = jnp.zeros_like(chosen)
        for j in range(width):
            out = jnp.where(chosen == j, table[j : j + 1, :], out)
        return out

    own = lax.broadcasted_iota(jnp.int32, (width, prompts), 0)
    lengths = lengths_ref[...]
    for s in range(steps):
        current = own
        for t in range(steps - 1, s, -1):
            chain_ref[s, t] = own - width
        chain_ref[s, s] = own
        for t in range(s, 0, -1):
            current = take(parents_ref[t], current)
            chain_ref[s, t - 1] = current
        root = take(parents_ref[0], current)
        roots_ref[s] = root
        starts_ref[s] = take(lengths, root)


def lineage_tables(parents, lengths):
    steps, width, prompts = parents.shape
    return pl.pallas_call(
        lineage_kernel,
        out_shape=(
            jax.ShapeDtypeStruct((steps, width, prompts), jnp.int32),
            jax.ShapeDtypeStruct((steps, width, prompts), jnp.int32),
            jax.ShapeDtypeStruct((steps, steps, width, prompts), jnp.int32),
        ),
        compiler_params=params(),
        name="lineage",
    )(parents, lengths)


def split_kernel(core_ref, x_ref, o_ref):
    o_ref[0] = x_ref[...]


def split_hidden(hidden, core, count):
    rows, width = hidden.shape
    half, part = rows // 2, width // count
    return pl.pallas_call(
        split_kernel,
        grid_spec=pltpu.PrefetchScalarGridSpec(
            num_scalar_prefetch=1,
            grid=(count,),
            in_specs=[pl.BlockSpec((half, part), lambda i, core: (core[0], i))],
            out_specs=pl.BlockSpec((1, half, part), lambda i, core: (i, 0, 0)),
        ),
        out_shape=jax.ShapeDtypeStruct((count, half, part), bf16),
        compiler_params=params(),
        name="split_hidden",
    )(core, hidden)


def project_kernel(count, prompts, info_ref, mine_ref, other_ref, w_ref, *refs):
    outs, y_ref = refs[:-1], refs[-1]
    half, part = mine_ref.shape[1:]
    units = 2 * half * count // prompts
    rows = half * count
    core = info_ref[0]
    w = w_ref[...]
    step = w.shape[1]
    span = pl.ds(pl.multiple_of(pl.program_id(0) * step, step), step)
    lower = pl.ds(pl.multiple_of(core * rows, rows), rows)
    upper = pl.ds(pl.multiple_of((1 - core) * rows, rows), rows)
    for at, ref in ((lower, mine_ref), (upper, other_ref)):
        y = jnp.dot(ref[...].reshape(rows, part), w, preferred_element_type=f32)
        for c in range(y_ref.shape[0]):
            y_ref[c, at] = y[:, c * 128 : (c + 1) * 128]
    at = 0
    for j in range(count):
        block = jnp.concatenate(
            [
                y_ref[c, pl.ds(info_ref[1 + j], units, stride=prompts)]
                for c in range(y_ref.shape[0])
            ],
            axis=1,
        )
        if j == count // 2:
            outs[at][:, span] = block[: units // 2].astype(bf16)
            outs[at + 1][:, span] = block[units // 2 :].astype(bf16)
            at += 2
        else:
            outs[at][:, span] = block
            at += 1


def project(info, mine, other, w, head, local, prompts):
    count, half, part = mine.shape
    columns = w.shape[1] // local
    step = project_step
    units = 2 * half * count // prompts
    middle = count // 2
    shapes = []
    for j in range(count):
        if j == middle:
            shapes += [jax.ShapeDtypeStruct((units // 2, columns), bf16)] * 2
        else:
            shapes.append(jax.ShapeDtypeStruct((units, columns), f32))
    outs = pl.pallas_call(
        functools.partial(project_kernel, count, prompts),
        grid_spec=pltpu.PrefetchScalarGridSpec(
            num_scalar_prefetch=1,
            grid=(columns // step,),
            in_specs=[
                whole(mine.shape),
                whole(other.shape),
                pl.BlockSpec((part, step), lambda i, info: (0, head * (columns // step) + i)),
            ],
            out_specs=[whole(s) for s in shapes],
            scratch_shapes=[pltpu.VMEM((step // 128, 2 * half * count, 128), f32)],
        ),
        out_shape=shapes,
        compiler_params=params(),
        cost_estimate=pl.CostEstimate(
            flops=2 * units * count * part * columns, bytes_accessed=6 << 20, transcendentals=0
        ),
        name="project",
    )(info, mine, other, w)
    return list(outs[:middle]) + [(outs[middle], outs[middle + 1])] + list(outs[middle + 2 :])


def rotate_kernel(local, *refs):
    sums, (bias_ref, cos_ref, sin_ref, q_ref, k_ref, v_ref) = refs[: 3 * local], refs[3 * local :]
    cosine, sine = cos_ref[...], sin_ref[...]
    scale = log2e * 128**-0.5
    for n in range(local):
        own_ref, front_ref, back_ref = sums[3 * n : 3 * n + 3]
        columns = own_ref.shape[1]
        x = own_ref[...] + front_ref[...].astype(f32) + back_ref[...].astype(f32)
        x = x + bias_ref[:, n * columns : (n + 1) * columns]
        for g in range(group + 1):
            part = x[:, g * 128 : (g + 1) * 128]
            turned = part * cosine + pltpu.roll(part, 64, 1) * sine
            if g < group:
                at = (n * group + g) * 128
                q_ref[:, at : at + 128] = (turned * scale).astype(bf16)
            else:
                k_ref[:, n * 128 : (n + 1) * 128] = turned.astype(bf16)
        v_ref[:, n * 128 : (n + 1) * 128] = x[:, (group + 1) * 128 :].astype(bf16)


def rotate(sums, bias, cosine, sine):
    local = len(sums)
    units = cosine.shape[0]
    given = [part for three in sums for part in three] + [bias, cosine, sine]
    return pl.pallas_call(
        functools.partial(rotate_kernel, local),
        in_specs=[whole(a.shape) for a in given],
        out_specs=[whole(None)] * 3,
        out_shape=(
            jax.ShapeDtypeStruct((units, local * group * 128), bf16),
            jax.ShapeDtypeStruct((units, local * 128), bf16),
            jax.ShapeDtypeStruct((units, local * 128), bf16),
        ),
        compiler_params=params(),
        name="rotate",
    )(*given)


def dot_nt(a, b):
    return lax.dot_general(a, b, (((1,), (1,)), ((), ())), preferred_element_type=f32)


def prompt_kernel(local, first, q_ref, *refs):
    if first:
        kf_ref, vf_ref, bias_ref = refs[:3]
    k_ref, v_ref, acc, peak, rows_ref = refs[-5:]
    units = q_ref.shape[0]
    rows = group * units
    block = k_ref.shape[2]

    @pl.when(pl.program_id(0) == 0)
    def _():
        for n in range(local):
            for g in range(group):
                at = (n * group + g) * 128
                rows_ref[n, g * units : (g + 1) * units] = q_ref[:, at : at + 128]
            if first:
                head = slice(n * 128, (n + 1) * 128)
                bias = jnp.concatenate([bias_ref[...]] * group)
                s = dot_nt(rows_ref[n], kf_ref[:, head]) + bias
                top = jnp.max(s, axis=1, keepdims=True)
                p = jnp.exp2(s - top).astype(bf16)
                v = jnp.concatenate([vf_ref[:, head], jnp.ones((units, 128), bf16)], axis=1)
                acc[n] = jnp.dot(p, v, preferred_element_type=f32)
                peak[n] = jnp.broadcast_to(top, (rows, 128))

    ones = jnp.ones((block, 128), bf16)
    cut = rows // 4
    for r in range(4):
        for n in range(local):
            at = slice(r * cut, (r + 1) * cut)
            s = dot_nt(rows_ref[n, at], k_ref[0, n])
            before = peak[n, at]
            now = jnp.maximum(before, jnp.max(s, axis=1, keepdims=True))
            peak[n, at] = now
            p = jnp.exp2(s - jnp.concatenate([now] * (block // 128), axis=1)).astype(bf16)
            fade = jnp.exp2(before - now)
            values = jnp.concatenate([v_ref[0, n], ones], axis=1)
            acc[n, at] = acc[n, at] * jnp.concatenate([fade, fade], axis=1) + jnp.dot(
                p, values, preferred_element_type=f32
            )


def prompt_piece(queries, fresh, state, keys, values, piece):
    units = queries.shape[0]
    local = keys.shape[1]
    rows = group * units
    first = state is None
    length = keys.shape[2] // pieces
    steps = length // key_block
    cache = pl.BlockSpec((1, local, key_block, 128), lambda i: (0, 0, piece * steps + i, 0))
    acc_shape, peak_shape = (local, rows, 256), (local, rows, 128)
    given = [queries, *(fresh if first else state)]
    return pl.pallas_call(
        functools.partial(prompt_kernel, local, first),
        grid=(steps,),
        in_specs=[whole(a.shape) for a in given] + [cache, cache],
        out_specs=(whole(acc_shape), whole(peak_shape)),
        out_shape=(
            jax.ShapeDtypeStruct(acc_shape, f32),
            jax.ShapeDtypeStruct(peak_shape, f32),
        ),
        input_output_aliases={} if first else {1: 0, 2: 1},
        scratch_shapes=[pltpu.VMEM((local, rows, 128), bf16)],
        compiler_params=params(),
        cost_estimate=pl.CostEstimate(
            flops=local * rows * length * 1536,
            bytes_accessed=local * length * 512,
            transcendentals=local * rows * length,
        ),
        name="prompt_attention",
    )(*given, keys, values)


def suffix_kernel(local, members, split, tiles_ref, lens_ref, ids_ref, *refs):
    parts = 2 if split else 1
    q_refs = refs[: parts * len(members)]
    code_ref, k_ref, v_ref = refs[parts * len(members) : parts * len(members) + 3]
    outs, acc = refs[-parts * local * len(members) - 1 : -1], refs[-1]
    units = parts * q_refs[0].shape[0]
    slots = k_ref.shape[0]
    keys = k_ref.shape[3]
    tile = tile_units
    wide = group * 128
    prompts = [ids_ref[j] for j in members]
    acc[...] = jnp.zeros_like(acc)
    key = lax.broadcasted_iota(jnp.int32, (1, keys), 1)
    ones = jnp.ones((keys, 128), bf16)
    lane = lax.broadcasted_iota(jnp.int32, (slots * tile, 128), 1)

    def body(t, _):
        spot = lax.broadcasted_iota(jnp.int32, (tile, units), 0) + t * tile
        for c, prompt in enumerate(prompts):
            pick = jnp.concatenate(
                [
                    jnp.where(code_ref[prompt, w : w + 1, :] == spot, 1.0, 0.0)
                    for w in range(slots)
                ]
            ).astype(bf16)
            q = jnp.concatenate([ref[...] for ref in q_refs[c * parts : (c + 1) * parts]])
            chosen = jnp.dot(pick, q, preferred_element_type=f32).astype(bf16)
            for n in range(local):
                blocks, levels = [], []
                for w in range(slots):
                    at = slice(w * tile, (w + 1) * tile)
                    rows = jnp.concatenate(
                        [
                            chosen[at, n * wide + g * 128 : n * wide + (g + 1) * 128]
                            for g in range(group)
                        ],
                        axis=0,
                    )
                    limit = jnp.where(key < lens_ref[w, prompt], 0.0, masked_score)
                    s = dot_nt(rows, k_ref[w, prompt, n]) + limit
                    top = jnp.max(s, axis=1, keepdims=True)
                    p = jnp.exp2(s - top).astype(bf16)
                    values = jnp.concatenate([v_ref[w, prompt, n], ones], axis=1)
                    o = jnp.dot(p, values, preferred_element_type=f32)
                    blocks.append((o[:, :128] / o[:, 128:]).astype(bf16))
                    levels.append(top + jnp.log2(o[:, 128:]))
                spread = jnp.zeros((slots * tile, 128), f32)
                for g in range(group):
                    part = jnp.concatenate([x[g * tile : (g + 1) * tile] for x in levels])
                    spread = jnp.where(lane % group == g, part, spread)
                high = spread.astype(bf16).astype(f32)
                rest = spread - high
                mid = rest.astype(bf16).astype(f32)
                low = rest - mid
                packed = jnp.where(
                    lane < group,
                    high,
                    jnp.where(lane < 2 * group, mid, jnp.where(lane < 3 * group, low, 0.0)),
                ).astype(bf16)
                result = jnp.concatenate(
                    [
                        jnp.concatenate([x[g * tile : (g + 1) * tile] for x in blocks])
                        for g in range(group)
                    ]
                    + [packed],
                    axis=1,
                )
                acc[c, n] += lax.dot_general(
                    pick, result, (((0,), (0,)), ((), ())), preferred_element_type=f32
                )
        return 0

    count = tiles_ref[prompts[0]]
    for prompt in prompts[1:]:
        count = jnp.maximum(count, tiles_ref[prompt])
    lax.fori_loop(0, count, body, 0)
    size = units // parts
    for c in range(len(members)):
        for n in range(local):
            for h in range(parts):
                outs[(c * local + n) * parts + h][...] = acc[
                    c, n, h * size : (h + 1) * size
                ].astype(bf16)


def suffix_attention(tiles, lens, ids, found, members, split, code, keys, values, after):
    local = keys.shape[2]
    listed = flat([found[j] for j in members])
    parts = 2 if split else 1
    units = parts * listed[0].shape[0]
    width = group * 128 + 128
    outs = len(members) * local * parts
    smem = pl.BlockSpec(memory_space=pltpu.SMEM)
    result = pl.pallas_call(
        functools.partial(suffix_kernel, local, members, split),
        in_specs=[smem] * 3
        + [whole(None)] * (len(listed) + 3)
        + [pl.BlockSpec(memory_space=pl.ANY)] * len(after),
        out_specs=[whole(None)] * outs,
        out_shape=[jax.ShapeDtypeStruct((units // parts, width), bf16)] * outs,
        scratch_shapes=[pltpu.VMEM((len(members), local, units, width), f32)],
        compiler_params=params(16),
        cost_estimate=pl.CostEstimate(
            flops=len(members) << 30, bytes_accessed=1 << 20, transcendentals=len(members) << 19
        ),
        name="suffix_attention",
    )(tiles, lens, ids, *listed, code, keys, values, *after)
    result = [
        tuple(result[i : i + parts]) if split else result[i] for i in range(0, outs, parts)
    ]
    return [[result[c * local + n] for n in range(local)] for c in range(len(members))]


def merge_kernel(acc_ref, peak_ref, own_ref, front_ref, back_ref, o_ref):
    units = own_ref.shape[0]
    part = own_ref[...].astype(f32) + front_ref[...].astype(f32) + back_ref[...].astype(f32)
    levels = part[:, group * 128 :]
    for g in range(group):
        at = slice(g * units, (g + 1) * units)
        level = (
            levels[:, g : g + 1]
            + levels[:, group + g : group + g + 1]
            + levels[:, 2 * group + g : 2 * group + g + 1]
        )
        peak = peak_ref[0, at]
        top = jnp.maximum(peak, level)
        one = jnp.exp2(peak - top)
        two = jnp.exp2(level - top)
        mixed = acc_ref[0, at, :128] * one + part[:, g * 128 : (g + 1) * 128] * two
        o_ref[:, g * 128 : (g + 1) * 128] = (
            mixed / (acc_ref[0, at, 128:] * one + two)
        ).astype(bf16)


def merge(state, own, front, back, head):
    acc, peak = state
    units = own.shape[0]
    return pl.pallas_call(
        merge_kernel,
        grid=(1,),
        in_specs=[
            pl.BlockSpec((1,) + acc.shape[1:], lambda i: (head, 0, 0)),
            pl.BlockSpec((1,) + peak.shape[1:], lambda i: (head, 0, 0)),
            whole(own.shape),
            whole(front.shape),
            whole(back.shape),
        ],
        out_specs=whole((units, group * 128)),
        out_shape=jax.ShapeDtypeStruct((units, group * 128), bf16),
        compiler_params=params(),
        name="merge",
    )(acc, peak, own, front, back)


def output_kernel(count, local, heads, per, info_ref, *refs):
    contexts = refs[: local * (count + 1)]
    w_ref = refs[local * (count + 1)]
    outs = refs[local * (count + 1) + 1 : -1]
    x_ref = refs[-1]
    middle = count // 2
    units = contexts[0].shape[0]

    @pl.when(pl.program_id(0) == 0)
    def _():
        for n in range(local):
            row = 0
            for i in range(count + 1):
                ref = contexts[n * (count + 1) + i]
                size = ref.shape[0]
                x_ref[row : row + size, n * group * 128 : (n + 1) * group * 128] = ref[...]
                row += size

    y = jnp.dot(x_ref[...], w_ref[...], preferred_element_type=f32).astype(bf16)
    for j in range(count):
        for r in range(heads):

            @pl.when(info_ref[j] == r)
            def _(j=j, r=r):
                outs[r][pl.ds(pl.multiple_of(info_ref[count + j] * units, units), units)] = y[
                    j * units : (j + 1) * units
                ]


def output(info, contexts, w, heads, per):
    local = len(contexts)
    count = len(contexts[0])
    units = contexts[0][0].shape[0]
    listed = [block for found in contexts for block in flat(found)]
    step = 256
    return pl.pallas_call(
        functools.partial(output_kernel, count, local, heads, per),
        grid_spec=pltpu.PrefetchScalarGridSpec(
            num_scalar_prefetch=1,
            grid=(w.shape[1] // step,),
            in_specs=[whole(a.shape) for a in listed]
            + [pl.BlockSpec((w.shape[0], step), lambda i, info: (0, i))],
            out_specs=[pl.BlockSpec((per * units, step), lambda i, info: (0, i))] * heads,
            scratch_shapes=[pltpu.VMEM((count * units, w.shape[0]), bf16)],
        ),
        out_shape=[jax.ShapeDtypeStruct((per * units, w.shape[1]), bf16)] * heads,
        compiler_params=params(),
        name="output_projection",
    )(info, *listed, w)


def finish_kernel(steps, local, count, *refs):
    terms, o_ref = refs[:-1], refs[-1]
    rows = o_ref.shape[0]
    per = rows // (steps * local * count)
    width = local * count
    total = terms[0][...].astype(f32)
    for term in terms[1:]:
        total = total + term[...].astype(f32)
    i = lax.broadcasted_iota(jnp.int32, (rows, rows), 1)
    t = lax.broadcasted_iota(jnp.int32, (rows, rows), 0)
    slot = i // (steps * width)
    part = (i // (steps // 2 * width)) % 2
    source = (i // (steps // 2 * local)) % count
    step = part * (steps // 2) + (i // local) % (steps // 2)
    target = (step * width + source * local + i % local) * per + slot
    perm = jnp.where(t == target, 1.0, 0.0).astype(bf16)
    o_ref[...] = jnp.dot(perm, total.astype(bf16), preferred_element_type=f32).astype(bf16)


def finish(terms, steps, local, count):
    return pl.pallas_call(
        functools.partial(finish_kernel, steps, local, count),
        out_shape=jax.ShapeDtypeStruct(terms[0].shape, bf16),
        compiler_params=params(),
        name="finish",
    )(*terms)


def shards(
    hidden,
    w_qkv,
    qkv_bias,
    prompt_keys,
    prompt_values,
    suffix_keys,
    suffix_values,
    w_out,
    parents,
    lengths,
):
    count = lax.axis_size("beam")
    heads = lax.axis_size("head")
    beam = lax.axis_index("beam").astype(jnp.int32)
    head = lax.axis_index("head").astype(jnp.int32)
    steps, local_slots, prompts, _ = hidden.shape
    local = prompt_keys.shape[1]
    prompt_len = prompt_keys.shape[2]
    width = local_slots * count
    units = steps * width
    place = ring_place(beam, count)
    core = head % 2
    partner = [(j, j ^ 1) for j in range(heads)]

    rows = hidden.reshape(steps * local_slots * prompts, hidden.shape[3])
    mine = lax.all_to_all(
        split_hidden(rows, core.reshape(1), count), "beam", split_axis=0, concat_axis=0, tiled=True
    )
    other = lax.ppermute(mine, "head", partner)

    roots, starts, chain = lineage_tables(parents, lengths)
    half = steps // 2

    def by_unit(table):
        table = table.reshape(2, half, count, local_slots, prompts)
        return jnp.transpose(table, (4, 0, 2, 1, 3)).reshape(prompts, units)

    unit_roots = by_unit(roots)
    unit_steps = jnp.arange(steps, dtype=jnp.int32).reshape(2, 1, half, 1)
    unit_steps = jnp.broadcast_to(unit_steps, (2, count, half, local_slots)).reshape(units)
    positions = prompt_len + lax.dynamic_index_in_dim(by_unit(starts), beam, 0, False) + unit_steps
    frequency = rope_base ** (-(jnp.arange(64, dtype=f32) * 2.0 / 128))
    angles = positions.astype(f32)[:, None] * frequency
    cosine, sine = jnp.cos(angles), jnp.sin(angles)
    cosine = jnp.concatenate([cosine, cosine], axis=1)
    sine = jnp.concatenate([-sine, sine], axis=1)
    slot_ids = beam * local_slots + jnp.arange(local_slots, dtype=jnp.int32)
    owned = unit_roots[:, None, :] == slot_ids[:, None]
    upto = jnp.arange(units)[:, None] <= jnp.arange(units)[None, :]
    ranks = jnp.einsum(
        "pwu,uv->pwv", owned.astype(f32), upto.astype(f32), preferred_element_type=f32
    ).astype(jnp.int32)
    code = jnp.where(owned, ranks - 1, -1)
    tiles = (jnp.max(ranks[:, :, -1], axis=1) + tile_units - 1) // tile_units
    lens = lax.dynamic_slice_in_dim(lengths, beam * local_slots, local_slots, 0)
    places = (place + jnp.arange(count, dtype=jnp.int32)) % count
    ids = ring_member(places, count)
    own_chain = lax.dynamic_index_in_dim(chain, beam, 3, False)
    linked = own_chain[..., None] == jnp.arange(width, dtype=jnp.int32)
    linked = linked.reshape(2, half, 2, half, count, local_slots, count, local_slots)
    linked = jnp.transpose(linked, (0, 4, 1, 5, 2, 6, 3, 7)).reshape(units, units)
    fresh_bias = jnp.where(linked, 0.0, masked_score).astype(f32)

    info = jnp.concatenate([core.reshape(1), ids])
    sums = []
    for n in range(local):
        blocks = project(info, mine, other, w_qkv, n, local, prompts)
        sums.append((blocks[0], *scatter_ring(blocks, count)))
    queries, fresh_keys, fresh_values = rotate(sums, qkv_bias.reshape(1, -1), cosine, sine)

    gathered = gather_ring(queries, count)
    state = None
    for piece in range(pieces):
        state = prompt_piece(
            queries,
            (fresh_keys, fresh_values, fresh_bias),
            state,
            prompt_keys,
            prompt_values,
            piece,
        )

    middle = count // 2
    parts = [[None] * count for _ in range(local)]
    for step in range(middle, -1, -1):
        members = (step,) if step in (0, middle) else (step, count - step)
        results = suffix_attention(
            tiles,
            lens,
            ids,
            gathered,
            members,
            step == middle,
            code,
            suffix_keys,
            suffix_values,
            (state[1],) if step == middle else (),
        )
        for j, result in zip(members, results):
            for n in range(local):
                parts[n][j] = result[n]
    contexts = []
    for n in range(local):
        front, back = scatter_ring(parts[n], count)
        contexts.append(gather_ring(merge(state, parts[n][0], front, back, n), count))

    per = prompts // heads
    targets = ids // per
    if heads == 4:
        info = jnp.concatenate([targets ^ head, ids % per])
        outs = output(info, contexts, w_out, heads, per)
        near, far = (lax.ppermute(outs[i], "head", partner) for i in (1, 3))
        far = (outs[2].astype(f32) + far.astype(f32)).astype(bf16)
        far = lax.ppermute(far, "head", [(j, j ^ 2) for j in range(heads)])
        result = finish([outs[0], near, far], steps, local_slots, count)
    else:
        info = jnp.concatenate([targets, ids % per])
        outs = jnp.stack(output(info, contexts, w_out, heads, per))
        summed = lax.psum_scatter(outs, "head", scatter_dimension=0, tiled=True)
        result = finish([summed[0]], steps, local_slots, count)
    return result.reshape(steps, width, per, result.shape[1])


def solution(mesh):
    return jax.shard_map(
        shards,
        mesh=mesh,
        in_specs=(
            P(None, "beam", None, None),
            P("beam", "head"),
            P("head"),
            P("beam", "head", None, None),
            P("beam", "head", None, None),
            P("beam", None, "head", None, None),
            P("beam", None, "head", None, None),
            P("head", "beam"),
            P(),
            P(),
        ),
        out_specs=P(None, None, "head", "beam"),
        check_vma=False,
    )
```

```python
import functools

import jax
import jax.numpy as jnp
from jax import lax
from jax.experimental import pallas as pl
from jax.experimental.pallas import tpu as pltpu
from jax.sharding import PartitionSpec as P

rope_base = 1000000.0
masked_score = -1e30
log2e = 1.4426950408889634
group = 8
bf16 = jnp.bfloat16
f32 = jnp.float32
key_block = 2048
pieces = 4
tile_units = 32
lift_limit = 64.0


def params(vmem_mib=24):
    return pltpu.CompilerParams(vmem_limit_bytes=vmem_mib << 20)


def whole(_):
    return pl.BlockSpec(memory_space=pltpu.VMEM)


def ring_order(count):
    return list(range(0, count, 2)) + list(range(count - 1, 0, -2))


def ring_pairs(count):
    order = ring_order(count)
    forward = [(order[i], order[(i + 1) % count]) for i in range(count)]
    return forward, [(b, a) for a, b in forward]


def ring_place(index, count):
    return jnp.where(index % 2 == 0, index // 2, count - 1 - index // 2)


def ring_member(place, count):
    return jnp.where(place < count // 2, 2 * place, 2 * (count - 1 - place) + 1)


def gather_ring(block, count):
    forward, backward = ring_pairs(count)
    middle = count // 2
    half = block.shape[0] // 2
    found = [None] * count
    found[0] = block
    ahead = behind = block
    for step in range(1, middle):
        ahead = lax.ppermute(ahead, "beam", forward)
        behind = lax.ppermute(behind, "beam", backward)
        found[count - step] = ahead
        found[step] = behind
    found[middle] = (
        lax.ppermute(ahead[:half], "beam", forward),
        lax.ppermute(behind[half:], "beam", backward),
    )
    return found


def scatter_ring(blocks, count):
    forward, backward = ring_pairs(count)
    middle = count // 2
    ahead, behind = blocks[middle]
    half = ahead.shape[0]
    for step in range(middle - 1, -1, -1):
        ahead = lax.ppermute(ahead, "beam", forward)
        behind = lax.ppermute(behind, "beam", backward)
        if step == 0:
            break
        front = blocks[step].astype(f32)
        back = blocks[count - step].astype(f32)
        ahead = ahead.astype(f32)
        behind = behind.astype(f32)
        if step == middle - 1:
            ahead = jnp.concatenate([ahead + front[:half], front[half:]])
            behind = jnp.concatenate([back[:half], behind + back[half:]])
        else:
            ahead = ahead + front
            behind = behind + back
        ahead = ahead.astype(bf16)
        behind = behind.astype(bf16)
    return ahead, behind


def flat(found):
    listed = []
    for block in found:
        listed.extend(block if isinstance(block, tuple) else (block,))
    return listed


def lineage_kernel(
    parents_ref, lengths_ref, w_ref, roots_ref, starts_ref, chain_ref, staged_ref, sem
):
    steps, width, prompts = parents_ref.shape
    stage = pltpu.make_async_copy(w_ref, staged_ref, sem)
    stage.start()

    def take(table, chosen):
        out = jnp.zeros_like(chosen)
        for j in range(width):
            out = jnp.where(chosen == j, table[j : j + 1, :], out)
        return out

    own = lax.broadcasted_iota(jnp.int32, (width, prompts), 0)
    lengths = lengths_ref[...]
    for s in range(steps):
        current = own
        for t in range(steps - 1, s, -1):
            chain_ref[s, t] = own - width
        chain_ref[s, s] = own
        for t in range(s, 0, -1):
            current = take(parents_ref[t], current)
            chain_ref[s, t - 1] = current
        root = take(parents_ref[0], current)
        roots_ref[s] = root
        starts_ref[s] = take(lengths, root)
    stage.wait()


def lineage_tables(parents, lengths, w):
    steps, width, prompts = parents.shape
    return pl.pallas_call(
        lineage_kernel,
        in_specs=[whole(None)] * 2 + [pl.BlockSpec(memory_space=pl.ANY)],
        out_specs=[whole(None)] * 4,
        out_shape=(
            jax.ShapeDtypeStruct((steps, width, prompts), jnp.int32),
            jax.ShapeDtypeStruct((steps, width, prompts), jnp.int32),
            jax.ShapeDtypeStruct((steps, steps, width, prompts), jnp.int32),
            jax.ShapeDtypeStruct(w.shape, w.dtype),
        ),
        scratch_shapes=[pltpu.SemaphoreType.DMA],
        compiler_params=params(8),
        cost_estimate=pl.CostEstimate(flops=1 << 24, bytes_accessed=6 << 20, transcendentals=0),
        name="lineage",
    )(parents, lengths, w)


def split_kernel(core_ref, x_ref, o_ref, sem):
    count, half, part = o_ref.shape
    rows = pl.ds(pl.multiple_of(core_ref[0] * half, half), half)
    copies = [
        pltpu.make_async_copy(x_ref.at[rows, b * part : (b + 1) * part], o_ref.at[b], sem.at[b])
        for b in range(count)
    ]
    for copy in copies:
        copy.start()
    for copy in copies:
        copy.wait()


def split_hidden(hidden, core, count):
    rows, width = hidden.shape
    half, part = rows // 2, width // count
    return pl.pallas_call(
        split_kernel,
        in_specs=[pl.BlockSpec(memory_space=pltpu.SMEM), pl.BlockSpec(memory_space=pl.ANY)],
        out_specs=whole(None),
        out_shape=jax.ShapeDtypeStruct((count, half, part), bf16),
        scratch_shapes=[pltpu.SemaphoreType.DMA((count,))],
        compiler_params=params(8),
        name="split_hidden",
    )(core, hidden)


def project_kernel(count, prompts, head, info_ref, mine_ref, other_ref, w_ref, *refs):
    outs, y_ref = refs[:-1], refs[-1]
    half, part = mine_ref.shape[1:]
    units = 2 * half * count // prompts
    rows = half * count
    core = info_ref[0]
    columns = y_ref.shape[0] * 128
    w = w_ref[:, head * columns : (head + 1) * columns]
    lower = pl.ds(pl.multiple_of(core * rows, rows), rows)
    upper = pl.ds(pl.multiple_of((1 - core) * rows, rows), rows)
    for at, ref in ((lower, mine_ref), (upper, other_ref)):
        y = jnp.dot(ref[...].reshape(rows, part), w, preferred_element_type=f32)
        for c in range(y_ref.shape[0]):
            y_ref[c, at] = y[:, c * 128 : (c + 1) * 128]
    at = 0
    for j in range(count):
        block = jnp.concatenate(
            [
                y_ref[c, pl.ds(info_ref[1 + j], units, stride=prompts)]
                for c in range(y_ref.shape[0])
            ],
            axis=1,
        )
        if j == count // 2:
            outs[at][...] = block[: units // 2].astype(bf16)
            outs[at + 1][...] = block[units // 2 :].astype(bf16)
            at += 2
        else:
            outs[at][...] = block
            at += 1


def project(info, mine, other, w, head, local, prompts):
    count, half, part = mine.shape
    columns = w.shape[1] // local
    units = 2 * half * count // prompts
    middle = count // 2
    shapes = []
    for j in range(count):
        if j == middle:
            shapes += [jax.ShapeDtypeStruct((units // 2, columns), bf16)] * 2
        else:
            shapes.append(jax.ShapeDtypeStruct((units, columns), f32))
    outs = pl.pallas_call(
        functools.partial(project_kernel, count, prompts, head),
        in_specs=[pl.BlockSpec(memory_space=pltpu.SMEM)] + [whole(None)] * 3,
        out_specs=[whole(None)] * len(shapes),
        scratch_shapes=[pltpu.VMEM((columns // 128, 2 * half * count, 128), f32)],
        out_shape=shapes,
        compiler_params=params(),
        cost_estimate=pl.CostEstimate(
            flops=2 * units * count * part * columns, bytes_accessed=6 << 20, transcendentals=0
        ),
        name="project",
    )(info, mine, other, w)
    return list(outs[:middle]) + [(outs[middle], outs[middle + 1])] + list(outs[middle + 2 :])


def rotate_kernel(local, *refs):
    sums, (bias_ref, cos_ref, sin_ref, q_ref, k_ref, v_ref) = refs[: 3 * local], refs[3 * local :]
    cosine, sine = cos_ref[...], sin_ref[...]
    scale = log2e * 128**-0.5
    for n in range(local):
        own_ref, front_ref, back_ref = sums[3 * n : 3 * n + 3]
        columns = own_ref.shape[1]
        x = own_ref[...] + front_ref[...].astype(f32) + back_ref[...].astype(f32)
        x = x + bias_ref[:, n * columns : (n + 1) * columns]
        for g in range(group + 1):
            part = x[:, g * 128 : (g + 1) * 128]
            turned = part * cosine + pltpu.roll(part, 64, 1) * sine
            if g < group:
                at = (n * group + g) * 128
                q_ref[:, at : at + 128] = (turned * scale).astype(bf16)
            else:
                k_ref[:, n * 128 : (n + 1) * 128] = turned.astype(bf16)
        v_ref[:, n * 128 : (n + 1) * 128] = x[:, (group + 1) * 128 :].astype(bf16)


def rotate(sums, bias, cosine, sine):
    local = len(sums)
    units = cosine.shape[0]
    given = [part for three in sums for part in three] + [bias, cosine, sine]
    return pl.pallas_call(
        functools.partial(rotate_kernel, local),
        in_specs=[whole(a.shape) for a in given],
        out_specs=[whole(None)] * 3,
        out_shape=(
            jax.ShapeDtypeStruct((units, local * group * 128), bf16),
            jax.ShapeDtypeStruct((units, local * 128), bf16),
            jax.ShapeDtypeStruct((units, local * 128), bf16),
        ),
        compiler_params=params(),
        name="rotate",
    )(*given)


def dot_nt(a, b):
    return lax.dot_general(a, b, (((1,), (1,)), ((), ())), preferred_element_type=f32)


def prompt_kernel(local, first, q_ref, *refs):
    if first:
        kf_ref, vf_ref, bias_ref = refs[:3]
    k_ref, v_ref, acc, peak, rows_ref, fresh_sum = refs[-6:]
    units = q_ref.shape[0]
    rows = group * units
    block = k_ref.shape[2]

    @pl.when(pl.program_id(0) == 0)
    def _():
        for n in range(local):
            for g in range(group):
                at = (n * group + g) * 128
                rows_ref[n, g * units : (g + 1) * units] = q_ref[:, at : at + 128]
            if first:
                head = slice(n * 128, (n + 1) * 128)
                bias = jnp.concatenate([bias_ref[...]] * group)
                s = dot_nt(rows_ref[n], kf_ref[:, head]) + bias
                top = jnp.max(s, axis=1, keepdims=True)
                p = jnp.exp2(s - top).astype(bf16)
                v = jnp.concatenate([vf_ref[:, head], jnp.ones((units, 128), bf16)], axis=1)
                acc[n] = jnp.dot(p, v, preferred_element_type=f32)
                peak[n] = jnp.broadcast_to(top, (rows, 128))

    ones = jnp.ones((block, 128), bf16)
    cut = rows // 4
    spots = [(n, slice(r * cut, (r + 1) * cut)) for n in range(local) for r in range(4)]
    over = None
    for n, at in spots:
        s = dot_nt(rows_ref[n, at], k_ref[0, n])
        level = peak[n, at]
        lifted = [s[:, c : c + 128] - level for c in range(0, block, 128)]
        most = functools.reduce(jnp.maximum, lifted)
        over = most if over is None else jnp.maximum(over, most)
        p = jnp.concatenate([jnp.exp2(x).astype(bf16) for x in lifted], axis=1)
        values = jnp.concatenate([v_ref[0, n], ones], axis=1)
        fresh_sum[n, at] = jnp.dot(p, values, preferred_element_type=f32)
    worst = jnp.max(over)

    @pl.when(worst < lift_limit)
    def _():
        acc[...] += fresh_sum[...]

    @pl.when(worst >= lift_limit)
    def _():
        for n, at in spots:
            s = dot_nt(rows_ref[n, at], k_ref[0, n])
            before = peak[n, at]
            now = jnp.maximum(before, jnp.max(s, axis=1, keepdims=True))
            peak[n, at] = now
            p = jnp.exp2(s - jnp.concatenate([now] * (block // 128), axis=1)).astype(bf16)
            fade = jnp.exp2(before - now)
            values = jnp.concatenate([v_ref[0, n], ones], axis=1)
            acc[n, at] = acc[n, at] * jnp.concatenate([fade, fade], axis=1) + jnp.dot(
                p, values, preferred_element_type=f32
            )


def prompt_piece(queries, fresh, state, keys, values, piece):
    units = queries.shape[0]
    local = keys.shape[1]
    rows = group * units
    first = state is None
    length = keys.shape[2] // pieces
    steps = length // key_block
    cache = pl.BlockSpec((1, local, key_block, 128), lambda i: (0, 0, piece * steps + i, 0))
    acc_shape, peak_shape = (local, rows, 256), (local, rows, 128)
    given = [queries, *(fresh if first else state)]
    return pl.pallas_call(
        functools.partial(prompt_kernel, local, first),
        grid=(steps,),
        in_specs=[whole(a.shape) for a in given] + [cache, cache],
        out_specs=(whole(acc_shape), whole(peak_shape)),
        out_shape=(
            jax.ShapeDtypeStruct(acc_shape, f32),
            jax.ShapeDtypeStruct(peak_shape, f32),
        ),
        input_output_aliases={} if first else {1: 0, 2: 1},
        scratch_shapes=[pltpu.VMEM((local, rows, 128), bf16), pltpu.VMEM(acc_shape, f32)],
        compiler_params=params(),
        cost_estimate=pl.CostEstimate(
            flops=local * rows * length * 1536,
            bytes_accessed=local * length * 512,
            transcendentals=local * rows * length,
        ),
        name="prompt_attention",
    )(*given, keys, values)


def suffix_kernel(local, members, split, tiles_ref, lens_ref, ids_ref, *refs):
    parts = 2 if split else 1
    q_refs = refs[: parts * len(members)]
    code_ref, k_ref, v_ref = refs[parts * len(members) : parts * len(members) + 3]
    outs, acc = refs[-parts * local * len(members) - 1 : -1], refs[-1]
    units = parts * q_refs[0].shape[0]
    slots = k_ref.shape[0]
    keys = k_ref.shape[3]
    tile = tile_units
    wide = group * 128
    span = local * group
    prompts = [ids_ref[j] for j in members]
    acc[...] = jnp.zeros_like(acc)
    key = lax.broadcasted_iota(jnp.int32, (1, keys), 1)
    ones = jnp.ones((keys, 128), bf16)
    lane = lax.broadcasted_iota(jnp.int32, (slots * tile, 128), 1)

    def body(t, _):
        spot = lax.broadcasted_iota(jnp.int32, (tile, units), 0) + t * tile
        for c, prompt in enumerate(prompts):
            pick = jnp.concatenate(
                [
                    jnp.where(code_ref[prompt, w : w + 1, :] == spot, 1.0, 0.0)
                    for w in range(slots)
                ]
            ).astype(bf16)
            q = jnp.concatenate([ref[...] for ref in q_refs[c * parts : (c + 1) * parts]])
            chosen = jnp.dot(pick, q, preferred_element_type=f32).astype(bf16)
            spread = jnp.zeros((slots * tile, 128), f32)
            results = []
            for n in range(local):
                blocks, levels = [], []
                for w in range(slots):
                    at = slice(w * tile, (w + 1) * tile)
                    rows = jnp.concatenate(
                        [
                            chosen[at, n * wide + g * 128 : n * wide + (g + 1) * 128]
                            for g in range(group)
                        ],
                        axis=0,
                    )
                    limit = jnp.where(key < lens_ref[w, prompt], 0.0, masked_score)
                    s = dot_nt(rows, k_ref[w, prompt, n]) + limit
                    top = jnp.max(s, axis=1, keepdims=True)
                    p = jnp.exp2(s - top).astype(bf16)
                    values = jnp.concatenate([v_ref[w, prompt, n], ones], axis=1)
                    o = jnp.dot(p, values, preferred_element_type=f32)
                    blocks.append((o[:, :128] / o[:, 128:]).astype(bf16))
                    levels.append(top + jnp.log2(o[:, 128:]))
                for g in range(group):
                    part = jnp.concatenate([x[g * tile : (g + 1) * tile] for x in levels])
                    spread = jnp.where(lane % span == n * group + g, part, spread)
                results.append(
                    [
                        jnp.concatenate([x[g * tile : (g + 1) * tile] for x in blocks])
                        for g in range(group)
                    ]
                )
            high = spread.astype(bf16).astype(f32)
            rest = spread - high
            mid = rest.astype(bf16).astype(f32)
            low = rest - mid
            packed = jnp.where(
                lane < span,
                high,
                jnp.where(lane < 2 * span, mid, jnp.where(lane < 3 * span, low, 0.0)),
            ).astype(bf16)
            for n in range(local):
                result = results[n] + [packed] if n == 0 else results[n]
                width = len(result) * 128
                acc[c, n, :, :width] += lax.dot_general(
                    pick,
                    jnp.concatenate(result, axis=1),
                    (((0,), (0,)), ((), ())),
                    preferred_element_type=f32,
                )
        return 0

    count = tiles_ref[prompts[0]]
    for prompt in prompts[1:]:
        count = jnp.maximum(count, tiles_ref[prompt])
    lax.fori_loop(0, count, body, 0)
    size = units // parts
    for c in range(len(members)):
        for n in range(local):
            for h in range(parts):
                ref = outs[(c * local + n) * parts + h]
                ref[...] = acc[c, n, h * size : (h + 1) * size, : ref.shape[1]].astype(bf16)


def suffix_attention(tiles, lens, ids, found, members, split, code, keys, values, after):
    local = keys.shape[2]
    listed = flat([found[j] for j in members])
    parts = 2 if split else 1
    units = parts * listed[0].shape[0]
    width = group * 128 + 128
    outs = len(members) * local * parts
    smem = pl.BlockSpec(memory_space=pltpu.SMEM)
    result = pl.pallas_call(
        functools.partial(suffix_kernel, local, members, split),
        in_specs=[smem] * 3
        + [whole(None)] * (len(listed) + 3)
        + [pl.BlockSpec(memory_space=pl.ANY)] * len(after),
        out_specs=[whole(None)] * outs,
        out_shape=[
            jax.ShapeDtypeStruct((units // parts, width if n == 0 else width - 128), bf16)
            for _ in members
            for n in range(local)
            for _ in range(parts)
        ],
        scratch_shapes=[pltpu.VMEM((len(members), local, units, width), f32)],
        compiler_params=params(16),
        cost_estimate=pl.CostEstimate(
            flops=len(members) << 30, bytes_accessed=1 << 20, transcendentals=len(members) << 19
        ),
        name="suffix_attention",
    )(tiles, lens, ids, *listed, code, keys, values, *after)
    result = [
        tuple(result[i : i + parts]) if split else result[i] for i in range(0, outs, parts)
    ]
    return [[result[c * local + n] for n in range(local)] for c in range(len(members))]


def merge_kernel(local, acc_ref, peak_ref, *refs):
    sums, outs = refs[: 3 * local], refs[3 * local :]
    units = outs[0].shape[0]
    span = local * group
    levels = None
    for n in range(local):
        part = sum(ref[...].astype(f32) for ref in sums[3 * n : 3 * n + 3])
        if n == 0:
            levels = part[:, group * 128 :]
        for g in range(group):
            at = slice(g * units, (g + 1) * units)
            lane = n * group + g
            level = (
                levels[:, lane : lane + 1]
                + levels[:, span + lane : span + lane + 1]
                + levels[:, 2 * span + lane : 2 * span + lane + 1]
            )
            peak = peak_ref[n, at]
            top = jnp.maximum(peak, level)
            one = jnp.exp2(peak - top)
            two = jnp.exp2(level - top)
            mixed = acc_ref[n, at, :128] * one + part[:, g * 128 : (g + 1) * 128] * two
            outs[n][:, g * 128 : (g + 1) * 128] = (
                mixed / (acc_ref[n, at, 128:] * one + two)
            ).astype(bf16)


def merge(state, sums):
    local = len(sums)
    units = sums[0][0].shape[0]
    given = [*state] + [part for three in sums for part in three]
    return pl.pallas_call(
        functools.partial(merge_kernel, local),
        in_specs=[whole(None)] * len(given),
        out_specs=[whole(None)] * local,
        out_shape=[jax.ShapeDtypeStruct((units, group * 128), bf16)] * local,
        compiler_params=params(8),
        name="merge",
    )(*given)


def output_kernel(local, members, middle, halves, info_ref, w_ref, *refs):
    outs = refs[-2 * len(halves) :]
    contexts = refs[: local * (len(members) + (middle in members))]
    per_head = len(contexts) // local
    units = sum(contexts[i].shape[0] for i in range(per_head)) // len(members)
    x = jnp.concatenate(
        [
            jnp.concatenate([ref[...] for ref in contexts[n * per_head : (n + 1) * per_head]])
            for n in range(local)
        ],
        axis=1,
    )
    for h, column in enumerate(halves):
        width = outs[2 * h].shape[1]
        w = w_ref[:, column * width : (column + 1) * width]
        y = jnp.dot(x, w, preferred_element_type=f32).astype(bf16)
        for at, j in enumerate(members):
            rows = pl.ds(pl.multiple_of(info_ref[1, j] * units, units), units)
            for away in range(2):

                @pl.when(info_ref[0, j] == away)
                def _(at=at, away=away, rows=rows, h=h, y=y):
                    outs[2 * h + away][rows] = y[at * units : (at + 1) * units]


def output(info, contexts, members, halves, w, blocks, held):
    local = len(contexts)
    count = len(contexts[0])
    units = contexts[0][0].shape[0]
    listed = [block for found in contexts for block in flat([found[j] for j in members])]
    held = [] if held is None else list(held)
    outs = 2 * len(halves)
    given = 2 + len(listed)
    return pl.pallas_call(
        functools.partial(output_kernel, local, members, count // 2, halves),
        in_specs=[pl.BlockSpec(memory_space=pltpu.SMEM)]
        + [whole(None)] * (1 + len(listed) + len(held)),
        out_specs=[whole(None)] * outs,
        out_shape=[jax.ShapeDtypeStruct((blocks * units, w.shape[1] // 2), bf16)] * outs,
        input_output_aliases={given + i: i for i in range(len(held))},
        compiler_params=params(16),
        cost_estimate=pl.CostEstimate(
            flops=len(members) * units * w.shape[0] * w.shape[1] * len(halves),
            bytes_accessed=2 << 20,
            transcendentals=0,
        ),
        name="output_projection",
    )(info, w, *listed, *held)


def finish_kernel(steps, local, count, *refs):
    terms, o_ref = refs[:-1], refs[-1]
    rows, width_out = o_ref.shape
    per = rows // (steps * local * count)
    width = local * count
    total = jnp.concatenate(
        [
            sum(term[:rows].astype(f32) for term in terms[h * len(terms) // 2 : (h + 1) * len(terms) // 2])
            for h in range(2)
        ],
        axis=1,
    )
    i = lax.broadcasted_iota(jnp.int32, (rows, rows), 1)
    t = lax.broadcasted_iota(jnp.int32, (rows, rows), 0)
    slot = i // (steps * width)
    part = (i // (steps // 2 * width)) % 2
    source = (i // (steps // 2 * local)) % count
    step = part * (steps // 2) + (i // local) % (steps // 2)
    target = (step * width + source * local + i % local) * per + slot
    perm = jnp.where(t == target, 1.0, 0.0).astype(bf16)
    o_ref[...] = jnp.dot(perm, total.astype(bf16), preferred_element_type=f32).astype(bf16)


def finish(terms, rows, steps, local, count):
    return pl.pallas_call(
        functools.partial(finish_kernel, steps, local, count),
        in_specs=[whole(None)] * len(terms),
        out_specs=whole(None),
        out_shape=jax.ShapeDtypeStruct((rows, 2 * terms[0].shape[1]), bf16),
        compiler_params=params(8),
        name="finish",
    )(*terms)


def shards(
    hidden,
    w_qkv,
    qkv_bias,
    prompt_keys,
    prompt_values,
    suffix_keys,
    suffix_values,
    w_out,
    parents,
    lengths,
):
    count = lax.axis_size("beam")
    heads = lax.axis_size("head")
    beam = lax.axis_index("beam").astype(jnp.int32)
    head = lax.axis_index("head").astype(jnp.int32)
    steps, local_slots, prompts, _ = hidden.shape
    local = prompt_keys.shape[1]
    prompt_len = prompt_keys.shape[2]
    width = local_slots * count
    units = steps * width
    place = ring_place(beam, count)
    core = head % 2
    partner = [(j, j ^ 1) for j in range(heads)]

    rows = hidden.reshape(steps * local_slots * prompts, hidden.shape[3])
    mine = lax.all_to_all(
        split_hidden(rows, core.reshape(1), count), "beam", split_axis=0, concat_axis=0, tiled=True
    )
    other = lax.ppermute(mine, "head", partner)

    roots, starts, chain, w_staged = lineage_tables(parents, lengths, w_qkv)
    half = steps // 2

    def by_unit(table):
        table = table.reshape(2, half, count, local_slots, prompts)
        return jnp.transpose(table, (4, 0, 2, 1, 3)).reshape(prompts, units)

    unit_roots = by_unit(roots)
    unit_steps = jnp.arange(steps, dtype=jnp.int32).reshape(2, 1, half, 1)
    unit_steps = jnp.broadcast_to(unit_steps, (2, count, half, local_slots)).reshape(units)
    positions = prompt_len + lax.dynamic_index_in_dim(by_unit(starts), beam, 0, False) + unit_steps
    frequency = rope_base ** (-(jnp.arange(64, dtype=f32) * 2.0 / 128))
    angles = positions.astype(f32)[:, None] * frequency
    cosine, sine = jnp.cos(angles), jnp.sin(angles)
    cosine = jnp.concatenate([cosine, cosine], axis=1)
    sine = jnp.concatenate([-sine, sine], axis=1)
    slot_ids = beam * local_slots + jnp.arange(local_slots, dtype=jnp.int32)
    owned = unit_roots[:, None, :] == slot_ids[:, None]
    upto = jnp.arange(units)[:, None] <= jnp.arange(units)[None, :]
    ranks = jnp.einsum(
        "pwu,uv->pwv", owned.astype(f32), upto.astype(f32), preferred_element_type=f32
    ).astype(jnp.int32)
    code = jnp.where(owned, ranks - 1, -1)
    tiles = (jnp.max(ranks[:, :, -1], axis=1) + tile_units - 1) // tile_units
    lens = lax.dynamic_slice_in_dim(lengths, beam * local_slots, local_slots, 0)
    places = (place + jnp.arange(count, dtype=jnp.int32)) % count
    ids = ring_member(places, count)
    own_chain = lax.dynamic_index_in_dim(chain, beam, 3, False)
    linked = own_chain[..., None] == jnp.arange(width, dtype=jnp.int32)
    linked = linked.reshape(2, half, 2, half, count, local_slots, count, local_slots)
    linked = jnp.transpose(linked, (0, 4, 1, 5, 2, 6, 3, 7)).reshape(units, units)
    fresh_bias = jnp.where(linked, 0.0, masked_score).astype(f32)

    info = jnp.concatenate([core.reshape(1), ids])
    sums = []
    for n in range(local):
        blocks = project(info, mine, other, w_staged, n, local, prompts)
        sums.append((blocks[0], *scatter_ring(blocks, count)))
    queries, fresh_keys, fresh_values = rotate(sums, qkv_bias.reshape(1, -1), cosine, sine)

    gathered = gather_ring(queries, count)
    state = None
    for piece in range(pieces):
        state = prompt_piece(
            queries,
            (fresh_keys, fresh_values, fresh_bias),
            state,
            prompt_keys,
            prompt_values,
            piece,
        )

    middle = count // 2
    parts = [[None] * count for _ in range(local)]
    for step in range(middle, -1, -1):
        members = (step,) if step in (0, middle) else (step, count - step)
        results = suffix_attention(
            tiles,
            lens,
            ids,
            gathered,
            members,
            step == middle,
            code,
            suffix_keys,
            suffix_values,
            (state[1],) if step == middle else (parts[0][middle][0],),
        )
        for j, result in zip(members, results):
            for n in range(local):
                parts[n][j] = result[n]
    sums = [(parts[n][0], *scatter_ring(parts[n], count)) for n in range(local)]
    contexts = [gather_ring(context, count) for context in merge(state, sums)]

    per = prompts // heads
    chips = heads // 2
    targets = ids // per
    away = (targets % 2) ^ core
    turn = (targets // 2 - head // 2) % chips
    info = jnp.stack([away, turn * per + ids % per]).astype(jnp.int32)
    late = (middle - 1, middle, middle + 1)
    early = tuple(j for j in range(count) if j not in late)
    held = output(info, contexts, early, (0, 1), w_out, chips * per, None)
    rows = per * units
    terms = []
    for h in range(2):
        keep, send = output(
            info, contexts, late, (h,), w_out, chips * per, held[2 * h : 2 * h + 2]
        )
        came = lax.ppermute(send, "head", partner)
        terms += [keep, came]
        for i in range(1, chips):
            at = slice(i * rows, (i + 1) * rows)
            far = (keep[at].astype(f32) + came[at].astype(f32)).astype(bf16)
            pairs = [(j, (j + 2 * i) % heads) for j in range(heads)]
            terms.append(lax.ppermute(far, "head", pairs))
    result = finish(terms, rows, steps, local_slots, count)
    return result.reshape(steps, width, per, result.shape[1])


def solution(mesh):
    return jax.shard_map(
        shards,
        mesh=mesh,
        in_specs=(
            P(None, "beam", None, None),
            P("beam", "head"),
            P("head"),
            P("beam", "head", None, None),
            P("beam", "head", None, None),
            P("beam", None, "head", None, None),
            P("beam", None, "head", None, None),
            P("head", "beam"),
            P(),
            P(),
        ),
        out_specs=P(None, None, "head", "beam"),
        check_vma=False,
    )
```

```python
import functools

import jax
import jax.numpy as jnp
from jax import lax
from jax.experimental import pallas as pl
from jax.experimental.pallas import tpu as pltpu
from jax.sharding import PartitionSpec as P

rope_base = 1000000.0
masked_score = -1e30
log2e = 1.4426950408889634
group = 8
bf16 = jnp.bfloat16
f32 = jnp.float32
key_block = 2048
pieces = 4
tile_units = 32
lift_limit = 64.0


def params(vmem_mib=24):
    return pltpu.CompilerParams(vmem_limit_bytes=vmem_mib << 20)


def whole(_):
    return pl.BlockSpec(memory_space=pltpu.VMEM)


def ring_order(count):
    return list(range(0, count, 2)) + list(range(count - 1, 0, -2))


def ring_pairs(count):
    order = ring_order(count)
    forward = [(order[i], order[(i + 1) % count]) for i in range(count)]
    return forward, [(b, a) for a, b in forward]


def ring_place(index, count):
    return jnp.where(index % 2 == 0, index // 2, count - 1 - index // 2)


def ring_member(place, count):
    return jnp.where(place < count // 2, 2 * place, 2 * (count - 1 - place) + 1)


def gather_ring(block, count):
    forward, backward = ring_pairs(count)
    middle = count // 2
    half = block.shape[0] // 2
    found = [None] * count
    found[0] = block
    ahead = behind = block
    for step in range(1, middle):
        ahead = lax.ppermute(ahead, "beam", forward)
        behind = lax.ppermute(behind, "beam", backward)
        found[count - step] = ahead
        found[step] = behind
    found[middle] = (
        lax.ppermute(ahead[:half], "beam", forward),
        lax.ppermute(behind[half:], "beam", backward),
    )
    return found


def scatter_ring(blocks, count):
    forward, backward = ring_pairs(count)
    middle = count // 2
    ahead, behind = blocks[middle]
    half = ahead.shape[0]
    for step in range(middle - 1, -1, -1):
        ahead = lax.ppermute(ahead, "beam", forward)
        behind = lax.ppermute(behind, "beam", backward)
        if step == 0:
            break
        front = blocks[step].astype(f32)
        back = blocks[count - step].astype(f32)
        ahead = ahead.astype(f32)
        behind = behind.astype(f32)
        if step == middle - 1:
            ahead = jnp.concatenate([ahead + front[:half], front[half:]])
            behind = jnp.concatenate([back[:half], behind + back[half:]])
        else:
            ahead = ahead + front
            behind = behind + back
        ahead = ahead.astype(bf16)
        behind = behind.astype(bf16)
    return ahead, behind


def return_ring(produce, after, count):
    forward, backward = ring_pairs(count)
    middle = count // 2
    first = produce(middle, (after,))[0]
    ahead = [pair[0] for pair in first]
    behind = [pair[1] for pair in first]
    heads = range(len(first))
    half = ahead[0].shape[0]
    for step in range(middle - 1, -1, -1):
        marker = ahead[0]
        ahead = [lax.ppermute(block, "beam", forward) for block in ahead]
        behind = [lax.ppermute(block, "beam", backward) for block in behind]
        made = produce(step, (marker,))
        if step == 0:
            return [(made[0][n], ahead[n], behind[n]) for n in heads]
        for n in heads:
            front, back = (block[n].astype(f32) for block in made)
            one, two = ahead[n].astype(f32), behind[n].astype(f32)
            if step == middle - 1:
                one = jnp.concatenate([one + front[:half], front[half:]])
                two = jnp.concatenate([back[:half], two + back[half:]])
            else:
                one, two = one + front, two + back
            ahead[n], behind[n] = one.astype(bf16), two.astype(bf16)


def flat(found):
    listed = []
    for block in found:
        listed.extend(block if isinstance(block, tuple) else (block,))
    return listed


def lineage_kernel(parents_ref, lengths_ref, roots_ref, starts_ref, chain_ref):
    steps, width, prompts = parents_ref.shape

    def take(table, chosen):
        out = jnp.zeros_like(chosen)
        for j in range(width):
            out = jnp.where(chosen == j, table[j : j + 1, :], out)
        return out

    own = lax.broadcasted_iota(jnp.int32, (width, prompts), 0)
    lengths = lengths_ref[...]
    for s in range(steps):
        current = own
        for t in range(steps - 1, s, -1):
            chain_ref[s, t] = own - width
        chain_ref[s, s] = own
        for t in range(s, 0, -1):
            current = take(parents_ref[t], current)
            chain_ref[s, t - 1] = current
        root = take(parents_ref[0], current)
        roots_ref[s] = root
        starts_ref[s] = take(lengths, root)


def lineage_tables(parents, lengths):
    steps, width, prompts = parents.shape
    return pl.pallas_call(
        lineage_kernel,
        in_specs=[whole(None)] * 2,
        out_specs=[whole(None)] * 3,
        out_shape=(
            jax.ShapeDtypeStruct((steps, width, prompts), jnp.int32),
            jax.ShapeDtypeStruct((steps, width, prompts), jnp.int32),
            jax.ShapeDtypeStruct((steps, steps, width, prompts), jnp.int32),
        ),
        compiler_params=params(8),
        name="lineage",
    )(parents, lengths)


def split_kernel(core_ref, x_ref, o_ref, sem):
    count, half, part = o_ref.shape
    rows = pl.ds(pl.multiple_of(core_ref[0] * half, half), half)
    copies = [
        pltpu.make_async_copy(x_ref.at[rows, b * part : (b + 1) * part], o_ref.at[b], sem.at[b])
        for b in range(count)
    ]
    for copy in copies:
        copy.start()
    for copy in copies:
        copy.wait()


def split_hidden(hidden, core, count):
    rows, width = hidden.shape
    half, part = rows // 2, width // count
    return pl.pallas_call(
        split_kernel,
        in_specs=[pl.BlockSpec(memory_space=pltpu.SMEM), pl.BlockSpec(memory_space=pltpu.HBM)],
        out_specs=whole(None),
        out_shape=jax.ShapeDtypeStruct((count, half, part), bf16),
        scratch_shapes=[pltpu.SemaphoreType.DMA((count,))],
        compiler_params=params(62),
        name="split_hidden",
    )(core, hidden)


def project_kernel(count, prompts, head, info_ref, mine_ref, other_ref, w_ref, *refs):
    outs, (y_ref, held_ref, sem) = refs[:-3], refs[-3:]
    half, part = mine_ref.shape[1:]
    units = 2 * half * count // prompts
    rows = half * count
    core = info_ref[0]
    columns = y_ref.shape[0] * 128
    step = held_ref.shape[2]
    fetches = [
        pltpu.make_async_copy(
            w_ref.at[:, head * columns + i * step : head * columns + (i + 1) * step],
            held_ref.at[i],
            sem.at[i],
        )
        for i in range(columns // step)
    ]
    for fetch in fetches:
        fetch.start()
    lower = pl.ds(pl.multiple_of(core * rows, rows), rows)
    upper = pl.ds(pl.multiple_of((1 - core) * rows, rows), rows)
    for i, fetch in enumerate(fetches):
        fetch.wait()
        for at, ref in ((lower, mine_ref), (upper, other_ref)):
            y = jnp.dot(ref[...].reshape(rows, part), held_ref[i], preferred_element_type=f32)
            for c in range(step // 128):
                y_ref[i * (step // 128) + c, at] = y[:, c * 128 : (c + 1) * 128]
    at = 0
    for j in range(count):
        block = jnp.concatenate(
            [
                y_ref[c, pl.ds(info_ref[1 + j], units, stride=prompts)]
                for c in range(y_ref.shape[0])
            ],
            axis=1,
        )
        if j == count // 2:
            outs[at][...] = block[: units // 2].astype(bf16)
            outs[at + 1][...] = block[units // 2 :].astype(bf16)
            at += 2
        else:
            outs[at][...] = block
            at += 1


def project(info, mine, other, w, head, local, prompts):
    count, half, part = mine.shape
    columns = w.shape[1] // local
    units = 2 * half * count // prompts
    middle = count // 2
    shapes = []
    for j in range(count):
        if j == middle:
            shapes += [jax.ShapeDtypeStruct((units // 2, columns), bf16)] * 2
        else:
            shapes.append(jax.ShapeDtypeStruct((units, columns), f32))
    outs = pl.pallas_call(
        functools.partial(project_kernel, count, prompts, head),
        in_specs=[pl.BlockSpec(memory_space=pltpu.SMEM)]
        + [whole(None)] * 2
        + [pl.BlockSpec(memory_space=pltpu.HBM)],
        out_specs=[whole(None)] * len(shapes),
        scratch_shapes=[
            pltpu.VMEM((columns // 128, 2 * half * count, 128), f32),
            pltpu.VMEM((columns // 256, part, 256), bf16),
            pltpu.SemaphoreType.DMA((columns // 256,)),
        ],
        out_shape=shapes,
        compiler_params=params(49),
        cost_estimate=pl.CostEstimate(
            flops=2 * units * count * part * columns, bytes_accessed=6 << 20, transcendentals=0
        ),
        name="project",
    )(info, mine, other, w)
    return list(outs[:middle]) + [(outs[middle], outs[middle + 1])] + list(outs[middle + 2 :])


def rotate_kernel(local, *refs):
    sums, (bias_ref, cos_ref, sin_ref, q_ref, k_ref, v_ref) = refs[: 3 * local], refs[3 * local :]
    cosine, sine = cos_ref[...], sin_ref[...]
    scale = log2e * 128**-0.5
    for n in range(local):
        own_ref, front_ref, back_ref = sums[3 * n : 3 * n + 3]
        columns = own_ref.shape[1]
        x = own_ref[...] + front_ref[...].astype(f32) + back_ref[...].astype(f32)
        x = x + bias_ref[:, n * columns : (n + 1) * columns]
        for g in range(group + 1):
            part = x[:, g * 128 : (g + 1) * 128]
            turned = part * cosine + pltpu.roll(part, 64, 1) * sine
            if g < group:
                at = (n * group + g) * 128
                q_ref[:, at : at + 128] = (turned * scale).astype(bf16)
            else:
                k_ref[:, n * 128 : (n + 1) * 128] = turned.astype(bf16)
        v_ref[:, n * 128 : (n + 1) * 128] = x[:, (group + 1) * 128 :].astype(bf16)


def rotate(sums, bias, cosine, sine):
    local = len(sums)
    units = cosine.shape[0]
    given = [part for three in sums for part in three] + [bias, cosine, sine]
    return pl.pallas_call(
        functools.partial(rotate_kernel, local),
        in_specs=[whole(a.shape) for a in given],
        out_specs=[whole(None)] * 3,
        out_shape=(
            jax.ShapeDtypeStruct((units, local * group * 128), bf16),
            jax.ShapeDtypeStruct((units, local * 128), bf16),
            jax.ShapeDtypeStruct((units, local * 128), bf16),
        ),
        compiler_params=params(),
        name="rotate",
    )(*given)


def dot_nt(a, b):
    return lax.dot_general(a, b, (((1,), (1,)), ((), ())), preferred_element_type=f32)


def prompt_kernel(local, first, piece, q_ref, *refs):
    if first:
        kf_ref, vf_ref, bias_ref = refs[:3]
    k_hbm, v_hbm, acc, peak, rows_ref, fresh_sum, k_held, v_held, sem = refs[-9:]
    units = q_ref.shape[0]
    rows = group * units
    steps, _, block, _ = k_held.shape
    now_at = pl.program_id(0)

    def fetch(i, n):
        keys = pl.ds(piece * steps * block + i * block, block)
        return (
            pltpu.make_async_copy(k_hbm.at[0, n, keys], k_held.at[i, n], sem.at[i, n, 0]),
            pltpu.make_async_copy(v_hbm.at[0, n, keys], v_held.at[i, n], sem.at[i, n, 1]),
        )

    @pl.when(now_at == 0)
    def _():
        for i in range(steps):
            for n in range(local):
                for copy in fetch(i, n):
                    copy.start()
        for n in range(local):
            for g in range(group):
                at = (n * group + g) * 128
                rows_ref[n, g * units : (g + 1) * units] = q_ref[:, at : at + 128]
            if first:
                head = slice(n * 128, (n + 1) * 128)
                bias = jnp.concatenate([bias_ref[...]] * group)
                s = dot_nt(rows_ref[n], kf_ref[:, head]) + bias
                top = jnp.max(s, axis=1, keepdims=True)
                p = jnp.exp2(s - top).astype(bf16)
                v = jnp.concatenate([vf_ref[:, head], jnp.ones((units, 128), bf16)], axis=1)
                acc[n] = jnp.dot(p, v, preferred_element_type=f32)
                peak[n] = jnp.broadcast_to(top, (rows, 128))

    ones = jnp.ones((block, 128), bf16)
    cut = rows // 4
    spots = [(n, slice(r * cut, (r + 1) * cut)) for n in range(local) for r in range(4)]
    over = None
    for n, at in spots:
        if at.start == 0:
            for copy in fetch(now_at, n):
                copy.wait()
        s = dot_nt(rows_ref[n, at], k_held[now_at, n])
        level = peak[n, at]
        lifted = [s[:, c : c + 128] - level for c in range(0, block, 128)]
        most = functools.reduce(jnp.maximum, lifted)
        over = most if over is None else jnp.maximum(over, most)
        p = jnp.concatenate([jnp.exp2(x).astype(bf16) for x in lifted], axis=1)
        values = jnp.concatenate([v_held[now_at, n], ones], axis=1)
        fresh_sum[n, at] = jnp.dot(p, values, preferred_element_type=f32)
    worst = jnp.max(over)

    @pl.when(worst < lift_limit)
    def _():
        acc[...] += fresh_sum[...]

    @pl.when(worst >= lift_limit)
    def _():
        for n, at in spots:
            s = dot_nt(rows_ref[n, at], k_held[now_at, n])
            before = peak[n, at]
            now = jnp.maximum(before, jnp.max(s, axis=1, keepdims=True))
            peak[n, at] = now
            p = jnp.exp2(s - jnp.concatenate([now] * (block // 128), axis=1)).astype(bf16)
            fade = jnp.exp2(before - now)
            values = jnp.concatenate([v_held[now_at, n], ones], axis=1)
            acc[n, at] = acc[n, at] * jnp.concatenate([fade, fade], axis=1) + jnp.dot(
                p, values, preferred_element_type=f32
            )


def prompt_piece(queries, fresh, state, keys, values, piece):
    units = queries.shape[0]
    local = keys.shape[1]
    rows = group * units
    first = state is None
    length = keys.shape[2] // pieces
    steps = length // key_block
    cache = pl.BlockSpec(memory_space=pltpu.HBM)
    acc_shape, peak_shape = (local, rows, 256), (local, rows, 128)
    given = [queries, *(fresh if first else state)]
    return pl.pallas_call(
        functools.partial(prompt_kernel, local, first, piece),
        grid=(steps,),
        in_specs=[whole(a.shape) for a in given] + [cache, cache],
        out_specs=(whole(acc_shape), whole(peak_shape)),
        out_shape=(
            jax.ShapeDtypeStruct(acc_shape, f32),
            jax.ShapeDtypeStruct(peak_shape, f32),
        ),
        input_output_aliases={} if first else {1: 0, 2: 1},
        scratch_shapes=[
            pltpu.VMEM((local, rows, 128), bf16),
            pltpu.VMEM(acc_shape, f32),
            pltpu.VMEM((steps, local, key_block, 128), bf16),
            pltpu.VMEM((steps, local, key_block, 128), bf16),
            pltpu.SemaphoreType.DMA((steps, local, 2)),
        ],
        compiler_params=params(50),
        cost_estimate=pl.CostEstimate(
            flops=local * rows * length * 1536,
            bytes_accessed=local * length * 512,
            transcendentals=local * rows * length,
        ),
        name="prompt_attention",
    )(*given, keys, values)


def suffix_kernel(local, members, split, tiles_ref, lens_ref, ids_ref, *refs):
    parts = 2 if split else 1
    q_refs = refs[: parts * len(members)]
    code_ref, k_ref, v_ref = refs[parts * len(members) : parts * len(members) + 3]
    *outs, acc, k_held, v_held, sem = refs[-parts * local * len(members) - 4 :]
    units = parts * q_refs[0].shape[0]
    slots = k_ref.shape[0]
    keys = k_ref.shape[3]
    fetches = []
    for c, j in enumerate(members):
        prompt = ids_ref[j]
        fetches.append(pltpu.make_async_copy(k_ref.at[:, prompt], k_held.at[c], sem.at[c, 0]))
        fetches.append(pltpu.make_async_copy(v_ref.at[:, prompt], v_held.at[c], sem.at[c, 1]))
    for fetch in fetches:
        fetch.start()
    tile = tile_units
    wide = group * 128
    span = local * group
    prompts = [ids_ref[j] for j in members]
    acc[...] = jnp.zeros_like(acc)
    key = lax.broadcasted_iota(jnp.int32, (1, keys), 1)
    ones = jnp.ones((keys, 128), bf16)
    lane = lax.broadcasted_iota(jnp.int32, (slots * tile, 128), 1)

    def body(t, _):
        spot = lax.broadcasted_iota(jnp.int32, (tile, units), 0) + t * tile
        for c, prompt in enumerate(prompts):
            pick = jnp.concatenate(
                [
                    jnp.where(code_ref[prompt, w : w + 1, :] == spot, 1.0, 0.0)
                    for w in range(slots)
                ]
            ).astype(bf16)
            q = jnp.concatenate([ref[...] for ref in q_refs[c * parts : (c + 1) * parts]])
            chosen = jnp.dot(pick, q, preferred_element_type=f32).astype(bf16)
            spread = jnp.zeros((slots * tile, 128), f32)
            results = []
            for n in range(local):
                blocks, levels = [], []
                for w in range(slots):
                    at = slice(w * tile, (w + 1) * tile)
                    rows = jnp.concatenate(
                        [
                            chosen[at, n * wide + g * 128 : n * wide + (g + 1) * 128]
                            for g in range(group)
                        ],
                        axis=0,
                    )
                    limit = jnp.where(key < lens_ref[w, prompt], 0.0, masked_score)
                    s = dot_nt(rows, k_held[c, w, n]) + limit
                    top = jnp.max(s, axis=1, keepdims=True)
                    p = jnp.exp2(s - top).astype(bf16)
                    values = jnp.concatenate([v_held[c, w, n], ones], axis=1)
                    o = jnp.dot(p, values, preferred_element_type=f32)
                    blocks.append((o[:, :128] / o[:, 128:]).astype(bf16))
                    levels.append(top + jnp.log2(o[:, 128:]))
                for g in range(group):
                    part = jnp.concatenate([x[g * tile : (g + 1) * tile] for x in levels])
                    spread = jnp.where(lane % span == n * group + g, part, spread)
                results.append(
                    [
                        jnp.concatenate([x[g * tile : (g + 1) * tile] for x in blocks])
                        for g in range(group)
                    ]
                )
            high = spread.astype(bf16).astype(f32)
            rest = spread - high
            mid = rest.astype(bf16).astype(f32)
            low = rest - mid
            packed = jnp.where(
                lane < span,
                high,
                jnp.where(lane < 2 * span, mid, jnp.where(lane < 3 * span, low, 0.0)),
            ).astype(bf16)
            for n in range(local):
                result = results[n] + [packed] if n == 0 else results[n]
                width = len(result) * 128
                acc[c, n, :, :width] += lax.dot_general(
                    pick,
                    jnp.concatenate(result, axis=1),
                    (((0,), (0,)), ((), ())),
                    preferred_element_type=f32,
                )
        return 0

    count = tiles_ref[prompts[0]]
    for prompt in prompts[1:]:
        count = jnp.maximum(count, tiles_ref[prompt])
    for fetch in fetches:
        fetch.wait()
    lax.fori_loop(0, count, body, 0)
    size = units // parts
    for c in range(len(members)):
        for n in range(local):
            for h in range(parts):
                ref = outs[(c * local + n) * parts + h]
                ref[...] = acc[c, n, h * size : (h + 1) * size, : ref.shape[1]].astype(bf16)


def suffix_attention(tiles, lens, ids, found, members, split, code, keys, values, after):
    slots, _, local, span, _ = keys.shape
    listed = flat([found[j] for j in members])
    parts = 2 if split else 1
    units = parts * listed[0].shape[0]
    width = group * 128 + 128
    outs = len(members) * local * parts
    smem = pl.BlockSpec(memory_space=pltpu.SMEM)
    result = pl.pallas_call(
        functools.partial(suffix_kernel, local, members, split),
        in_specs=[smem] * 3
        + [whole(None)] * (len(listed) + 1)
        + [pl.BlockSpec(memory_space=pltpu.HBM)] * 2
        + [pl.BlockSpec(memory_space=pl.ANY)] * len(after),
        out_specs=[whole(None)] * outs,
        out_shape=[
            jax.ShapeDtypeStruct((units // parts, width if n == 0 else width - 128), bf16)
            for _ in members
            for n in range(local)
            for _ in range(parts)
        ],
        scratch_shapes=[
            pltpu.VMEM((len(members), local, units, width), f32),
            pltpu.VMEM((len(members), slots, local, span, 128), bf16),
            pltpu.VMEM((len(members), slots, local, span, 128), bf16),
            pltpu.SemaphoreType.DMA((len(members), 2)),
        ],
        compiler_params=params(50),
        cost_estimate=pl.CostEstimate(
            flops=len(members) << 30, bytes_accessed=1 << 20, transcendentals=len(members) << 19
        ),
        name="suffix_attention",
    )(tiles, lens, ids, *listed, code, keys, values, *after)
    result = [
        tuple(result[i : i + parts]) if split else result[i] for i in range(0, outs, parts)
    ]
    return [[result[c * local + n] for n in range(local)] for c in range(len(members))]


def merge_kernel(local, acc_ref, peak_ref, *refs):
    sums, outs = refs[: 3 * local], refs[3 * local :]
    units = outs[0].shape[0]
    span = local * group
    levels = None
    for n in range(local):
        part = sum(ref[...].astype(f32) for ref in sums[3 * n : 3 * n + 3])
        if n == 0:
            levels = part[:, group * 128 :]
        for g in range(group):
            at = slice(g * units, (g + 1) * units)
            lane = n * group + g
            level = (
                levels[:, lane : lane + 1]
                + levels[:, span + lane : span + lane + 1]
                + levels[:, 2 * span + lane : 2 * span + lane + 1]
            )
            peak = peak_ref[n, at]
            top = jnp.maximum(peak, level)
            one = jnp.exp2(peak - top)
            two = jnp.exp2(level - top)
            mixed = acc_ref[n, at, :128] * one + part[:, g * 128 : (g + 1) * 128] * two
            outs[n][:, g * 128 : (g + 1) * 128] = (
                mixed / (acc_ref[n, at, 128:] * one + two)
            ).astype(bf16)


def merge(state, sums):
    local = len(sums)
    units = sums[0][0].shape[0]
    given = [*state] + [part for three in sums for part in three]
    return pl.pallas_call(
        functools.partial(merge_kernel, local),
        in_specs=[whole(None)] * len(given),
        out_specs=[whole(None)] * local,
        out_shape=[jax.ShapeDtypeStruct((units, group * 128), bf16)] * local,
        compiler_params=params(8),
        name="merge",
    )(*given)


def output_kernel(local, members, middle, halves, info_ref, w_ref, *refs):
    early = len(halves) == 2
    if early:
        refs, (held_ref, sem) = refs[:-2], refs[-2:]
        step = held_ref.shape[2]
        fetches = [
            pltpu.make_async_copy(
                w_ref.at[:, i * step : (i + 1) * step], held_ref.at[i], sem.at[i]
            )
            for i in range(held_ref.shape[0])
        ]
        for fetch in fetches:
            fetch.start()
    outs = refs[-2 * len(halves) :]
    contexts = refs[: local * (len(members) + (middle in members))]
    per_head = len(contexts) // local
    units = sum(contexts[i].shape[0] for i in range(per_head)) // len(members)
    x = jnp.concatenate(
        [
            jnp.concatenate([ref[...] for ref in contexts[n * per_head : (n + 1) * per_head]])
            for n in range(local)
        ],
        axis=1,
    )
    for h, column in enumerate(halves):
        width = outs[2 * h].shape[1]
        if early:
            blocks = []
            for i in range(column * width // step, (column + 1) * width // step):
                fetches[i].wait()
                blocks.append(jnp.dot(x, held_ref[i], preferred_element_type=f32).astype(bf16))
            y = jnp.concatenate(blocks, axis=1)
        else:
            step = w_ref.shape[2]
            y = jnp.concatenate(
                [
                    jnp.dot(x, w_ref[i], preferred_element_type=f32).astype(bf16)
                    for i in range(column * width // step, (column + 1) * width // step)
                ],
                axis=1,
            )
        for at, j in enumerate(members):
            rows = pl.ds(pl.multiple_of(info_ref[1, j] * units, units), units)
            for away in range(2):

                @pl.when(info_ref[0, j] == away)
                def _(at=at, away=away, rows=rows, h=h, y=y):
                    outs[2 * h + away][rows] = y[at * units : (at + 1) * units]


def output(info, contexts, members, halves, w, blocks, held):
    local = len(contexts)
    count = len(contexts[0])
    units = contexts[0][0].shape[0]
    listed = [block for found in contexts for block in flat([found[j] for j in members])]
    held = [] if held is None else list(held)
    outs = 2 * len(halves)
    given = 2 + len(listed)
    early = len(halves) == 2
    step = 256
    depth = local * group * 128
    columns = w.shape[1] if early else w.shape[0] * step
    shapes = [jax.ShapeDtypeStruct((blocks * units, columns // 2), bf16)] * outs
    if early:
        shapes.append(jax.ShapeDtypeStruct((columns // step, depth, step), bf16))
    return pl.pallas_call(
        functools.partial(output_kernel, local, members, count // 2, halves),
        in_specs=[pl.BlockSpec(memory_space=pltpu.SMEM)]
        + [pl.BlockSpec(memory_space=pltpu.HBM) if early else whole(None)]
        + [whole(None)] * (len(listed) + len(held)),
        out_specs=[whole(None)] * len(shapes),
        scratch_shapes=[pltpu.SemaphoreType.DMA((columns // step,))] if early else [],
        out_shape=shapes,
        input_output_aliases={given + i: i for i in range(len(held))},
        compiler_params=params(45 if early else 16),
        cost_estimate=pl.CostEstimate(
            flops=len(members) * units * depth * columns * len(halves),
            bytes_accessed=2 << 20,
            transcendentals=0,
        ),
        name="output_projection",
    )(info, w, *listed, *held)


def finish_kernel(steps, local, count, *refs):
    terms, o_ref = refs[:-1], refs[-1]
    rows, width_out = o_ref.shape
    per = rows // (steps * local * count)
    width = local * count
    total = jnp.concatenate(
        [
            sum(term[:rows].astype(f32) for term in terms[h * len(terms) // 2 : (h + 1) * len(terms) // 2])
            for h in range(2)
        ],
        axis=1,
    )
    i = lax.broadcasted_iota(jnp.int32, (rows, rows), 1)
    t = lax.broadcasted_iota(jnp.int32, (rows, rows), 0)
    slot = i // (steps * width)
    part = (i // (steps // 2 * width)) % 2
    source = (i // (steps // 2 * local)) % count
    step = part * (steps // 2) + (i // local) % (steps // 2)
    target = (step * width + source * local + i % local) * per + slot
    perm = jnp.where(t == target, 1.0, 0.0).astype(bf16)
    o_ref[...] = jnp.dot(perm, total.astype(bf16), preferred_element_type=f32).astype(bf16)


def finish(terms, rows, steps, local, count):
    return pl.pallas_call(
        functools.partial(finish_kernel, steps, local, count),
        in_specs=[whole(None)] * len(terms),
        out_specs=whole(None),
        out_shape=jax.ShapeDtypeStruct((rows, 2 * terms[0].shape[1]), bf16),
        compiler_params=params(8),
        name="finish",
    )(*terms)


def shards(
    hidden,
    w_qkv,
    qkv_bias,
    prompt_keys,
    prompt_values,
    suffix_keys,
    suffix_values,
    w_out,
    parents,
    lengths,
):
    count = lax.axis_size("beam")
    heads = lax.axis_size("head")
    beam = lax.axis_index("beam").astype(jnp.int32)
    head = lax.axis_index("head").astype(jnp.int32)
    steps, local_slots, prompts, _ = hidden.shape
    local = prompt_keys.shape[1]
    prompt_len = prompt_keys.shape[2]
    width = local_slots * count
    units = steps * width
    place = ring_place(beam, count)
    core = head % 2
    partner = [(j, j ^ 1) for j in range(heads)]

    rows = hidden.reshape(steps * local_slots * prompts, hidden.shape[3])
    mine = lax.all_to_all(
        split_hidden(rows, core.reshape(1), count), "beam", split_axis=0, concat_axis=0, tiled=True
    )
    other = lax.ppermute(mine, "head", partner)

    roots, starts, chain = lineage_tables(parents, lengths)
    half = steps // 2

    def by_unit(table):
        table = table.reshape(2, half, count, local_slots, prompts)
        return jnp.transpose(table, (4, 0, 2, 1, 3)).reshape(prompts, units)

    unit_roots = by_unit(roots)
    unit_steps = jnp.arange(steps, dtype=jnp.int32).reshape(2, 1, half, 1)
    unit_steps = jnp.broadcast_to(unit_steps, (2, count, half, local_slots)).reshape(units)
    positions = prompt_len + lax.dynamic_index_in_dim(by_unit(starts), beam, 0, False) + unit_steps
    frequency = rope_base ** (-(jnp.arange(64, dtype=f32) * 2.0 / 128))
    angles = positions.astype(f32)[:, None] * frequency
    cosine, sine = jnp.cos(angles), jnp.sin(angles)
    cosine = jnp.concatenate([cosine, cosine], axis=1)
    sine = jnp.concatenate([-sine, sine], axis=1)
    slot_ids = beam * local_slots + jnp.arange(local_slots, dtype=jnp.int32)
    owned = unit_roots[:, None, :] == slot_ids[:, None]
    upto = jnp.arange(units)[:, None] <= jnp.arange(units)[None, :]
    ranks = jnp.einsum(
        "pwu,uv->pwv", owned.astype(f32), upto.astype(f32), preferred_element_type=f32
    ).astype(jnp.int32)
    code = jnp.where(owned, ranks - 1, -1)
    tiles = (jnp.max(ranks[:, :, -1], axis=1) + tile_units - 1) // tile_units
    lens = lax.dynamic_slice_in_dim(lengths, beam * local_slots, local_slots, 0)
    places = (place + jnp.arange(count, dtype=jnp.int32)) % count
    ids = ring_member(places, count)
    own_chain = lax.dynamic_index_in_dim(chain, beam, 3, False)
    linked = own_chain[..., None] == jnp.arange(width, dtype=jnp.int32)
    linked = linked.reshape(2, half, 2, half, count, local_slots, count, local_slots)
    linked = jnp.transpose(linked, (0, 4, 1, 5, 2, 6, 3, 7)).reshape(units, units)
    fresh_bias = jnp.where(linked, 0.0, masked_score).astype(f32)

    info = jnp.concatenate([core.reshape(1), ids])
    sums = []
    for n in range(local):
        blocks = project(info, mine, other, w_qkv, n, local, prompts)
        sums.append((blocks[0], *scatter_ring(blocks, count)))
    queries, fresh_keys, fresh_values = rotate(sums, qkv_bias.reshape(1, -1), cosine, sine)

    gathered = gather_ring(queries, count)
    state = None
    for piece in range(pieces):
        state = prompt_piece(
            queries,
            (fresh_keys, fresh_values, fresh_bias),
            state,
            prompt_keys,
            prompt_values,
            piece,
        )

    middle = count // 2

    def produce(step, after):
        members = (step,) if step in (0, middle) else (step, count - step)
        return suffix_attention(
            tiles,
            lens,
            ids,
            gathered,
            members,
            step == middle,
            code,
            suffix_keys,
            suffix_values,
            after,
        )

    sums = return_ring(produce, state[1], count)
    contexts = [gather_ring(context, count) for context in merge(state, sums)]

    per = prompts // heads
    chips = heads // 2
    targets = ids // per
    away = (targets % 2) ^ core
    turn = (targets // 2 - head // 2) % chips
    info = jnp.stack([away, turn * per + ids % per]).astype(jnp.int32)
    late = (middle - 1, middle, middle + 1)
    early = tuple(j for j in range(count) if j not in late)
    *held, w_held = output(info, contexts, early, (0, 1), w_out, chips * per, None)
    rows = per * units
    terms = []
    for h in range(2):
        keep, send = output(
            info, contexts, late, (h,), w_held, chips * per, held[2 * h : 2 * h + 2]
        )
        came = lax.ppermute(send, "head", partner)
        terms += [keep, came]
        for i in range(1, chips):
            at = slice(i * rows, (i + 1) * rows)
            far = (keep[at].astype(f32) + came[at].astype(f32)).astype(bf16)
            pairs = [(j, (j + 2 * i) % heads) for j in range(heads)]
            terms.append(lax.ppermute(far, "head", pairs))
    result = finish(terms, rows, steps, local_slots, count)
    return result.reshape(steps, width, per, result.shape[1])


def solution(mesh):
    return jax.shard_map(
        shards,
        mesh=mesh,
        in_specs=(
            P(None, "beam", None, None),
            P("beam", "head"),
            P("head"),
            P("beam", "head", None, None),
            P("beam", "head", None, None),
            P("beam", None, "head", None, None),
            P("beam", None, "head", None, None),
            P("head", "beam"),
            P(),
            P(),
        ),
        out_specs=P(None, None, "head", "beam"),
        check_vma=False,
    )
```

```python
import functools

import jax
import jax.numpy as jnp
from jax import lax
from jax.experimental import pallas as pl
from jax.experimental.pallas import tpu as pltpu
from jax.sharding import PartitionSpec as P

rope_base = 1000000.0
masked_score = -1e30
log2e = 1.4426950408889634
group = 8
bf16 = jnp.bfloat16
f32 = jnp.float32
key_block = 2048
pieces = 4
tile_units = 32
lift_limit = 64.0
prompt_vmem = 48
output_vmem = 45
suffix_vmem = 48


def params(vmem_mib=24):
    return pltpu.CompilerParams(vmem_limit_bytes=vmem_mib << 20)


def whole(_):
    return pl.BlockSpec(memory_space=pltpu.VMEM)


def ring_order(count):
    return list(range(0, count, 2)) + list(range(count - 1, 0, -2))


def ring_pairs(count):
    order = ring_order(count)
    forward = [(order[i], order[(i + 1) % count]) for i in range(count)]
    return forward, [(b, a) for a, b in forward]


def ring_place(index, count):
    return jnp.where(index % 2 == 0, index // 2, count - 1 - index // 2)


def ring_member(place, count):
    return jnp.where(place < count // 2, 2 * place, 2 * (count - 1 - place) + 1)


def gather_ring(block, count):
    forward, backward = ring_pairs(count)
    middle = count // 2
    half = block.shape[0] // 2
    found = [None] * count
    found[0] = block
    ahead = behind = block
    for step in range(1, middle):
        ahead = lax.ppermute(ahead, "beam", forward)
        behind = lax.ppermute(behind, "beam", backward)
        found[count - step] = ahead
        found[step] = behind
    found[middle] = (
        lax.ppermute(ahead[:half], "beam", forward),
        lax.ppermute(behind[half:], "beam", backward),
    )
    return found


def scatter_ring(blocks, count):
    forward, backward = ring_pairs(count)
    middle = count // 2
    ahead, behind = blocks[middle]
    half = ahead.shape[0]
    for step in range(middle - 1, -1, -1):
        ahead = lax.ppermute(ahead, "beam", forward)
        behind = lax.ppermute(behind, "beam", backward)
        if step == 0:
            break
        front = blocks[step].astype(f32)
        back = blocks[count - step].astype(f32)
        ahead = ahead.astype(f32)
        behind = behind.astype(f32)
        if step == middle - 1:
            ahead = jnp.concatenate([ahead + front[:half], front[half:]])
            behind = jnp.concatenate([back[:half], behind + back[half:]])
        else:
            ahead = ahead + front
            behind = behind + back
        ahead = ahead.astype(bf16)
        behind = behind.astype(bf16)
        mark = ahead if step == middle - 1 else mark
    return ahead, behind, mark


def return_ring(produce, after, count):
    forward, backward = ring_pairs(count)
    middle = count // 2
    ((ahead, behind),) = produce(middle, after)
    half = ahead.shape[0]
    for step in range(middle - 1, -1, -1):
        marker = ahead
        ahead = lax.ppermute(ahead, "beam", forward)
        behind = lax.ppermute(behind, "beam", backward)
        made = produce(step, (marker,))
        if step == 0:
            return made[0], ahead, behind
        front, back = (block.astype(f32) for block in made)
        one, two = ahead.astype(f32), behind.astype(f32)
        if step == middle - 1:
            one = jnp.concatenate([one + front[:half], front[half:]])
            two = jnp.concatenate([back[:half], two + back[half:]])
        else:
            one, two = one + front, two + back
        ahead, behind = one.astype(bf16), two.astype(bf16)


def flat(found):
    listed = []
    for block in found:
        listed.extend(block if isinstance(block, tuple) else (block,))
    return listed


def lineage_kernel(parents_ref, lengths_ref, roots_ref, starts_ref, chain_ref):
    steps, width, prompts = parents_ref.shape

    def take(table, chosen):
        out = jnp.zeros_like(chosen)
        for j in range(width):
            out = jnp.where(chosen == j, table[j : j + 1, :], out)
        return out

    own = lax.broadcasted_iota(jnp.int32, (width, prompts), 0)
    lengths = lengths_ref[...]
    for s in range(steps):
        current = own
        for t in range(steps - 1, s, -1):
            chain_ref[s, t] = own - width
        chain_ref[s, s] = own
        for t in range(s, 0, -1):
            current = take(parents_ref[t], current)
            chain_ref[s, t - 1] = current
        root = take(parents_ref[0], current)
        roots_ref[s] = root
        starts_ref[s] = take(lengths, root)


def lineage_tables(parents, lengths):
    steps, width, prompts = parents.shape
    return pl.pallas_call(
        lineage_kernel,
        in_specs=[whole(None)] * 2,
        out_specs=[whole(None)] * 3,
        out_shape=(
            jax.ShapeDtypeStruct((steps, width, prompts), jnp.int32),
            jax.ShapeDtypeStruct((steps, width, prompts), jnp.int32),
            jax.ShapeDtypeStruct((steps, steps, width, prompts), jnp.int32),
        ),
        compiler_params=params(8),
        name="lineage",
    )(parents, lengths)


def split_kernel(core_ref, x_ref, o_ref, sem):
    count, half, part = o_ref.shape
    rows = pl.ds(pl.multiple_of(core_ref[0] * half, half), half)
    copies = [
        pltpu.make_async_copy(x_ref.at[rows, b * part : (b + 1) * part], o_ref.at[b], sem.at[b])
        for b in range(count)
    ]
    for copy in copies:
        copy.start()
    for copy in copies:
        copy.wait()


def split_hidden(hidden, core, count):
    rows, width = hidden.shape
    half, part = rows // 2, width // count
    return pl.pallas_call(
        split_kernel,
        in_specs=[pl.BlockSpec(memory_space=pltpu.SMEM), pl.BlockSpec(memory_space=pltpu.HBM)],
        out_specs=whole(None),
        out_shape=jax.ShapeDtypeStruct((count, half, part), bf16),
        scratch_shapes=[pltpu.SemaphoreType.DMA((count,))],
        compiler_params=params(62),
        name="split_hidden",
    )(core, hidden)


def project_kernel(count, prompts, head, info_ref, mine_ref, other_ref, w_ref, *refs):
    outs, y_ref = refs[:-1], refs[-1]
    half, part = mine_ref.shape[1:]
    units = 2 * half * count // prompts
    rows = half * count
    core = info_ref[0]
    columns = y_ref.shape[0] * 128
    w = w_ref[:, head * columns : (head + 1) * columns]
    lower = pl.ds(pl.multiple_of(core * rows, rows), rows)
    upper = pl.ds(pl.multiple_of((1 - core) * rows, rows), rows)
    for at, ref in ((lower, mine_ref), (upper, other_ref)):
        y = jnp.dot(ref[...].reshape(rows, part), w, preferred_element_type=f32)
        for c in range(y_ref.shape[0]):
            y_ref[c, at] = y[:, c * 128 : (c + 1) * 128]
    at = 0
    for j in range(count):
        block = jnp.concatenate(
            [
                y_ref[c, pl.ds(info_ref[1 + j], units, stride=prompts)]
                for c in range(y_ref.shape[0])
            ],
            axis=1,
        )
        if j == count // 2:
            outs[at][...] = block[: units // 2].astype(bf16)
            outs[at + 1][...] = block[units // 2 :].astype(bf16)
            at += 2
        else:
            outs[at][...] = block
            at += 1


def project(info, mine, other, w, head, local, prompts):
    count, half, part = mine.shape
    columns = w.shape[1] // local
    units = 2 * half * count // prompts
    middle = count // 2
    shapes = []
    for j in range(count):
        if j == middle:
            shapes += [jax.ShapeDtypeStruct((units // 2, columns), bf16)] * 2
        else:
            shapes.append(jax.ShapeDtypeStruct((units, columns), f32))
    outs = pl.pallas_call(
        functools.partial(project_kernel, count, prompts, head),
        in_specs=[pl.BlockSpec(memory_space=pltpu.SMEM)]
        + [whole(None)] * 3,
        out_specs=[whole(None)] * len(shapes),
        scratch_shapes=[pltpu.VMEM((columns // 128, 2 * half * count, 128), f32)],
        out_shape=shapes,
        compiler_params=params(44),
        cost_estimate=pl.CostEstimate(
            flops=2 * units * count * part * columns, bytes_accessed=6 << 20, transcendentals=0
        ),
        name="project",
    )(info, mine, other, w)
    return list(outs[:middle]) + [(outs[middle], outs[middle + 1])] + list(outs[middle + 2 :])


def fetch_kernel(k_hbm, v_hbm, _, k_next, v_next, sem):
    size = k_next.shape[1] // 4
    fetches = [
        pltpu.make_async_copy(
            source.at[0, n, i * size : (i + 1) * size],
            target.at[n, i * size : (i + 1) * size],
            sem.at[h, n, i],
        )
        for n in range(k_next.shape[0])
        for i in range(4)
        for h, (source, target) in enumerate(((k_hbm, k_next), (v_hbm, v_next)))
    ]
    for fetch in fetches:
        fetch.start()
    for fetch in fetches:
        fetch.wait()


def fetch_first(keys, values, after):
    local = keys.shape[1]
    return pl.pallas_call(
        fetch_kernel,
        in_specs=[pl.BlockSpec(memory_space=pl.ANY)] * 3,
        out_specs=[whole(None)] * 2,
        out_shape=[jax.ShapeDtypeStruct((local, key_block, 128), bf16)] * 2,
        scratch_shapes=[pltpu.SemaphoreType.DMA((2, local, 4))],
        compiler_params=params(48),
        cost_estimate=pl.CostEstimate(flops=0, bytes_accessed=8 << 20, transcendentals=0),
        name="fetch_first",
    )(keys, values, after)


def rotate_kernel(local, *refs):
    sums, (bias_ref, cos_ref, sin_ref, q_ref, k_ref, v_ref) = refs[: 3 * local], refs[3 * local :]
    cosine, sine = cos_ref[...], sin_ref[...]
    scale = log2e * 128**-0.5
    for n in range(local):
        own_ref, front_ref, back_ref = sums[3 * n : 3 * n + 3]
        columns = own_ref.shape[1]
        x = own_ref[...] + front_ref[...].astype(f32) + back_ref[...].astype(f32)
        x = x + bias_ref[:, n * columns : (n + 1) * columns]
        for g in range(group + 1):
            part = x[:, g * 128 : (g + 1) * 128]
            turned = part * cosine + pltpu.roll(part, 64, 1) * sine
            if g < group:
                at = (n * group + g) * 128
                q_ref[:, at : at + 128] = (turned * scale).astype(bf16)
            else:
                k_ref[:, n * 128 : (n + 1) * 128] = turned.astype(bf16)
        v_ref[:, n * 128 : (n + 1) * 128] = x[:, (group + 1) * 128 :].astype(bf16)


def rotate(sums, bias, cosine, sine):
    local = len(sums)
    units = cosine.shape[0]
    given = [part for three in sums for part in three] + [bias, cosine, sine]
    return pl.pallas_call(
        functools.partial(rotate_kernel, local),
        in_specs=[whole(a.shape) for a in given],
        out_specs=[whole(None)] * 3,
        out_shape=(
            jax.ShapeDtypeStruct((units, local * group * 128), bf16),
            jax.ShapeDtypeStruct((units, local * 128), bf16),
            jax.ShapeDtypeStruct((units, local * 128), bf16),
        ),
        compiler_params=params(),
        name="rotate",
    )(*given)


def dot_nt(a, b):
    return lax.dot_general(a, b, (((1,), (1,)), ((), ())), preferred_element_type=f32)


def prompt_kernel(local, first, piece, last, q_ref, *refs):
    if first:
        kf_ref, vf_ref, bias_ref = refs[:3]
        refs = refs[3:]
    else:
        refs = refs[2:]
    k_first, v_first, k_hbm, v_hbm = refs[:4]
    acc, peak, k_next, v_next, rows_ref, fresh_sum, k_held, v_held, sem = refs[-9:]
    units = q_ref.shape[0]
    rows = group * units
    block = k_first.shape[1]
    steps = k_held.shape[0] + 1
    rest = []
    for i in range(1, steps):
        keys = pl.ds((piece * steps + i) * block, block)
        rest.append(
            (
                pltpu.make_async_copy(k_hbm.at[0, :, keys], k_held.at[i - 1], sem.at[i, 0]),
                pltpu.make_async_copy(v_hbm.at[0, :, keys], v_held.at[i - 1], sem.at[i, 1]),
            )
        )
    if last:
        ids_ref, ks_hbm, vs_hbm = refs[4:7]
        prompt = ids_ref[ids_ref.shape[0] // 2]
        k_source, v_source = ks_hbm.at[:, prompt], vs_hbm.at[:, prompt]
        k_target, v_target = k_next.at[0], v_next.at[0]
    else:
        keys = pl.ds((piece + 1) * steps * block, block)
        k_source, v_source = k_hbm.at[0, :, keys], v_hbm.at[0, :, keys]
        k_target, v_target = k_next, v_next
    rest.append(
        (
            pltpu.make_async_copy(k_source, k_target, sem.at[0, 0]),
            pltpu.make_async_copy(v_source, v_target, sem.at[0, 1]),
        )
    )
    for pair in rest:
        for copy in pair:
            copy.start()

    for n in range(local):
        for g in range(group):
            at = (n * group + g) * 128
            rows_ref[n, g * units : (g + 1) * units] = q_ref[:, at : at + 128]
        if first:
            head = slice(n * 128, (n + 1) * 128)
            bias = jnp.concatenate([bias_ref[...]] * group)
            s = dot_nt(rows_ref[n], kf_ref[:, head]) + bias
            top = jnp.max(s, axis=1, keepdims=True)
            p = jnp.exp2(s - top).astype(bf16)
            v = jnp.concatenate([vf_ref[:, head], jnp.ones((units, 128), bf16)], axis=1)
            acc[n] = jnp.dot(p, v, preferred_element_type=f32)
            peak[n] = jnp.broadcast_to(top, (rows, 128))

    ones = jnp.ones((block, 128), bf16)
    cut = rows // 4
    spots = [(n, slice(r * cut, (r + 1) * cut)) for n in range(local) for r in range(4)]
    for i in range(steps):
        k_ref, v_ref = (k_first, v_first) if i == 0 else (k_held.at[i - 1], v_held.at[i - 1])
        if i > 0:
            for copy in rest[i - 1]:
                copy.wait()
        over = None
        for n, at in spots:
            s = dot_nt(rows_ref[n, at], k_ref[n])
            level = peak[n, at]
            lifted = [s[:, c : c + 128] - level for c in range(0, block, 128)]
            most = functools.reduce(jnp.maximum, lifted)
            over = most if over is None else jnp.maximum(over, most)
            p = jnp.concatenate([jnp.exp2(x).astype(bf16) for x in lifted], axis=1)
            values = jnp.concatenate([v_ref[n], ones], axis=1)
            fresh_sum[n, at] = jnp.dot(p, values, preferred_element_type=f32)
        worst = jnp.max(over)

        @pl.when(worst < lift_limit)
        def _():
            acc[...] += fresh_sum[...]

        @pl.when(worst >= lift_limit)
        def _(k_ref=k_ref, v_ref=v_ref):
            for n, at in spots:
                s = dot_nt(rows_ref[n, at], k_ref[n])
                before = peak[n, at]
                now = jnp.maximum(before, jnp.max(s, axis=1, keepdims=True))
                peak[n, at] = now
                p = jnp.exp2(s - jnp.concatenate([now] * (block // 128), axis=1)).astype(bf16)
                fade = jnp.exp2(before - now)
                values = jnp.concatenate([v_ref[n], ones], axis=1)
                acc[n, at] = acc[n, at] * jnp.concatenate([fade, fade], axis=1) + jnp.dot(
                    p, values, preferred_element_type=f32
                )

    for copy in rest[-1]:
        copy.wait()


def prompt_piece(queries, fresh, state, block, keys, values, piece, ids, suffix):
    units = queries.shape[0]
    local = keys.shape[1]
    rows = group * units
    first = state is None
    last = piece == pieces - 1
    steps = keys.shape[2] // pieces // key_block
    length = steps * key_block
    acc_shape, peak_shape = (local, rows, 256), (local, rows, 128)
    given = [queries, *(fresh if first else state), *block]
    hbm = [keys, values]
    following = block[0].shape
    if last:
        slots, _, _, span, _ = suffix[0].shape
        following = (1, slots, local, span, 128)
    anywhere = pl.BlockSpec(memory_space=pl.ANY)
    outs = pl.pallas_call(
        functools.partial(prompt_kernel, local, first, piece, last),
        in_specs=[whole(None)] * len(given)
        + [anywhere] * 2
        + ([pl.BlockSpec(memory_space=pltpu.SMEM), anywhere, anywhere] if last else []),
        out_specs=[whole(None)] * 4,
        out_shape=(
            jax.ShapeDtypeStruct(acc_shape, f32),
            jax.ShapeDtypeStruct(peak_shape, f32),
            jax.ShapeDtypeStruct(following, bf16),
            jax.ShapeDtypeStruct(following, bf16),
        ),
        input_output_aliases={} if first else {1: 0, 2: 1},
        scratch_shapes=[
            pltpu.VMEM((local, rows, 128), bf16),
            pltpu.VMEM(acc_shape, f32),
            pltpu.VMEM((steps - 1, local, key_block, 128), bf16),
            pltpu.VMEM((steps - 1, local, key_block, 128), bf16),
            pltpu.SemaphoreType.DMA((steps, 2)),
        ],
        compiler_params=params(prompt_vmem),
        cost_estimate=pl.CostEstimate(
            flops=local * rows * length * 1536,
            bytes_accessed=local * length * 512,
            transcendentals=local * rows * length,
        ),
        name="prompt_attention",
    )(*given, *hbm, *((ids, *suffix) if last else ()))
    return outs[:2], outs[2:]


def suffix_kernel(local, members, following, split, tiles_ref, lens_ref, ids_ref, *refs):
    parts = 2 if split else 1
    listed = parts * len(members)
    q_refs = refs[:listed]
    code_ref, k_ref, v_ref = refs[listed : listed + 3]
    hbm = refs[listed + 3 : listed + 5] if following else ()
    fetched = 2 if following else 0
    tail = refs[-listed - fetched - 2 :]
    outs, nexts, (acc, sem) = tail[:listed], tail[listed : listed + fetched], tail[-2:]
    units = parts * q_refs[0].shape[0]
    slots = k_ref.shape[1]
    keys = k_ref.shape[3]
    tile = tile_units
    wide = group * 128
    span = local * group
    fetches = []
    if following:
        for c, j in enumerate(following):
            prompt = ids_ref[j]
            for h in range(2):
                fetches.append(
                    pltpu.make_async_copy(hbm[h].at[:, prompt], nexts[h].at[c], sem.at[c, h])
                )
    for fetch in fetches:
        fetch.start()

    prompts = [ids_ref[j] for j in members]
    acc[...] = jnp.zeros_like(acc)
    key = lax.broadcasted_iota(jnp.int32, (1, keys), 1)
    ones = jnp.ones((keys, 128), bf16)
    lane = lax.broadcasted_iota(jnp.int32, (slots * tile, 128), 1)
    chains = [(n, w) for n in range(local) for w in range(slots)]

    def body(t, _):
        spot = lax.broadcasted_iota(jnp.int32, (tile, units), 0) + t * tile
        picks, rows = [], {}
        for c, prompt in enumerate(prompts):
            pick = jnp.concatenate(
                [
                    jnp.where(code_ref[prompt, w : w + 1, :] == spot, 1.0, 0.0)
                    for w in range(slots)
                ]
            ).astype(bf16)
            picks.append(pick)
            q = jnp.concatenate([ref[...] for ref in q_refs[c * parts : (c + 1) * parts]])
            chosen = jnp.dot(pick, q, preferred_element_type=f32).astype(bf16)
            for n, w in chains:
                rows[c, n, w] = jnp.concatenate(
                    [
                        chosen[w * tile : (w + 1) * tile, at : at + 128]
                        for at in range(n * wide, (n + 1) * wide, 128)
                    ],
                    axis=0,
                )

        def score(c, n, w):
            limit = jnp.where(key < lens_ref[w, prompts[c]], 0.0, masked_score)
            return dot_nt(rows[c, n, w], k_ref[c, w, n]) + limit

        def weigh(c, n, w, p):
            values = jnp.concatenate([v_ref[c, w, n], ones], axis=1)
            return jnp.dot(p.astype(bf16), values, preferred_element_type=f32)

        def by_lane(found, c):
            out = jnp.zeros((slots * tile, 128), f32)
            for n in range(local):
                for g in range(group):
                    at = slice(g * tile, (g + 1) * tile)
                    part = jnp.concatenate([found[c, n, w][at] for w in range(slots)])
                    out = jnp.where(lane % span == n * group + g, part, out)
            high = out.astype(bf16).astype(f32)
            rest = out - high
            mid = rest.astype(bf16).astype(f32)
            low = rest - mid
            third = lane // span % 3
            return jnp.where(third == 0, high, jnp.where(third == 1, mid, low))

        def add(sums, tops):
            for c in range(len(members)):
                packed = by_lane({k: x[:, 128:] for k, x in sums.items()}, c)
                packed = jnp.where(lane // span < 6, packed, 0.0)
                levels = 0.0 if tops is None else by_lane(tops, c)
                packed = jnp.where(lane // span < 3, levels, packed).astype(bf16)
                result = [
                    jnp.concatenate(
                        [
                            sums[c, n, w][g * tile : (g + 1) * tile, :128].astype(bf16)
                            for w in range(slots)
                        ]
                    )
                    for n in range(local)
                    for g in range(group)
                ]
                acc[c] += lax.dot_general(
                    picks[c],
                    jnp.concatenate([*result, packed], axis=1),
                    (((0,), (0,)), ((), ())),
                    preferred_element_type=f32,
                )

        sums, over, under = {}, None, None
        for c in range(len(members)):
            for n, w in chains:
                s = score(c, n, w)
                most = functools.reduce(
                    jnp.maximum, [s[:, i : i + 128] for i in range(0, keys, 128)]
                )
                over = most if over is None else jnp.maximum(over, most)
                o = weigh(c, n, w, jnp.exp2(s))
                under = o[:, 128:] if under is None else jnp.minimum(under, o[:, 128:])
                sums[c, n, w] = o
        plain = (jnp.max(over) < lift_limit) & (jnp.min(under) > 2.0**-lift_limit)

        @pl.when(plain)
        def _():
            add(sums, None)

        @pl.when(jnp.logical_not(plain))
        def _():
            sums, tops = {}, {}
            for c in range(len(members)):
                for n, w in chains:
                    s = score(c, n, w)
                    top = jnp.max(s, axis=1, keepdims=True)
                    sums[c, n, w] = weigh(c, n, w, jnp.exp2(s - top))
                    tops[c, n, w] = jnp.broadcast_to(top, (s.shape[0], 128))
            add(sums, tops)

        return 0

    count = tiles_ref[prompts[0]]
    for prompt in prompts[1:]:
        count = jnp.maximum(count, tiles_ref[prompt])
    lax.fori_loop(0, count, body, 0)
    size = units // parts
    for c in range(len(members)):
        for h in range(parts):
            outs[c * parts + h][...] = acc[c, h * size : (h + 1) * size].astype(bf16)
    for fetch in fetches:
        fetch.wait()


def suffix_attention(tables, found, members, following, split, block, hbm, after):
    tiles, lens, ids, code = tables
    _, slots, local, span, _ = block[0].shape
    listed = flat([found[j] for j in members])
    parts = 2 if split else 1
    units = parts * listed[0].shape[0]
    width = local * group * 128 + 128
    shapes = [jax.ShapeDtypeStruct((units // parts, width), bf16)] * len(listed)
    if following:
        shapes += [jax.ShapeDtypeStruct((len(following), slots, local, span, 128), bf16)] * 2
    else:
        hbm = ()
    smem = pl.BlockSpec(memory_space=pltpu.SMEM)
    anywhere = pl.BlockSpec(memory_space=pl.ANY)
    result = pl.pallas_call(
        functools.partial(suffix_kernel, local, members, following, split),
        in_specs=[smem] * 3
        + [whole(None)] * (len(listed) + 3)
        + [anywhere] * (len(hbm) + len(after)),
        out_specs=[whole(None)] * len(shapes),
        out_shape=shapes,
        scratch_shapes=[
            pltpu.VMEM((len(members), units, width), f32),
            pltpu.SemaphoreType.DMA((max(len(following), 1), 2)),
        ],
        compiler_params=params(suffix_vmem),
        cost_estimate=pl.CostEstimate(
            flops=len(members) << 30, bytes_accessed=1 << 20, transcendentals=len(members) << 19
        ),
        name="suffix_attention",
    )(tiles, lens, ids, *listed, code, *block, *hbm, *after)
    sums, block = result[: len(listed)], result[len(listed) :]
    return [tuple(sums)] if split else list(sums), block


def merge_kernel(local, acc_ref, peak_ref, own_ref, front_ref, back_ref, *outs):
    units = outs[0].shape[0]
    span = local * group
    wide = local * group * 128
    part = own_ref[...].astype(f32) + front_ref[...].astype(f32) + back_ref[...].astype(f32)
    stats = part[:, wide:]
    for n in range(local):
        for g in range(group):
            at = slice(g * units, (g + 1) * units)
            lane = n * group + g
            level, total = (
                sum(stats[:, i * span + lane : i * span + lane + 1] for i in range(h, h + 3))
                for h in (0, 3)
            )
            peak = peak_ref[n, at]
            top = jnp.maximum(peak, level)
            one = jnp.exp2(peak - top)
            two = jnp.exp2(level - top)
            mixed = acc_ref[n, at, :128] * one + part[:, lane * 128 : (lane + 1) * 128] * two
            outs[n][:, g * 128 : (g + 1) * 128] = (
                mixed / (acc_ref[n, at, 128:] * one + total * two)
            ).astype(bf16)


def merge(state, sums, local):
    units = sums[0].shape[0]
    given = [*state, *sums]
    return pl.pallas_call(
        functools.partial(merge_kernel, local),
        in_specs=[whole(None)] * len(given),
        out_specs=[whole(None)] * local,
        out_shape=[jax.ShapeDtypeStruct((units, group * 128), bf16)] * local,
        compiler_params=params(8),
        name="merge",
    )(*given)


def output_kernel(local, members, middle, halves, info_ref, w_ref, *refs):
    early = len(halves) == 2
    if early:
        *refs, w_held, sem = refs
        size = w_held.shape[0] // sem.shape[0]
        fetches = [
            pltpu.make_async_copy(
                w_ref.at[i * size : (i + 1) * size], w_held.at[i * size : (i + 1) * size], sem.at[i]
            )
            for i in range(sem.shape[0])
        ]
        for fetch in fetches:
            fetch.start()
        w_ref = w_held
    outs = refs[-2 * len(halves) :]
    contexts = refs[: local * (len(members) + (middle in members))]
    per_head = len(contexts) // local
    units = sum(contexts[i].shape[0] for i in range(per_head)) // len(members)
    x = jnp.concatenate(
        [
            jnp.concatenate([ref[...] for ref in contexts[n * per_head : (n + 1) * per_head]])
            for n in range(local)
        ],
        axis=1,
    )
    if early:
        for fetch in fetches:
            fetch.wait()
    for h, column in enumerate(halves):
        width = outs[2 * h].shape[1]
        w = w_ref[:, column * width : (column + 1) * width]
        y = jnp.dot(x, w, preferred_element_type=f32).astype(bf16)
        for at, j in enumerate(members):
            rows = pl.ds(pl.multiple_of(info_ref[1, j] * units, units), units)
            for away in range(2):

                @pl.when(info_ref[0, j] == away)
                def _(at=at, away=away, rows=rows, h=h, y=y):
                    outs[2 * h + away][rows] = y[at * units : (at + 1) * units]


def output(info, contexts, members, halves, w, blocks, held):
    local = len(contexts)
    count = len(contexts[0])
    units = contexts[0][0].shape[0]
    listed = [block for found in contexts for block in flat([found[j] for j in members])]
    held = [] if held is None else list(held)
    outs = 2 * len(halves)
    given = 2 + len(listed)
    early = len(halves) == 2
    shapes = [jax.ShapeDtypeStruct((blocks * units, w.shape[1] // 2), bf16)] * outs
    return pl.pallas_call(
        functools.partial(output_kernel, local, members, count // 2, halves),
        in_specs=[pl.BlockSpec(memory_space=pltpu.SMEM)]
        + [pl.BlockSpec(memory_space=pl.ANY) if early else whole(None)]
        + [whole(None)] * (len(listed) + len(held)),
        out_specs=[whole(None)] * (outs + early),
        out_shape=shapes + ([jax.ShapeDtypeStruct(w.shape, w.dtype)] if early else []),
        scratch_shapes=[pltpu.SemaphoreType.DMA((16,))] if early else [],
        input_output_aliases={given + i: i for i in range(len(held))},
        compiler_params=params(output_vmem if early else 16),
        cost_estimate=pl.CostEstimate(
            flops=len(members) * units * w.shape[0] * w.shape[1] * len(halves),
            bytes_accessed=2 << 20,
            transcendentals=0,
        ),
        name="output_projection",
    )(info, w, *listed, *held)


def finish_kernel(steps, local, count, *refs):
    terms, o_ref = refs[:-1], refs[-1]
    rows, width_out = o_ref.shape
    per = rows // (steps * local * count)
    width = local * count
    total = jnp.concatenate(
        [
            sum(term[:rows].astype(f32) for term in terms[h * len(terms) // 2 : (h + 1) * len(terms) // 2])
            for h in range(2)
        ],
        axis=1,
    )
    i = lax.broadcasted_iota(jnp.int32, (rows, rows), 1)
    t = lax.broadcasted_iota(jnp.int32, (rows, rows), 0)
    slot = i // (steps * width)
    part = (i // (steps // 2 * width)) % 2
    source = (i // (steps // 2 * local)) % count
    step = part * (steps // 2) + (i // local) % (steps // 2)
    target = (step * width + source * local + i % local) * per + slot
    perm = jnp.where(t == target, 1.0, 0.0).astype(bf16)
    o_ref[...] = jnp.dot(perm, total.astype(bf16), preferred_element_type=f32).astype(bf16)


def finish(terms, rows, steps, local, count):
    return pl.pallas_call(
        functools.partial(finish_kernel, steps, local, count),
        in_specs=[whole(None)] * len(terms),
        out_specs=whole(None),
        out_shape=jax.ShapeDtypeStruct((rows, 2 * terms[0].shape[1]), bf16),
        compiler_params=params(8),
        name="finish",
    )(*terms)


def shards(
    hidden,
    w_qkv,
    qkv_bias,
    prompt_keys,
    prompt_values,
    suffix_keys,
    suffix_values,
    w_out,
    parents,
    lengths,
):
    count = lax.axis_size("beam")
    heads = lax.axis_size("head")
    beam = lax.axis_index("beam").astype(jnp.int32)
    head = lax.axis_index("head").astype(jnp.int32)
    steps, local_slots, prompts, _ = hidden.shape
    local = prompt_keys.shape[1]
    prompt_len = prompt_keys.shape[2]
    width = local_slots * count
    units = steps * width
    place = ring_place(beam, count)
    core = head % 2
    partner = [(j, j ^ 1) for j in range(heads)]

    rows = hidden.reshape(steps * local_slots * prompts, hidden.shape[3])
    mine = lax.all_to_all(
        split_hidden(rows, core.reshape(1), count), "beam", split_axis=0, concat_axis=0, tiled=True
    )
    other = lax.ppermute(mine, "head", partner)

    roots, starts, chain = lineage_tables(parents, lengths)
    half = steps // 2

    def by_unit(table):
        table = table.reshape(2, half, count, local_slots, prompts)
        return jnp.transpose(table, (4, 0, 2, 1, 3)).reshape(prompts, units)

    unit_roots = by_unit(roots)
    unit_steps = jnp.arange(steps, dtype=jnp.int32).reshape(2, 1, half, 1)
    unit_steps = jnp.broadcast_to(unit_steps, (2, count, half, local_slots)).reshape(units)
    positions = prompt_len + lax.dynamic_index_in_dim(by_unit(starts), beam, 0, False) + unit_steps
    frequency = rope_base ** (-(jnp.arange(64, dtype=f32) * 2.0 / 128))
    angles = positions.astype(f32)[:, None] * frequency
    cosine, sine = jnp.cos(angles), jnp.sin(angles)
    cosine = jnp.concatenate([cosine, cosine], axis=1)
    sine = jnp.concatenate([-sine, sine], axis=1)
    slot_ids = beam * local_slots + jnp.arange(local_slots, dtype=jnp.int32)
    owned = unit_roots[:, None, :] == slot_ids[:, None]
    upto = jnp.arange(units)[:, None] <= jnp.arange(units)[None, :]
    ranks = jnp.einsum(
        "pwu,uv->pwv", owned.astype(f32), upto.astype(f32), preferred_element_type=f32
    ).astype(jnp.int32)
    code = jnp.where(owned, ranks - 1, -1)
    tiles = (jnp.max(ranks[:, :, -1], axis=1) + tile_units - 1) // tile_units
    lens = lax.dynamic_slice_in_dim(lengths, beam * local_slots, local_slots, 0)
    places = (place + jnp.arange(count, dtype=jnp.int32)) % count
    ids = ring_member(places, count)
    own_chain = lax.dynamic_index_in_dim(chain, beam, 3, False)
    linked = own_chain[..., None] == jnp.arange(width, dtype=jnp.int32)
    linked = linked.reshape(2, half, 2, half, count, local_slots, count, local_slots)
    linked = jnp.transpose(linked, (0, 4, 1, 5, 2, 6, 3, 7)).reshape(units, units)
    fresh_bias = jnp.where(linked, 0.0, masked_score).astype(f32)

    info = jnp.concatenate([core.reshape(1), ids])
    sums = []
    for n in range(local):
        blocks = project(info, mine, other, w_qkv, n, local, prompts)
        front, back, mark = scatter_ring(blocks, count)
        sums.append((blocks[0], front, back))
    block = fetch_first(prompt_keys, prompt_values, mark)
    queries, fresh_keys, fresh_values = rotate(sums, qkv_bias.reshape(1, -1), cosine, sine)

    gathered = gather_ring(queries, count)
    state = None
    for piece in range(pieces):
        state, block = prompt_piece(
            queries,
            (fresh_keys, fresh_values, fresh_bias),
            state,
            block,
            prompt_keys,
            prompt_values,
            piece,
            ids,
            (suffix_keys, suffix_values),
        )

    middle = count // 2
    held = [block]

    def members(step):
        return (step,) if step in (0, middle) else (step, count - step)

    def produce(step, after):
        made, held[0] = suffix_attention(
            (tiles, lens, ids, code),
            gathered,
            members(step),
            members(step - 1) if step > 0 else (),
            step == middle,
            held[0],
            (suffix_keys, suffix_values),
            after,
        )
        return made

    sums = return_ring(produce, (), count)
    contexts = merge(state, sums, local)

    per = prompts // heads
    chips = heads // 2
    targets = ids // per
    away = (targets % 2) ^ core
    turn = (targets // 2 - head // 2) % chips
    info = jnp.stack([away, turn * per + ids % per]).astype(jnp.int32)
    late = (middle - 1, middle, middle + 1)
    early = tuple(j for j in range(count) if j not in late)
    contexts = [gather_ring(context, count) for context in contexts]
    *held, w_held = output(info, contexts, early, (0, 1), w_out, chips * per, None)
    rows = per * units
    terms = []
    for h in range(2):
        keep, send = output(
            info, contexts, late, (h,), w_held, chips * per, held[2 * h : 2 * h + 2]
        )
        came = lax.ppermute(send, "head", partner)
        terms += [keep, came]
        for i in range(1, chips):
            at = slice(i * rows, (i + 1) * rows)
            far = (keep[at].astype(f32) + came[at].astype(f32)).astype(bf16)
            pairs = [(j, (j + 2 * i) % heads) for j in range(heads)]
            terms.append(lax.ppermute(far, "head", pairs))
    result = finish(terms, rows, steps, local_slots, count)
    return result.reshape(steps, width, per, result.shape[1])


def solution(mesh):
    return jax.shard_map(
        shards,
        mesh=mesh,
        in_specs=(
            P(None, "beam", None, None),
            P("beam", "head"),
            P("head"),
            P("beam", "head", None, None),
            P("beam", "head", None, None),
            P("beam", None, "head", None, None),
            P("beam", None, "head", None, None),
            P("head", "beam"),
            P(),
            P(),
        ),
        out_specs=P(None, None, "head", "beam"),
        check_vma=False,
    )
```

```python
import functools

import jax
import jax.numpy as jnp
from jax import lax
from jax.experimental import pallas as pl
from jax.experimental.pallas import tpu as pltpu
from jax.sharding import PartitionSpec as P

rope_base = 1000000.0
masked_score = -1e30
log2e = 1.4426950408889634
group = 8
bf16 = jnp.bfloat16
f32 = jnp.float32
key_block = 2048
pieces = 4
tile_units = 32
lift_limit = 64.0
prompt_vmem = 48
output_vmem = 45
suffix_vmem = 48


def params(vmem_mib=24):
    return pltpu.CompilerParams(vmem_limit_bytes=vmem_mib << 20)


def whole(_):
    return pl.BlockSpec(memory_space=pltpu.VMEM)


def ring_order(count):
    return list(range(0, count, 2)) + list(range(count - 1, 0, -2))


def ring_pairs(count):
    order = ring_order(count)
    forward = [(order[i], order[(i + 1) % count]) for i in range(count)]
    return forward, [(b, a) for a, b in forward]


def ring_place(index, count):
    return jnp.where(index % 2 == 0, index // 2, count - 1 - index // 2)


def ring_member(place, count):
    return jnp.where(place < count // 2, 2 * place, 2 * (count - 1 - place) + 1)


def gather_ring(block, count):
    forward, backward = ring_pairs(count)
    middle = count // 2
    half = block.shape[0] // 2
    found = [None] * count
    found[0] = block
    ahead = behind = block
    for step in range(1, middle):
        ahead = lax.ppermute(ahead, "beam", forward)
        behind = lax.ppermute(behind, "beam", backward)
        found[count - step] = ahead
        found[step] = behind
    found[middle] = (
        lax.ppermute(ahead[:half], "beam", forward),
        lax.ppermute(behind[half:], "beam", backward),
    )
    return found


def scatter_ring(blocks, count):
    forward, backward = ring_pairs(count)
    middle = count // 2
    ahead, behind = blocks[middle]
    half = ahead.shape[0]
    for step in range(middle - 1, -1, -1):
        ahead = lax.ppermute(ahead, "beam", forward)
        behind = lax.ppermute(behind, "beam", backward)
        if step == 0:
            break
        front = blocks[step].astype(f32)
        back = blocks[count - step].astype(f32)
        ahead = ahead.astype(f32)
        behind = behind.astype(f32)
        if step == middle - 1:
            ahead = jnp.concatenate([ahead + front[:half], front[half:]])
            behind = jnp.concatenate([back[:half], behind + back[half:]])
        else:
            ahead = ahead + front
            behind = behind + back
        ahead = ahead.astype(bf16)
        behind = behind.astype(bf16)
        mark = ahead if step == middle - 1 else mark
    return ahead, behind, mark


def return_ring(produce, after, count):
    forward, backward = ring_pairs(count)
    middle = count // 2
    ((ahead, behind),) = produce(middle, after)
    half = ahead.shape[0]
    for step in range(middle - 1, -1, -1):
        marker = (ahead, behind)
        ahead = lax.ppermute(ahead, "beam", forward)
        behind = lax.ppermute(behind, "beam", backward)
        made = produce(step, marker)
        if step == 0:
            return made[0], ahead, behind
        front, back = (block.astype(f32) for block in made)
        one, two = ahead.astype(f32), behind.astype(f32)
        if step == middle - 1:
            one = jnp.concatenate([one + front[:half], front[half:]])
            two = jnp.concatenate([back[:half], two + back[half:]])
        else:
            one, two = one + front, two + back
        ahead, behind = one.astype(bf16), two.astype(bf16)


def flat(found):
    listed = []
    for block in found:
        listed.extend(block if isinstance(block, tuple) else (block,))
    return listed


def lineage_kernel(parents_ref, lengths_ref, roots_ref, starts_ref, chain_ref):
    steps, width, prompts = parents_ref.shape

    def take(table, chosen):
        out = jnp.zeros_like(chosen)
        for j in range(width):
            out = jnp.where(chosen == j, table[j : j + 1, :], out)
        return out

    own = lax.broadcasted_iota(jnp.int32, (width, prompts), 0)
    lengths = lengths_ref[...]
    for s in range(steps):
        current = own
        for t in range(steps - 1, s, -1):
            chain_ref[s, t] = own - width
        chain_ref[s, s] = own
        for t in range(s, 0, -1):
            current = take(parents_ref[t], current)
            chain_ref[s, t - 1] = current
        root = take(parents_ref[0], current)
        roots_ref[s] = root
        starts_ref[s] = take(lengths, root)


def lineage_tables(parents, lengths):
    steps, width, prompts = parents.shape
    return pl.pallas_call(
        lineage_kernel,
        in_specs=[whole(None)] * 2,
        out_specs=[whole(None)] * 3,
        out_shape=(
            jax.ShapeDtypeStruct((steps, width, prompts), jnp.int32),
            jax.ShapeDtypeStruct((steps, width, prompts), jnp.int32),
            jax.ShapeDtypeStruct((steps, steps, width, prompts), jnp.int32),
        ),
        compiler_params=params(8),
        name="lineage",
    )(parents, lengths)


def split_kernel(core_ref, x_ref, o_ref, sem):
    count, half, part = o_ref.shape
    rows = pl.ds(pl.multiple_of(core_ref[0] * half, half), half)
    copies = [
        pltpu.make_async_copy(x_ref.at[rows, b * part : (b + 1) * part], o_ref.at[b], sem.at[b])
        for b in range(count)
    ]
    for copy in copies:
        copy.start()
    for copy in copies:
        copy.wait()


def split_hidden(hidden, core, count):
    rows, width = hidden.shape
    half, part = rows // 2, width // count
    return pl.pallas_call(
        split_kernel,
        in_specs=[pl.BlockSpec(memory_space=pltpu.SMEM), pl.BlockSpec(memory_space=pltpu.HBM)],
        out_specs=whole(None),
        out_shape=jax.ShapeDtypeStruct((count, half, part), bf16),
        scratch_shapes=[pltpu.SemaphoreType.DMA((count,))],
        compiler_params=params(62),
        name="split_hidden",
    )(core, hidden)


def project_kernel(count, prompts, head, info_ref, mine_ref, other_ref, w_ref, *refs):
    outs, y_ref = refs[:-1], refs[-1]
    half, part = mine_ref.shape[1:]
    units = 2 * half * count // prompts
    rows = half * count
    core = info_ref[0]
    columns = y_ref.shape[0] * 128
    w = w_ref[:, head * columns : (head + 1) * columns]
    lower = pl.ds(pl.multiple_of(core * rows, rows), rows)
    upper = pl.ds(pl.multiple_of((1 - core) * rows, rows), rows)
    for at, ref in ((lower, mine_ref), (upper, other_ref)):
        y = jnp.dot(ref[...].reshape(rows, part), w, preferred_element_type=f32)
        for c in range(y_ref.shape[0]):
            y_ref[c, at] = y[:, c * 128 : (c + 1) * 128]
    at = 0
    for j in range(count):
        block = jnp.concatenate(
            [
                y_ref[c, pl.ds(info_ref[1 + j], units, stride=prompts)]
                for c in range(y_ref.shape[0])
            ],
            axis=1,
        )
        if j == count // 2:
            outs[at][...] = block[: units // 2].astype(bf16)
            outs[at + 1][...] = block[units // 2 :].astype(bf16)
            at += 2
        else:
            outs[at][...] = block
            at += 1


def project(info, mine, other, w, head, local, prompts):
    count, half, part = mine.shape
    columns = w.shape[1] // local
    units = 2 * half * count // prompts
    middle = count // 2
    shapes = []
    for j in range(count):
        if j == middle:
            shapes += [jax.ShapeDtypeStruct((units // 2, columns), bf16)] * 2
        else:
            shapes.append(jax.ShapeDtypeStruct((units, columns), f32))
    outs = pl.pallas_call(
        functools.partial(project_kernel, count, prompts, head),
        in_specs=[pl.BlockSpec(memory_space=pltpu.SMEM)]
        + [whole(None)] * 3,
        out_specs=[whole(None)] * len(shapes),
        scratch_shapes=[pltpu.VMEM((columns // 128, 2 * half * count, 128), f32)],
        out_shape=shapes,
        compiler_params=params(44),
        cost_estimate=pl.CostEstimate(
            flops=2 * units * count * part * columns, bytes_accessed=6 << 20, transcendentals=0
        ),
        name="project",
    )(info, mine, other, w)
    return list(outs[:middle]) + [(outs[middle], outs[middle + 1])] + list(outs[middle + 2 :])


def fetch_kernel(k_hbm, v_hbm, _, k_next, v_next, sem):
    size = k_next.shape[1] // 4
    fetches = [
        pltpu.make_async_copy(
            source.at[0, n, i * size : (i + 1) * size],
            target.at[n, i * size : (i + 1) * size],
            sem.at[h, n, i],
        )
        for n in range(k_next.shape[0])
        for i in range(4)
        for h, (source, target) in enumerate(((k_hbm, k_next), (v_hbm, v_next)))
    ]
    for fetch in fetches:
        fetch.start()
    for fetch in fetches:
        fetch.wait()


def fetch_first(keys, values, after):
    local = keys.shape[1]
    return pl.pallas_call(
        fetch_kernel,
        in_specs=[pl.BlockSpec(memory_space=pl.ANY)] * 3,
        out_specs=[whole(None)] * 2,
        out_shape=[jax.ShapeDtypeStruct((local, key_block, 128), bf16)] * 2,
        scratch_shapes=[pltpu.SemaphoreType.DMA((2, local, 4))],
        compiler_params=params(48),
        cost_estimate=pl.CostEstimate(flops=0, bytes_accessed=8 << 20, transcendentals=0),
        name="fetch_first",
    )(keys, values, after)


def rotate_kernel(local, *refs):
    sums, (bias_ref, cos_ref, sin_ref) = refs[: 3 * local], refs[3 * local : 3 * local + 3]
    q_ref, k_ref, v_ref = refs[-3:]
    cosine, sine = cos_ref[...], sin_ref[...]
    scale = log2e * 128**-0.5
    for n in range(local):
        own_ref, front_ref, back_ref = sums[3 * n : 3 * n + 3]
        columns = own_ref.shape[1]
        x = own_ref[...] + front_ref[...].astype(f32) + back_ref[...].astype(f32)
        x = x + bias_ref[:, n * columns : (n + 1) * columns]
        for g in range(group + 1):
            part = x[:, g * 128 : (g + 1) * 128]
            turned = part * cosine + pltpu.roll(part, 64, 1) * sine
            if g < group:
                at = (n * group + g) * 128
                q_ref[:, at : at + 128] = (turned * scale).astype(bf16)
            else:
                k_ref[:, n * 128 : (n + 1) * 128] = turned.astype(bf16)
        v_ref[:, n * 128 : (n + 1) * 128] = x[:, (group + 1) * 128 :].astype(bf16)


def rotate(sums, bias, cosine, sine, after):
    local = len(sums)
    units = cosine.shape[0]
    given = [part for three in sums for part in three] + [bias, cosine, sine]
    return pl.pallas_call(
        functools.partial(rotate_kernel, local),
        in_specs=[whole(None)] * len(given) + [pl.BlockSpec(memory_space=pl.ANY)] * len(after),
        out_specs=[whole(None)] * 3,
        out_shape=(
            jax.ShapeDtypeStruct((units, local * group * 128), bf16),
            jax.ShapeDtypeStruct((units, local * 128), bf16),
            jax.ShapeDtypeStruct((units, local * 128), bf16),
        ),
        compiler_params=params(),
        name="rotate",
    )(*given, *after)


def dot_nt(a, b):
    return lax.dot_general(a, b, (((1,), (1,)), ((), ())), preferred_element_type=f32)


def prompt_kernel(local, first, piece, last, q_ref, *refs):
    if first:
        kf_ref, vf_ref, bias_ref = refs[:3]
        refs = refs[3:]
    else:
        refs = refs[2:]
    k_first, v_first, k_hbm, v_hbm = refs[:4]
    rows_ref, fresh_sum, k_held, v_held, sem = refs[-5:]
    outs = refs[-9:-5] if last < 2 else refs[-7:-5]
    acc, peak = outs[:2]
    units = q_ref.shape[0]
    rows = group * units
    block = k_first.shape[1]
    steps = k_held.shape[0] + 1
    rest = []
    for i in range(1, steps):
        keys = pl.ds((piece * steps + i) * block, block)
        rest.append(
            (
                pltpu.make_async_copy(k_hbm.at[0, :, keys], k_held.at[i - 1], sem.at[i, 0]),
                pltpu.make_async_copy(v_hbm.at[0, :, keys], v_held.at[i - 1], sem.at[i, 1]),
            )
        )
    if last == 0:
        keys = pl.ds((piece + 1) * steps * block, block)
        sources = [k_hbm.at[0, :, keys], v_hbm.at[0, :, keys]]
        targets = outs[2:]
    elif last == 1:
        ids_ref, ks_hbm, vs_hbm = refs[4:7]
        prompt = ids_ref[ids_ref.shape[0] // 2]
        sources = [ks_hbm.at[:, prompt], vs_hbm.at[:, prompt]]
        targets = [ref.at[0] for ref in outs[2:]]
    if last < 2:
        rest.append(
            [pltpu.make_async_copy(sources[h], targets[h], sem.at[0, h]) for h in range(2)]
        )
    for pair in rest:
        for copy in pair:
            copy.start()

    for n in range(local):
        for g in range(group):
            at = (n * group + g) * 128
            rows_ref[n, g * units : (g + 1) * units] = q_ref[:, at : at + 128]
        if first:
            head = slice(n * 128, (n + 1) * 128)
            bias = jnp.concatenate([bias_ref[...]] * group)
            s = dot_nt(rows_ref[n], kf_ref[:, head]) + bias
            top = jnp.max(s, axis=1, keepdims=True)
            p = jnp.exp2(s - top).astype(bf16)
            v = jnp.concatenate([vf_ref[:, head], jnp.ones((units, 128), bf16)], axis=1)
            acc[n] = jnp.dot(p, v, preferred_element_type=f32)
            peak[n] = jnp.broadcast_to(top, (rows, 128))

    ones = jnp.ones((block, 128), bf16)
    cut = rows // 4
    spots = [(n, slice(r * cut, (r + 1) * cut)) for n in range(local) for r in range(4)]
    for i in range(steps):
        k_ref, v_ref = (k_first, v_first) if i == 0 else (k_held.at[i - 1], v_held.at[i - 1])
        if i > 0:
            for copy in rest[i - 1]:
                copy.wait()
        over = None
        for n, at in spots:
            s = dot_nt(rows_ref[n, at], k_ref[n])
            level = peak[n, at]
            lifted = [s[:, c : c + 128] - level for c in range(0, block, 128)]
            most = functools.reduce(jnp.maximum, lifted)
            over = most if over is None else jnp.maximum(over, most)
            p = jnp.concatenate([jnp.exp2(x).astype(bf16) for x in lifted], axis=1)
            values = jnp.concatenate([v_ref[n], ones], axis=1)
            fresh_sum[n, at] = jnp.dot(p, values, preferred_element_type=f32)
        worst = jnp.max(over)

        @pl.when(worst < lift_limit)
        def _():
            acc[...] += fresh_sum[...]

        @pl.when(worst >= lift_limit)
        def _(k_ref=k_ref, v_ref=v_ref):
            for n, at in spots:
                s = dot_nt(rows_ref[n, at], k_ref[n])
                before = peak[n, at]
                now = jnp.maximum(before, jnp.max(s, axis=1, keepdims=True))
                peak[n, at] = now
                p = jnp.exp2(s - jnp.concatenate([now] * (block // 128), axis=1)).astype(bf16)
                fade = jnp.exp2(before - now)
                values = jnp.concatenate([v_ref[n], ones], axis=1)
                acc[n, at] = acc[n, at] * jnp.concatenate([fade, fade], axis=1) + jnp.dot(
                    p, values, preferred_element_type=f32
                )

    if last < 2:
        for copy in rest[-1]:
            copy.wait()


def prompt_piece(queries, fresh, state, block, keys, values, piece, ids, suffix):
    units = queries.shape[0]
    local = keys.shape[1]
    rows = group * units
    first = state is None
    last = max(piece + 3 - pieces, 0)
    steps = keys.shape[2] // pieces // key_block
    length = steps * key_block
    acc_shape, peak_shape = (local, rows, 256), (local, rows, 128)
    given = [queries, *(fresh if first else state), *block]
    hbm = [keys, values]
    following = block[0].shape
    if last == 1:
        slots, _, _, span, _ = suffix[0].shape
        following = (1, slots, local, span, 128)
    anywhere = pl.BlockSpec(memory_space=pl.ANY)
    outs = pl.pallas_call(
        functools.partial(prompt_kernel, local, first, piece, last),
        in_specs=[whole(None)] * len(given)
        + [anywhere] * 2
        + ([pl.BlockSpec(memory_space=pltpu.SMEM), anywhere, anywhere] if last == 1 else []),
        out_specs=[whole(None)] * (4 if last < 2 else 2),
        out_shape=(
            jax.ShapeDtypeStruct(acc_shape, f32),
            jax.ShapeDtypeStruct(peak_shape, f32),
            *([jax.ShapeDtypeStruct(following, bf16)] * (2 if last < 2 else 0)),
        ),
        input_output_aliases={} if first else {1: 0, 2: 1},
        scratch_shapes=[
            pltpu.VMEM((local, rows, 128), bf16),
            pltpu.VMEM(acc_shape, f32),
            pltpu.VMEM((steps - 1, local, key_block, 128), bf16),
            pltpu.VMEM((steps - 1, local, key_block, 128), bf16),
            pltpu.SemaphoreType.DMA((steps, 2)),
        ],
        compiler_params=params(prompt_vmem),
        cost_estimate=pl.CostEstimate(
            flops=local * rows * length * 1536,
            bytes_accessed=local * length * 512,
            transcendentals=local * rows * length,
        ),
        name="prompt_attention",
    )(*given, *hbm, *((ids, *suffix) if last == 1 else ()))
    return outs


def suffix_kernel(local, members, following, split, tiles_ref, lens_ref, ids_ref, *refs):
    parts = 2 if split else 1
    listed = parts * len(members)
    q_refs = refs[:listed]
    code_ref, k_ref, v_ref = refs[listed : listed + 3]
    hbm = refs[listed + 3 : listed + 5]
    fetched = 2
    tail = refs[-listed - fetched - 2 :]
    outs, nexts, (acc, sem) = tail[:listed], tail[listed : listed + fetched], tail[-2:]
    units = parts * q_refs[0].shape[0]
    slots = k_ref.shape[1]
    keys = k_ref.shape[3]
    tile = tile_units
    wide = group * 128
    span = local * group
    fetches = []
    if following:
        for c, j in enumerate(following):
            prompt = ids_ref[j]
            for h in range(2):
                fetches.append(
                    pltpu.make_async_copy(hbm[h].at[:, prompt], nexts[h].at[c], sem.at[c, h])
                )
    else:
        block = nexts[0].shape[1]
        keys_at = pl.ds(hbm[0].shape[2] // pieces * (pieces - 1), block)
        for h in range(2):
            fetches.append(
                pltpu.make_async_copy(hbm[h].at[0, :, keys_at], nexts[h], sem.at[0, h])
            )
    for fetch in fetches:
        fetch.start()

    prompts = [ids_ref[j] for j in members]
    acc[...] = jnp.zeros_like(acc)
    key = lax.broadcasted_iota(jnp.int32, (1, keys), 1)
    ones = jnp.ones((keys, 128), bf16)
    lane = lax.broadcasted_iota(jnp.int32, (slots * tile, 128), 1)
    chains = [(n, w) for n in range(local) for w in range(slots)]

    def body(t, _):
        spot = lax.broadcasted_iota(jnp.int32, (tile, units), 0) + t * tile
        picks, rows = [], {}
        for c, prompt in enumerate(prompts):
            pick = jnp.concatenate(
                [
                    jnp.where(code_ref[prompt, w : w + 1, :] == spot, 1.0, 0.0)
                    for w in range(slots)
                ]
            ).astype(bf16)
            picks.append(pick)
            q = jnp.concatenate([ref[...] for ref in q_refs[c * parts : (c + 1) * parts]])
            chosen = jnp.dot(pick, q, preferred_element_type=f32).astype(bf16)
            for n, w in chains:
                rows[c, n, w] = jnp.concatenate(
                    [
                        chosen[w * tile : (w + 1) * tile, at : at + 128]
                        for at in range(n * wide, (n + 1) * wide, 128)
                    ],
                    axis=0,
                )

        def score(c, n, w):
            limit = jnp.where(key < lens_ref[w, prompts[c]], 0.0, masked_score)
            return dot_nt(rows[c, n, w], k_ref[c, w, n]) + limit

        def weigh(c, n, w, p):
            values = jnp.concatenate([v_ref[c, w, n], ones], axis=1)
            return jnp.dot(p.astype(bf16), values, preferred_element_type=f32)

        def by_lane(found, c):
            out = jnp.zeros((slots * tile, 128), f32)
            for n in range(local):
                for g in range(group):
                    at = slice(g * tile, (g + 1) * tile)
                    part = jnp.concatenate([found[c, n, w][at] for w in range(slots)])
                    out = jnp.where(lane % span == n * group + g, part, out)
            high = out.astype(bf16).astype(f32)
            rest = out - high
            mid = rest.astype(bf16).astype(f32)
            low = rest - mid
            third = lane // span % 3
            return jnp.where(third == 0, high, jnp.where(third == 1, mid, low))

        def add(sums, tops):
            for c in range(len(members)):
                packed = by_lane({k: x[:, 128:] for k, x in sums.items()}, c)
                packed = jnp.where(lane // span < 6, packed, 0.0)
                levels = 0.0 if tops is None else by_lane(tops, c)
                packed = jnp.where(lane // span < 3, levels, packed).astype(bf16)
                result = [
                    jnp.concatenate(
                        [
                            sums[c, n, w][g * tile : (g + 1) * tile, :128].astype(bf16)
                            for w in range(slots)
                        ]
                    )
                    for n in range(local)
                    for g in range(group)
                ]
                acc[c] += lax.dot_general(
                    picks[c],
                    jnp.concatenate([*result, packed], axis=1),
                    (((0,), (0,)), ((), ())),
                    preferred_element_type=f32,
                )

        sums, over, under = {}, None, None
        for c in range(len(members)):
            for n, w in chains:
                s = score(c, n, w)
                most = functools.reduce(
                    jnp.maximum, [s[:, i : i + 128] for i in range(0, keys, 128)]
                )
                over = most if over is None else jnp.maximum(over, most)
                o = weigh(c, n, w, jnp.exp2(s))
                under = o[:, 128:] if under is None else jnp.minimum(under, o[:, 128:])
                sums[c, n, w] = o
        plain = (jnp.max(over) < lift_limit) & (jnp.min(under) > 2.0**-lift_limit)

        @pl.when(plain)
        def _():
            add(sums, None)

        @pl.when(jnp.logical_not(plain))
        def _():
            sums, tops = {}, {}
            for c in range(len(members)):
                for n, w in chains:
                    s = score(c, n, w)
                    top = jnp.max(s, axis=1, keepdims=True)
                    sums[c, n, w] = weigh(c, n, w, jnp.exp2(s - top))
                    tops[c, n, w] = jnp.broadcast_to(top, (s.shape[0], 128))
            add(sums, tops)

        return 0

    count = tiles_ref[prompts[0]]
    for prompt in prompts[1:]:
        count = jnp.maximum(count, tiles_ref[prompt])
    lax.fori_loop(0, count, body, 0)
    size = units // parts
    for c in range(len(members)):
        for h in range(parts):
            outs[c * parts + h][...] = acc[c, h * size : (h + 1) * size].astype(bf16)
    for fetch in fetches:
        fetch.wait()


def suffix_attention(tables, found, members, following, split, block, hbm, after):
    tiles, lens, ids, code = tables
    _, slots, local, span, _ = block[0].shape
    listed = flat([found[j] for j in members])
    parts = 2 if split else 1
    units = parts * listed[0].shape[0]
    width = local * group * 128 + 128
    shapes = [jax.ShapeDtypeStruct((units // parts, width), bf16)] * len(listed)
    if following:
        shapes += [jax.ShapeDtypeStruct((len(following), slots, local, span, 128), bf16)] * 2
    else:
        shapes += [jax.ShapeDtypeStruct((local, key_block, 128), bf16)] * 2
    smem = pl.BlockSpec(memory_space=pltpu.SMEM)
    anywhere = pl.BlockSpec(memory_space=pl.ANY)
    result = pl.pallas_call(
        functools.partial(suffix_kernel, local, members, following, split),
        in_specs=[smem] * 3
        + [whole(None)] * (len(listed) + 3)
        + [anywhere] * (len(hbm) + len(after)),
        out_specs=[whole(None)] * len(shapes),
        out_shape=shapes,
        scratch_shapes=[
            pltpu.VMEM((len(members), units, width), f32),
            pltpu.SemaphoreType.DMA((max(len(following), 1), 2)),
        ],
        compiler_params=params(suffix_vmem),
        cost_estimate=pl.CostEstimate(
            flops=len(members) << 30, bytes_accessed=1 << 20, transcendentals=len(members) << 19
        ),
        name="suffix_attention",
    )(tiles, lens, ids, *listed, code, *block, *hbm, *after)
    sums, block = result[: len(listed)], result[len(listed) :]
    return [tuple(sums)] if split else list(sums), block


def merge_kernel(local, acc_ref, peak_ref, own_ref, front_ref, back_ref, *outs):
    units = outs[0].shape[0]
    span = local * group
    wide = local * group * 128
    part = own_ref[...].astype(f32) + front_ref[...].astype(f32) + back_ref[...].astype(f32)
    stats = part[:, wide:]
    for n in range(local):
        for g in range(group):
            at = slice(g * units, (g + 1) * units)
            lane = n * group + g
            level, total = (
                sum(stats[:, i * span + lane : i * span + lane + 1] for i in range(h, h + 3))
                for h in (0, 3)
            )
            peak = peak_ref[n, at]
            top = jnp.maximum(peak, level)
            one = jnp.exp2(peak - top)
            two = jnp.exp2(level - top)
            mixed = acc_ref[n, at, :128] * one + part[:, lane * 128 : (lane + 1) * 128] * two
            outs[n][:, g * 128 : (g + 1) * 128] = (
                mixed / (acc_ref[n, at, 128:] * one + total * two)
            ).astype(bf16)


def merge(state, sums, local):
    units = sums[0].shape[0]
    given = [*state, *sums]
    return pl.pallas_call(
        functools.partial(merge_kernel, local),
        in_specs=[whole(None)] * len(given),
        out_specs=[whole(None)] * local,
        out_shape=[jax.ShapeDtypeStruct((units, group * 128), bf16)] * local,
        compiler_params=params(8),
        name="merge",
    )(*given)


def output_kernel(local, members, middle, halves, info_ref, w_ref, *refs):
    early = len(halves) == 2
    if early:
        *refs, w_held, sem = refs
        size = w_held.shape[0] // sem.shape[0]
        fetches = [
            pltpu.make_async_copy(
                w_ref.at[i * size : (i + 1) * size], w_held.at[i * size : (i + 1) * size], sem.at[i]
            )
            for i in range(sem.shape[0])
        ]
        for fetch in fetches:
            fetch.start()
        w_ref = w_held
    outs = refs[-2 * len(halves) :]
    contexts = refs[: local * (len(members) + (middle in members))]
    per_head = len(contexts) // local
    units = sum(contexts[i].shape[0] for i in range(per_head)) // len(members)
    x = jnp.concatenate(
        [
            jnp.concatenate([ref[...] for ref in contexts[n * per_head : (n + 1) * per_head]])
            for n in range(local)
        ],
        axis=1,
    )
    width = outs[0].shape[1]
    depth = x.shape[1] // 2
    if early:
        for fetch in fetches[: len(fetches) // 2]:
            fetch.wait()
        started = [
            jnp.dot(
                x[:, :depth],
                w_ref[:depth, column * width : (column + 1) * width],
                preferred_element_type=f32,
            )
            for column in halves
        ]
        for fetch in fetches[len(fetches) // 2 :]:
            fetch.wait()
    for h, column in enumerate(halves):
        w = w_ref[:, column * width : (column + 1) * width]
        if early:
            y = jnp.dot(x[:, depth:], w[depth:], preferred_element_type=f32) + started[h]
        else:
            y = jnp.dot(x, w, preferred_element_type=f32)
        y = y.astype(bf16)
        for at, j in enumerate(members):
            rows = pl.ds(pl.multiple_of(info_ref[1, j] * units, units), units)
            for away in range(2):

                @pl.when(info_ref[0, j] == away)
                def _(at=at, away=away, rows=rows, h=h, y=y):
                    outs[2 * h + away][rows] = y[at * units : (at + 1) * units]


def output(info, contexts, members, halves, w, blocks, held):
    local = len(contexts)
    count = len(contexts[0])
    units = contexts[0][0].shape[0]
    listed = [block for found in contexts for block in flat([found[j] for j in members])]
    held = [] if held is None else list(held)
    outs = 2 * len(halves)
    given = 2 + len(listed)
    early = len(halves) == 2
    shapes = [jax.ShapeDtypeStruct((blocks * units, w.shape[1] // 2), bf16)] * outs
    return pl.pallas_call(
        functools.partial(output_kernel, local, members, count // 2, halves),
        in_specs=[pl.BlockSpec(memory_space=pltpu.SMEM)]
        + [pl.BlockSpec(memory_space=pl.ANY) if early else whole(None)]
        + [whole(None)] * (len(listed) + len(held)),
        out_specs=[whole(None)] * (outs + early),
        out_shape=shapes + ([jax.ShapeDtypeStruct(w.shape, w.dtype)] if early else []),
        scratch_shapes=[pltpu.SemaphoreType.DMA((16,))] if early else [],
        input_output_aliases={given + i: i for i in range(len(held))},
        compiler_params=params(output_vmem if early else 16),
        cost_estimate=pl.CostEstimate(
            flops=len(members) * units * w.shape[0] * w.shape[1] * len(halves),
            bytes_accessed=2 << 20,
            transcendentals=0,
        ),
        name="output_projection",
    )(info, w, *listed, *held)


def finish_kernel(steps, local, count, *refs):
    terms, o_ref = refs[:-1], refs[-1]
    rows, width_out = o_ref.shape
    per = rows // (steps * local * count)
    width = local * count
    total = jnp.concatenate(
        [
            sum(term[:rows].astype(f32) for term in terms[h * len(terms) // 2 : (h + 1) * len(terms) // 2])
            for h in range(2)
        ],
        axis=1,
    )
    i = lax.broadcasted_iota(jnp.int32, (rows, rows), 1)
    t = lax.broadcasted_iota(jnp.int32, (rows, rows), 0)
    slot = i // (steps * width)
    part = (i // (steps // 2 * width)) % 2
    source = (i // (steps // 2 * local)) % count
    step = part * (steps // 2) + (i // local) % (steps // 2)
    target = (step * width + source * local + i % local) * per + slot
    perm = jnp.where(t == target, 1.0, 0.0).astype(bf16)
    o_ref[...] = jnp.dot(perm, total.astype(bf16), preferred_element_type=f32).astype(bf16)


def finish(terms, rows, steps, local, count):
    return pl.pallas_call(
        functools.partial(finish_kernel, steps, local, count),
        in_specs=[whole(None)] * len(terms),
        out_specs=whole(None),
        out_shape=jax.ShapeDtypeStruct((rows, 2 * terms[0].shape[1]), bf16),
        compiler_params=params(8),
        name="finish",
    )(*terms)


def shards(
    hidden,
    w_qkv,
    qkv_bias,
    prompt_keys,
    prompt_values,
    suffix_keys,
    suffix_values,
    w_out,
    parents,
    lengths,
):
    count = lax.axis_size("beam")
    heads = lax.axis_size("head")
    beam = lax.axis_index("beam").astype(jnp.int32)
    head = lax.axis_index("head").astype(jnp.int32)
    steps, local_slots, prompts, _ = hidden.shape
    local = prompt_keys.shape[1]
    prompt_len = prompt_keys.shape[2]
    width = local_slots * count
    units = steps * width
    place = ring_place(beam, count)
    core = head % 2
    partner = [(j, j ^ 1) for j in range(heads)]

    rows = hidden.reshape(steps * local_slots * prompts, hidden.shape[3])
    mine = lax.all_to_all(
        split_hidden(rows, core.reshape(1), count), "beam", split_axis=0, concat_axis=0, tiled=True
    )
    other = lax.ppermute(mine, "head", partner)

    roots, starts, chain = lineage_tables(parents, lengths)
    half = steps // 2

    def by_unit(table):
        table = table.reshape(2, half, count, local_slots, prompts)
        return jnp.transpose(table, (4, 0, 2, 1, 3)).reshape(prompts, units)

    unit_roots = by_unit(roots)
    unit_steps = jnp.arange(steps, dtype=jnp.int32).reshape(2, 1, half, 1)
    unit_steps = jnp.broadcast_to(unit_steps, (2, count, half, local_slots)).reshape(units)
    positions = prompt_len + lax.dynamic_index_in_dim(by_unit(starts), beam, 0, False) + unit_steps
    frequency = rope_base ** (-(jnp.arange(64, dtype=f32) * 2.0 / 128))
    angles = positions.astype(f32)[:, None] * frequency
    cosine, sine = jnp.cos(angles), jnp.sin(angles)
    cosine = jnp.concatenate([cosine, cosine], axis=1)
    sine = jnp.concatenate([-sine, sine], axis=1)
    slot_ids = beam * local_slots + jnp.arange(local_slots, dtype=jnp.int32)
    owned = unit_roots[:, None, :] == slot_ids[:, None]
    upto = jnp.arange(units)[:, None] <= jnp.arange(units)[None, :]
    ranks = jnp.einsum(
        "pwu,uv->pwv", owned.astype(f32), upto.astype(f32), preferred_element_type=f32
    ).astype(jnp.int32)
    code = jnp.where(owned, ranks - 1, -1)
    tiles = (jnp.max(ranks[:, :, -1], axis=1) + tile_units - 1) // tile_units
    lens = lax.dynamic_slice_in_dim(lengths, beam * local_slots, local_slots, 0)
    places = (place + jnp.arange(count, dtype=jnp.int32)) % count
    ids = ring_member(places, count)
    own_chain = lax.dynamic_index_in_dim(chain, beam, 3, False)
    linked = own_chain[..., None] == jnp.arange(width, dtype=jnp.int32)
    linked = linked.reshape(2, half, 2, half, count, local_slots, count, local_slots)
    linked = jnp.transpose(linked, (0, 4, 1, 5, 2, 6, 3, 7)).reshape(units, units)
    fresh_bias = jnp.where(linked, 0.0, masked_score).astype(f32)

    info = jnp.concatenate([core.reshape(1), ids])
    sums = []
    for n in range(local):
        blocks = project(info, mine, other, w_qkv, n, local, prompts)
        front, back, mark = scatter_ring(blocks, count)
        sums.append((blocks[0], front, back))
    block = fetch_first(prompt_keys, prompt_values, mark)
    queries, fresh_keys, fresh_values = rotate(
        sums, qkv_bias.reshape(1, -1), cosine, sine, (block[0], fresh_bias, code)
    )

    gathered = gather_ring(queries, count)
    def attend(state, block, piece):
        outs = prompt_piece(
            queries,
            (fresh_keys, fresh_values, fresh_bias),
            state,
            block,
            prompt_keys,
            prompt_values,
            piece,
            ids,
            (suffix_keys, suffix_values),
        )
        return outs[:2], outs[2:]

    state = None
    for piece in range(pieces - 1):
        state, block = attend(state, block, piece)

    middle = count // 2
    held = [block]

    def members(step):
        return (step,) if step in (0, middle) else (step, count - step)

    def produce(step, after):
        made, held[0] = suffix_attention(
            (tiles, lens, ids, code),
            gathered,
            members(step),
            members(step - 1) if step > 0 else (),
            step == middle,
            held[0],
            (suffix_keys, suffix_values) if step > 0 else (prompt_keys, prompt_values),
            after,
        )
        return made

    sums = return_ring(produce, (), count)
    state, _ = attend(state, held[0], pieces - 1)
    contexts = merge(state, sums, local)

    per = prompts // heads
    chips = heads // 2
    targets = ids // per
    away = (targets % 2) ^ core
    turn = (targets // 2 - head // 2) % chips
    info = jnp.stack([away, turn * per + ids % per]).astype(jnp.int32)
    late = (middle - 1, middle, middle + 1)
    early = tuple(j for j in range(count) if j not in late)
    contexts = [gather_ring(context, count) for context in contexts]
    *held, w_held = output(info, contexts, early, (0, 1), w_out, chips * per, None)
    rows = per * units
    terms = []
    for h in range(2):
        keep, send = output(
            info, contexts, late, (h,), w_held, chips * per, held[2 * h : 2 * h + 2]
        )
        came = lax.ppermute(send, "head", partner)
        terms += [keep, came]
        for i in range(1, chips):
            at = slice(i * rows, (i + 1) * rows)
            far = (keep[at].astype(f32) + came[at].astype(f32)).astype(bf16)
            pairs = [(j, (j + 2 * i) % heads) for j in range(heads)]
            terms.append(lax.ppermute(far, "head", pairs))
    result = finish(terms, rows, steps, local_slots, count)
    return result.reshape(steps, width, per, result.shape[1])


def solution(mesh):
    return jax.shard_map(
        shards,
        mesh=mesh,
        in_specs=(
            P(None, "beam", None, None),
            P("beam", "head"),
            P("head"),
            P("beam", "head", None, None),
            P("beam", "head", None, None),
            P("beam", None, "head", None, None),
            P("beam", None, "head", None, None),
            P("head", "beam"),
            P(),
            P(),
        ),
        out_specs=P(None, None, "head", "beam"),
        check_vma=False,
    )
```

```python
import functools

import jax
import jax.numpy as jnp
from jax import lax
from jax.experimental import pallas as pl
from jax.experimental.pallas import tpu as pltpu
from jax.sharding import PartitionSpec as P

rope_base = 1000000.0
masked_score = -1e30
log2e = 1.4426950408889634
group = 8
bf16 = jnp.bfloat16
f32 = jnp.float32
key_block = 2048
pieces = 4
tile_units = 32
lift_limit = 64.0
prompt_vmem = 46
output_vmem = 45
suffix_vmem = 48


def params(vmem_mib=24):
    return pltpu.CompilerParams(vmem_limit_bytes=vmem_mib << 20)


def whole(_):
    return pl.BlockSpec(memory_space=pltpu.VMEM)


def ring_order(count):
    return list(range(0, count, 2)) + list(range(count - 1, 0, -2))


def ring_pairs(count):
    order = ring_order(count)
    forward = [(order[i], order[(i + 1) % count]) for i in range(count)]
    return forward, [(b, a) for a, b in forward]


def ring_place(index, count):
    return jnp.where(index % 2 == 0, index // 2, count - 1 - index // 2)


def ring_member(place, count):
    return jnp.where(place < count // 2, 2 * place, 2 * (count - 1 - place) + 1)


def relay_kernel(ahead_ref, behind_ref, _, front_ref, back_ref):
    half = front_ref.shape[0]
    front_ref[...] = ahead_ref[:half]
    back_ref[...] = behind_ref[half:]


def relay(ahead, behind, after):
    rows, columns = ahead.shape
    return pl.pallas_call(
        relay_kernel,
        in_specs=[whole(None)] * 2 + [pl.BlockSpec(memory_space=pl.ANY)],
        out_specs=[whole(None)] * 2,
        out_shape=[jax.ShapeDtypeStruct((rows // 2, columns), bf16)] * 2,
        compiler_params=params(8),
        name="relay",
    )(ahead, behind, after)


def gather_ring(block, count, after=None):
    forward, backward = ring_pairs(count)
    middle = count // 2
    half = block.shape[0] // 2
    found = [None] * count
    found[0] = block
    ahead = behind = block
    for step in range(1, middle):
        ahead = lax.ppermute(ahead, "beam", forward)
        behind = lax.ppermute(behind, "beam", backward)
        found[count - step] = ahead
        found[step] = behind
    if after is None:
        ahead, behind = ahead[:half], behind[half:]
    else:
        ahead, behind = relay(ahead, behind, after)
    found[middle] = (
        lax.ppermute(ahead, "beam", forward),
        lax.ppermute(behind, "beam", backward),
    )
    return found


def scatter_ring(blocks, count):
    forward, backward = ring_pairs(count)
    middle = count // 2
    ahead, behind = blocks[middle]
    half = ahead.shape[0]
    for step in range(middle - 1, -1, -1):
        ahead = lax.ppermute(ahead, "beam", forward)
        behind = lax.ppermute(behind, "beam", backward)
        if step == 0:
            break
        front = blocks[step].astype(f32)
        back = blocks[count - step].astype(f32)
        ahead = ahead.astype(f32)
        behind = behind.astype(f32)
        if step == middle - 1:
            ahead = jnp.concatenate([ahead + front[:half], front[half:]])
            behind = jnp.concatenate([back[:half], behind + back[half:]])
        else:
            ahead = ahead + front
            behind = behind + back
        ahead = ahead.astype(bf16)
        behind = behind.astype(bf16)
        mark = ahead if step == middle - 1 else mark
    return ahead, behind, mark


def return_ring(produce, after, count):
    forward, backward = ring_pairs(count)
    middle = count // 2
    ((ahead, behind),) = produce(middle, after)
    half = ahead.shape[0]
    for step in range(middle - 1, -1, -1):
        marker = (ahead, behind)
        ahead = lax.ppermute(ahead, "beam", forward)
        behind = lax.ppermute(behind, "beam", backward)
        if step == 0:
            return ahead, behind
        made = produce(step, marker)
        front, back = (block.astype(f32) for block in made)
        one, two = ahead.astype(f32), behind.astype(f32)
        if step == middle - 1:
            one = jnp.concatenate([one + front[:half], front[half:]])
            two = jnp.concatenate([back[:half], two + back[half:]])
        else:
            one, two = one + front, two + back
        ahead, behind = one.astype(bf16), two.astype(bf16)


def flat(found):
    listed = []
    for block in found:
        listed.extend(block if isinstance(block, tuple) else (block,))
    return listed


def lineage_kernel(parents_ref, lengths_ref, roots_ref, starts_ref, chain_ref):
    steps, width, prompts = parents_ref.shape

    def take(table, chosen):
        out = jnp.zeros_like(chosen)
        for j in range(width):
            out = jnp.where(chosen == j, table[j : j + 1, :], out)
        return out

    own = lax.broadcasted_iota(jnp.int32, (width, prompts), 0)
    lengths = lengths_ref[...]
    for s in range(steps):
        current = own
        for t in range(steps - 1, s, -1):
            chain_ref[s, t] = own - width
        chain_ref[s, s] = own
        for t in range(s, 0, -1):
            current = take(parents_ref[t], current)
            chain_ref[s, t - 1] = current
        root = take(parents_ref[0], current)
        roots_ref[s] = root
        starts_ref[s] = take(lengths, root)


def lineage_tables(parents, lengths):
    steps, width, prompts = parents.shape
    return pl.pallas_call(
        lineage_kernel,
        in_specs=[whole(None)] * 2,
        out_specs=[whole(None)] * 3,
        out_shape=(
            jax.ShapeDtypeStruct((steps, width, prompts), jnp.int32),
            jax.ShapeDtypeStruct((steps, width, prompts), jnp.int32),
            jax.ShapeDtypeStruct((steps, steps, width, prompts), jnp.int32),
        ),
        compiler_params=params(8),
        name="lineage",
    )(parents, lengths)


def split_kernel(core_ref, x_ref, o_ref, sem):
    count, half, part = o_ref.shape
    rows = pl.ds(pl.multiple_of(core_ref[0] * half, half), half)
    copies = [
        pltpu.make_async_copy(x_ref.at[rows, b * part : (b + 1) * part], o_ref.at[b], sem.at[b])
        for b in range(count)
    ]
    for copy in copies:
        copy.start()
    for copy in copies:
        copy.wait()


def split_hidden(hidden, core, count):
    rows, width = hidden.shape
    half, part = rows // 2, width // count
    return pl.pallas_call(
        split_kernel,
        in_specs=[pl.BlockSpec(memory_space=pltpu.SMEM), pl.BlockSpec(memory_space=pltpu.HBM)],
        out_specs=whole(None),
        out_shape=jax.ShapeDtypeStruct((count, half, part), bf16),
        scratch_shapes=[pltpu.SemaphoreType.DMA((count,))],
        compiler_params=params(62),
        name="split_hidden",
    )(core, hidden)


def project_kernel(count, prompts, head, info_ref, mine_ref, other_ref, w_ref, *refs):
    outs, y_ref = refs[:-1], refs[-1]
    half, part = mine_ref.shape[1:]
    units = 2 * half * count // prompts
    rows = half * count
    core = info_ref[0]
    columns = y_ref.shape[0] * 128
    w = w_ref[:, head * columns : (head + 1) * columns]
    lower = pl.ds(pl.multiple_of(core * rows, rows), rows)
    upper = pl.ds(pl.multiple_of((1 - core) * rows, rows), rows)
    for at, ref in ((lower, mine_ref), (upper, other_ref)):
        y = jnp.dot(ref[...].reshape(rows, part), w, preferred_element_type=f32)
        for c in range(y_ref.shape[0]):
            y_ref[c, at] = y[:, c * 128 : (c + 1) * 128]
    at = 0
    for j in range(count):
        block = jnp.concatenate(
            [
                y_ref[c, pl.ds(info_ref[1 + j], units, stride=prompts)]
                for c in range(y_ref.shape[0])
            ],
            axis=1,
        )
        if j == count // 2:
            outs[at][...] = block[: units // 2].astype(bf16)
            outs[at + 1][...] = block[units // 2 :].astype(bf16)
            at += 2
        else:
            outs[at][...] = block
            at += 1


def project(info, mine, other, w, head, local, prompts):
    count, half, part = mine.shape
    columns = w.shape[1] // local
    units = 2 * half * count // prompts
    middle = count // 2
    shapes = []
    for j in range(count):
        if j == middle:
            shapes += [jax.ShapeDtypeStruct((units // 2, columns), bf16)] * 2
        else:
            shapes.append(jax.ShapeDtypeStruct((units, columns), f32))
    outs = pl.pallas_call(
        functools.partial(project_kernel, count, prompts, head),
        in_specs=[pl.BlockSpec(memory_space=pltpu.SMEM)]
        + [whole(None)] * 3,
        out_specs=[whole(None)] * len(shapes),
        scratch_shapes=[pltpu.VMEM((columns // 128, 2 * half * count, 128), f32)],
        out_shape=shapes,
        compiler_params=params(44),
        cost_estimate=pl.CostEstimate(
            flops=2 * units * count * part * columns, bytes_accessed=6 << 20, transcendentals=0
        ),
        name="project",
    )(info, mine, other, w)
    return list(outs[:middle]) + [(outs[middle], outs[middle + 1])] + list(outs[middle + 2 :])


def fetch_kernel(k_hbm, v_hbm, _, k_next, v_next, sem):
    size = k_next.shape[1] // 4
    fetches = [
        pltpu.make_async_copy(
            source.at[0, n, i * size : (i + 1) * size],
            target.at[n, i * size : (i + 1) * size],
            sem.at[h, n, i],
        )
        for n in range(k_next.shape[0])
        for i in range(4)
        for h, (source, target) in enumerate(((k_hbm, k_next), (v_hbm, v_next)))
    ]
    for fetch in fetches:
        fetch.start()
    for fetch in fetches:
        fetch.wait()


def fetch_first(keys, values, after):
    local = keys.shape[1]
    return pl.pallas_call(
        fetch_kernel,
        in_specs=[pl.BlockSpec(memory_space=pl.ANY)] * 3,
        out_specs=[whole(None)] * 2,
        out_shape=[jax.ShapeDtypeStruct((local, key_block, 128), bf16)] * 2,
        scratch_shapes=[pltpu.SemaphoreType.DMA((2, local, 4))],
        compiler_params=params(48),
        cost_estimate=pl.CostEstimate(flops=0, bytes_accessed=8 << 20, transcendentals=0),
        name="fetch_first",
    )(keys, values, after)


def rotate_kernel(local, *refs):
    sums, (bias_ref, cos_ref, sin_ref) = refs[: 3 * local], refs[3 * local : 3 * local + 3]
    q_ref, k_ref, v_ref = refs[-3:]
    cosine, sine = cos_ref[...], sin_ref[...]
    scale = log2e * 128**-0.5
    for n in range(local):
        own_ref, front_ref, back_ref = sums[3 * n : 3 * n + 3]
        columns = own_ref.shape[1]
        x = own_ref[...] + front_ref[...].astype(f32) + back_ref[...].astype(f32)
        x = x + bias_ref[:, n * columns : (n + 1) * columns]
        for g in range(group + 1):
            part = x[:, g * 128 : (g + 1) * 128]
            turned = part * cosine + pltpu.roll(part, 64, 1) * sine
            if g < group:
                at = (n * group + g) * 128
                q_ref[:, at : at + 128] = (turned * scale).astype(bf16)
            else:
                k_ref[:, n * 128 : (n + 1) * 128] = turned.astype(bf16)
        v_ref[:, n * 128 : (n + 1) * 128] = x[:, (group + 1) * 128 :].astype(bf16)


def rotate(sums, bias, cosine, sine, after):
    local = len(sums)
    units = cosine.shape[0]
    given = [part for three in sums for part in three] + [bias, cosine, sine]
    return pl.pallas_call(
        functools.partial(rotate_kernel, local),
        in_specs=[whole(None)] * len(given) + [pl.BlockSpec(memory_space=pl.ANY)] * len(after),
        out_specs=[whole(None)] * 3,
        out_shape=(
            jax.ShapeDtypeStruct((units, local * group * 128), bf16),
            jax.ShapeDtypeStruct((units, local * 128), bf16),
            jax.ShapeDtypeStruct((units, local * 128), bf16),
        ),
        compiler_params=params(),
        name="rotate",
    )(*given, *after)


def dot_nt(a, b):
    return lax.dot_general(a, b, (((1,), (1,)), ((), ())), preferred_element_type=f32)


def prompt_kernel(local, first, piece, last, q_ref, *refs):
    if first:
        kf_ref, vf_ref, bias_ref = refs[:3]
        refs = refs[3:]
    else:
        refs = refs[2:]
    k_first, v_first, k_hbm, v_hbm = refs[:4]
    rows_ref, fresh_sum, k_held, v_held, sem = refs[-5:]
    outs = refs[-9:-5] if last < 2 else refs[-7:-5]
    acc, peak = outs[:2]
    units = q_ref.shape[0]
    rows = group * units
    block = k_first.shape[1]
    steps = k_held.shape[0] + 1
    rest = []
    for i in range(1, steps):
        keys = pl.ds((piece * steps + i) * block, block)
        rest.append(
            (
                pltpu.make_async_copy(k_hbm.at[0, :, keys], k_held.at[i - 1], sem.at[i, 0]),
                pltpu.make_async_copy(v_hbm.at[0, :, keys], v_held.at[i - 1], sem.at[i, 1]),
            )
        )
    if last == 0:
        keys = pl.ds((piece + 1) * steps * block, block)
        sources = [k_hbm.at[0, :, keys], v_hbm.at[0, :, keys]]
        targets = outs[2:]
    elif last == 1:
        ids_ref, ks_hbm, vs_hbm = refs[4:7]
        prompt = ids_ref[0]
        sources = [ks_hbm.at[:, prompt], vs_hbm.at[:, prompt]]
        targets = [ref.at[0] for ref in outs[2:]]
    if last < 2:
        rest.append(
            [pltpu.make_async_copy(sources[h], targets[h], sem.at[0, h]) for h in range(2)]
        )
    for pair in rest:
        for copy in pair:
            copy.start()

    for n in range(local):
        for g in range(group):
            at = (n * group + g) * 128
            rows_ref[n, g * units : (g + 1) * units] = q_ref[:, at : at + 128]
        if first:
            head = slice(n * 128, (n + 1) * 128)
            bias = jnp.concatenate([bias_ref[...]] * group)
            s = dot_nt(rows_ref[n], kf_ref[:, head]) + bias
            top = jnp.max(s, axis=1, keepdims=True)
            p = jnp.exp2(s - top).astype(bf16)
            v = jnp.concatenate([vf_ref[:, head], jnp.ones((units, 128), bf16)], axis=1)
            acc[n] = jnp.dot(p, v, preferred_element_type=f32)
            peak[n] = jnp.broadcast_to(top, (rows, 128))

    ones = jnp.ones((block, 128), bf16)
    cut = rows // 4
    spots = [(n, slice(r * cut, (r + 1) * cut)) for n in range(local) for r in range(4)]
    for i in range(steps):
        k_ref, v_ref = (k_first, v_first) if i == 0 else (k_held.at[i - 1], v_held.at[i - 1])
        if i > 0:
            for copy in rest[i - 1]:
                copy.wait()
        over = None
        for n, at in spots:
            s = dot_nt(rows_ref[n, at], k_ref[n])
            level = peak[n, at]
            lifted = [s[:, c : c + 128] - level for c in range(0, block, 128)]
            most = functools.reduce(jnp.maximum, lifted)
            over = most if over is None else jnp.maximum(over, most)
            p = jnp.concatenate([jnp.exp2(x).astype(bf16) for x in lifted], axis=1)
            values = jnp.concatenate([v_ref[n], ones], axis=1)
            fresh_sum[n, at] = jnp.dot(p, values, preferred_element_type=f32)
        worst = jnp.max(over)

        @pl.when(worst < lift_limit)
        def _():
            acc[...] += fresh_sum[...]

        @pl.when(worst >= lift_limit)
        def _(k_ref=k_ref, v_ref=v_ref):
            for n, at in spots:
                s = dot_nt(rows_ref[n, at], k_ref[n])
                before = peak[n, at]
                now = jnp.maximum(before, jnp.max(s, axis=1, keepdims=True))
                peak[n, at] = now
                p = jnp.exp2(s - jnp.concatenate([now] * (block // 128), axis=1)).astype(bf16)
                fade = jnp.exp2(before - now)
                values = jnp.concatenate([v_ref[n], ones], axis=1)
                acc[n, at] = acc[n, at] * jnp.concatenate([fade, fade], axis=1) + jnp.dot(
                    p, values, preferred_element_type=f32
                )

    if last < 2:
        for copy in rest[-1]:
            copy.wait()


def prompt_piece(queries, fresh, state, block, keys, values, piece, ids, suffix):
    units = queries.shape[0]
    local = keys.shape[1]
    rows = group * units
    first = state is None
    last = max(piece + 3 - pieces, 0)
    steps = keys.shape[2] // pieces // key_block
    length = steps * key_block
    acc_shape, peak_shape = (local, rows, 256), (local, rows, 128)
    given = [queries, *(fresh if first else state), *block]
    hbm = [keys, values]
    following = block[0].shape
    if last == 1:
        slots, _, _, span, _ = suffix[0].shape
        following = (1, slots, local, span, 128)
    anywhere = pl.BlockSpec(memory_space=pl.ANY)
    outs = pl.pallas_call(
        functools.partial(prompt_kernel, local, first, piece, last),
        in_specs=[whole(None)] * len(given)
        + [anywhere] * 2
        + ([pl.BlockSpec(memory_space=pltpu.SMEM), anywhere, anywhere] if last == 1 else []),
        out_specs=[whole(None)] * (4 if last < 2 else 2),
        out_shape=(
            jax.ShapeDtypeStruct(acc_shape, f32),
            jax.ShapeDtypeStruct(peak_shape, f32),
            *([jax.ShapeDtypeStruct(following, bf16)] * (2 if last < 2 else 0)),
        ),
        input_output_aliases={} if first else {1: 0, 2: 1},
        scratch_shapes=[
            pltpu.VMEM((local, rows, 128), bf16),
            pltpu.VMEM(acc_shape, f32),
            pltpu.VMEM((steps - 1, local, key_block, 128), bf16),
            pltpu.VMEM((steps - 1, local, key_block, 128), bf16),
            pltpu.SemaphoreType.DMA((steps, 2)),
        ],
        compiler_params=params(prompt_vmem),
        cost_estimate=pl.CostEstimate(
            flops=local * rows * length * 1536,
            bytes_accessed=local * length * 512,
            transcendentals=local * rows * length,
        ),
        name="prompt_attention",
    )(*given, *hbm, *((ids, *suffix) if last == 1 else ()))
    return outs


def suffix_kernel(local, members, following, split, tiles_ref, lens_ref, ids_ref, *refs):
    parts = 2 if split else 1
    listed = parts * len(members)
    q_refs = refs[:listed]
    code_ref, k_ref, v_ref = refs[listed : listed + 3]
    hbm = refs[listed + 3 : listed + 5]
    fetched = 2
    tail = refs[-listed - fetched - 2 :]
    outs, nexts, (acc, sem) = tail[:listed], tail[listed : listed + fetched], tail[-2:]
    units = parts * q_refs[0].shape[0]
    slots = k_ref.shape[1]
    keys = k_ref.shape[3]
    tile = tile_units
    wide = group * 128
    span = local * group
    fetches = []
    if following:
        for c, j in enumerate(following):
            prompt = ids_ref[j]
            for h in range(2):
                fetches.append(
                    pltpu.make_async_copy(hbm[h].at[:, prompt], nexts[h].at[c], sem.at[c, h])
                )
    else:
        block = nexts[0].shape[1]
        keys_at = pl.ds(hbm[0].shape[2] // pieces * (pieces - 1), block)
        for h in range(2):
            fetches.append(
                pltpu.make_async_copy(hbm[h].at[0, :, keys_at], nexts[h], sem.at[0, h])
            )
    for fetch in fetches:
        fetch.start()

    prompts = [ids_ref[j] for j in members]
    acc[...] = jnp.zeros_like(acc)
    key = lax.broadcasted_iota(jnp.int32, (1, keys), 1)
    ones = jnp.ones((keys, 128), bf16)
    lane = lax.broadcasted_iota(jnp.int32, (slots * tile, 128), 1)
    chains = [(n, w) for n in range(local) for w in range(slots)]

    def body(t, _):
        spot = lax.broadcasted_iota(jnp.int32, (tile, units), 0) + t * tile
        picks, rows = [], {}
        for c, prompt in enumerate(prompts):
            pick = jnp.concatenate(
                [
                    jnp.where(code_ref[prompt, w : w + 1, :] == spot, 1.0, 0.0)
                    for w in range(slots)
                ]
            ).astype(bf16)
            picks.append(pick)
            q = jnp.concatenate([ref[...] for ref in q_refs[c * parts : (c + 1) * parts]])
            chosen = jnp.dot(pick, q, preferred_element_type=f32).astype(bf16)
            for n, w in chains:
                rows[c, n, w] = jnp.concatenate(
                    [
                        chosen[w * tile : (w + 1) * tile, at : at + 128]
                        for at in range(n * wide, (n + 1) * wide, 128)
                    ],
                    axis=0,
                )

        def score(c, n, w):
            limit = jnp.where(key < lens_ref[w, prompts[c]], 0.0, masked_score)
            return dot_nt(rows[c, n, w], k_ref[c, w, n]) + limit

        def weigh(c, n, w, p):
            values = jnp.concatenate([v_ref[c, w, n], ones], axis=1)
            return jnp.dot(p.astype(bf16), values, preferred_element_type=f32)

        def by_lane(found, c):
            out = jnp.zeros((slots * tile, 128), f32)
            for n in range(local):
                for g in range(group):
                    at = slice(g * tile, (g + 1) * tile)
                    part = jnp.concatenate([found[c, n, w][at] for w in range(slots)])
                    out = jnp.where(lane % span == n * group + g, part, out)
            high = out.astype(bf16).astype(f32)
            rest = out - high
            mid = rest.astype(bf16).astype(f32)
            low = rest - mid
            third = lane // span % 3
            return jnp.where(third == 0, high, jnp.where(third == 1, mid, low))

        def add(sums, tops):
            for c in range(len(members)):
                packed = by_lane({k: x[:, 128:] for k, x in sums.items()}, c)
                packed = jnp.where(lane // span < 6, packed, 0.0)
                levels = 0.0 if tops is None else by_lane(tops, c)
                packed = jnp.where(lane // span < 3, levels, packed).astype(bf16)
                result = [
                    jnp.concatenate(
                        [
                            sums[c, n, w][g * tile : (g + 1) * tile, :128].astype(bf16)
                            for w in range(slots)
                        ]
                    )
                    for n in range(local)
                    for g in range(group)
                ]
                acc[c] += lax.dot_general(
                    picks[c],
                    jnp.concatenate([*result, packed], axis=1),
                    (((0,), (0,)), ((), ())),
                    preferred_element_type=f32,
                )

        sums, over, under = {}, None, None
        for c in range(len(members)):
            for n, w in chains:
                s = score(c, n, w)
                most = functools.reduce(
                    jnp.maximum, [s[:, i : i + 128] for i in range(0, keys, 128)]
                )
                over = most if over is None else jnp.maximum(over, most)
                o = weigh(c, n, w, jnp.exp2(s))
                under = o[:, 128:] if under is None else jnp.minimum(under, o[:, 128:])
                sums[c, n, w] = o
        plain = (jnp.max(over) < lift_limit) & (jnp.min(under) > 2.0**-lift_limit)

        @pl.when(plain)
        def _():
            add(sums, None)

        @pl.when(jnp.logical_not(plain))
        def _():
            sums, tops = {}, {}
            for c in range(len(members)):
                for n, w in chains:
                    s = score(c, n, w)
                    top = jnp.max(s, axis=1, keepdims=True)
                    sums[c, n, w] = weigh(c, n, w, jnp.exp2(s - top))
                    tops[c, n, w] = jnp.broadcast_to(top, (s.shape[0], 128))
            add(sums, tops)

        return 0

    count = tiles_ref[prompts[0]]
    for prompt in prompts[1:]:
        count = jnp.maximum(count, tiles_ref[prompt])
    lax.fori_loop(0, count, body, 0)
    size = units // parts
    for c in range(len(members)):
        for h in range(parts):
            outs[c * parts + h][...] = acc[c, h * size : (h + 1) * size].astype(bf16)
    for fetch in fetches:
        fetch.wait()


def suffix_attention(tables, found, members, following, split, block, hbm, after):
    tiles, lens, ids, code = tables
    _, slots, local, span, _ = block[0].shape
    listed = flat([found[j] for j in members])
    parts = 2 if split else 1
    units = parts * listed[0].shape[0]
    width = local * group * 128 + 128
    shapes = [jax.ShapeDtypeStruct((units // parts, width), bf16)] * len(listed)
    if following:
        shapes += [jax.ShapeDtypeStruct((len(following), slots, local, span, 128), bf16)] * 2
    else:
        shapes += [jax.ShapeDtypeStruct((local, key_block, 128), bf16)] * 2
    smem = pl.BlockSpec(memory_space=pltpu.SMEM)
    anywhere = pl.BlockSpec(memory_space=pl.ANY)
    result = pl.pallas_call(
        functools.partial(suffix_kernel, local, members, following, split),
        in_specs=[smem] * 3
        + [whole(None)] * (len(listed) + 3)
        + [anywhere] * (len(hbm) + len(after)),
        out_specs=[whole(None)] * len(shapes),
        out_shape=shapes,
        scratch_shapes=[
            pltpu.VMEM((len(members), units, width), f32),
            pltpu.SemaphoreType.DMA((max(len(following), 1), 2)),
        ],
        compiler_params=params(suffix_vmem),
        cost_estimate=pl.CostEstimate(
            flops=len(members) << 30, bytes_accessed=1 << 20, transcendentals=len(members) << 19
        ),
        name="suffix_attention",
    )(tiles, lens, ids, *listed, code, *block, *hbm, *after)
    sums, block = result[: len(listed)], result[len(listed) :]
    return [tuple(sums)] if split else list(sums), block


def merge_kernel(local, acc_ref, peak_ref, own_ref, front_ref, back_ref, *outs):
    units = outs[0].shape[0]
    span = local * group
    wide = local * group * 128
    part = own_ref[...].astype(f32) + front_ref[...].astype(f32) + back_ref[...].astype(f32)
    stats = part[:, wide:]
    for n in range(local):
        for g in range(group):
            at = slice(g * units, (g + 1) * units)
            lane = n * group + g
            level, total = (
                sum(stats[:, i * span + lane : i * span + lane + 1] for i in range(h, h + 3))
                for h in (0, 3)
            )
            peak = peak_ref[n, at]
            top = jnp.maximum(peak, level)
            one = jnp.exp2(peak - top)
            two = jnp.exp2(level - top)
            mixed = acc_ref[n, at, :128] * one + part[:, lane * 128 : (lane + 1) * 128] * two
            outs[n][:, g * 128 : (g + 1) * 128] = (
                mixed / (acc_ref[n, at, 128:] * one + total * two)
            ).astype(bf16)


def merge(state, sums, local):
    units = sums[0].shape[0]
    given = [*state, *sums]
    return pl.pallas_call(
        functools.partial(merge_kernel, local),
        in_specs=[whole(None)] * len(given),
        out_specs=[whole(None)] * local,
        out_shape=[jax.ShapeDtypeStruct((units, group * 128), bf16)] * local,
        compiler_params=params(8),
        name="merge",
    )(*given)


def output_kernel(local, members, middle, halves, info_ref, w_ref, *refs):
    early = len(halves) == 2
    if early:
        *refs, w_held, sem = refs
        size = w_held.shape[0] // sem.shape[0]
        fetches = [
            pltpu.make_async_copy(
                w_ref.at[i * size : (i + 1) * size], w_held.at[i * size : (i + 1) * size], sem.at[i]
            )
            for i in range(sem.shape[0])
        ]
        for fetch in fetches:
            fetch.start()
        w_ref = w_held
    outs = refs[-2 * len(halves) :]
    contexts = refs[: local * (len(members) + (middle in members))]
    per_head = len(contexts) // local
    units = sum(contexts[i].shape[0] for i in range(per_head)) // len(members)
    x = jnp.concatenate(
        [
            jnp.concatenate([ref[...] for ref in contexts[n * per_head : (n + 1) * per_head]])
            for n in range(local)
        ],
        axis=1,
    )
    width = outs[0].shape[1]
    depth = x.shape[1] // 2
    if early:
        for fetch in fetches[: len(fetches) // 2]:
            fetch.wait()
        started = [
            jnp.dot(
                x[:, :depth],
                w_ref[:depth, column * width : (column + 1) * width],
                preferred_element_type=f32,
            )
            for column in halves
        ]
        for fetch in fetches[len(fetches) // 2 :]:
            fetch.wait()
    for h, column in enumerate(halves):
        w = w_ref[:, column * width : (column + 1) * width]
        if early:
            y = jnp.dot(x[:, depth:], w[depth:], preferred_element_type=f32) + started[h]
        else:
            y = jnp.dot(x, w, preferred_element_type=f32)
        y = y.astype(bf16)
        for at, j in enumerate(members):
            rows = pl.ds(pl.multiple_of(info_ref[1, j] * units, units), units)
            for away in range(2):

                @pl.when(info_ref[0, j] == away)
                def _(at=at, away=away, rows=rows, h=h, y=y):
                    outs[2 * h + away][rows] = y[at * units : (at + 1) * units]


def output(info, contexts, members, halves, w, blocks, held):
    local = len(contexts)
    count = len(contexts[0])
    units = contexts[0][0].shape[0]
    listed = [block for found in contexts for block in flat([found[j] for j in members])]
    held = [] if held is None else list(held)
    outs = 2 * len(halves)
    given = 2 + len(listed)
    early = len(halves) == 2
    shapes = [jax.ShapeDtypeStruct((blocks * units, w.shape[1] // 2), bf16)] * outs
    return pl.pallas_call(
        functools.partial(output_kernel, local, members, count // 2, halves),
        in_specs=[pl.BlockSpec(memory_space=pltpu.SMEM)]
        + [pl.BlockSpec(memory_space=pl.ANY) if early else whole(None)]
        + [whole(None)] * (len(listed) + len(held)),
        out_specs=[whole(None)] * (outs + early),
        out_shape=shapes + ([jax.ShapeDtypeStruct(w.shape, w.dtype)] if early else []),
        scratch_shapes=[pltpu.SemaphoreType.DMA((16,))] if early else [],
        input_output_aliases={given + i: i for i in range(len(held))},
        compiler_params=params(output_vmem if early else 16),
        cost_estimate=pl.CostEstimate(
            flops=len(members) * units * w.shape[0] * w.shape[1] * len(halves),
            bytes_accessed=2 << 20,
            transcendentals=0,
        ),
        name="output_projection",
    )(info, w, *listed, *held)


def finish_kernel(steps, local, count, *refs):
    terms, o_ref = refs[:-1], refs[-1]
    rows, width_out = o_ref.shape
    per = rows // (steps * local * count)
    width = local * count
    total = jnp.concatenate(
        [
            sum(term[:rows].astype(f32) for term in terms[h * len(terms) // 2 : (h + 1) * len(terms) // 2])
            for h in range(2)
        ],
        axis=1,
    )
    i = lax.broadcasted_iota(jnp.int32, (rows, rows), 1)
    t = lax.broadcasted_iota(jnp.int32, (rows, rows), 0)
    slot = i // (steps * width)
    part = (i // (steps // 2 * width)) % 2
    source = (i // (steps // 2 * local)) % count
    step = part * (steps // 2) + (i // local) % (steps // 2)
    target = (step * width + source * local + i % local) * per + slot
    perm = jnp.where(t == target, 1.0, 0.0).astype(bf16)
    o_ref[...] = jnp.dot(perm, total.astype(bf16), preferred_element_type=f32).astype(bf16)


def finish(terms, rows, steps, local, count):
    return pl.pallas_call(
        functools.partial(finish_kernel, steps, local, count),
        in_specs=[whole(None)] * len(terms),
        out_specs=whole(None),
        out_shape=jax.ShapeDtypeStruct((rows, 2 * terms[0].shape[1]), bf16),
        compiler_params=params(8),
        name="finish",
    )(*terms)


def shards(
    hidden,
    w_qkv,
    qkv_bias,
    prompt_keys,
    prompt_values,
    suffix_keys,
    suffix_values,
    w_out,
    parents,
    lengths,
):
    count = lax.axis_size("beam")
    heads = lax.axis_size("head")
    beam = lax.axis_index("beam").astype(jnp.int32)
    head = lax.axis_index("head").astype(jnp.int32)
    steps, local_slots, prompts, _ = hidden.shape
    local = prompt_keys.shape[1]
    prompt_len = prompt_keys.shape[2]
    width = local_slots * count
    units = steps * width
    place = ring_place(beam, count)
    core = head % 2
    partner = [(j, j ^ 1) for j in range(heads)]

    rows = hidden.reshape(steps * local_slots * prompts, hidden.shape[3])
    mine = lax.all_to_all(
        split_hidden(rows, core.reshape(1), count), "beam", split_axis=0, concat_axis=0, tiled=True
    )
    other = lax.ppermute(mine, "head", partner)

    roots, starts, chain = lineage_tables(parents, lengths)
    half = steps // 2

    def by_unit(table):
        table = table.reshape(2, half, count, local_slots, prompts)
        return jnp.transpose(table, (4, 0, 2, 1, 3)).reshape(prompts, units)

    unit_roots = by_unit(roots)
    unit_steps = jnp.arange(steps, dtype=jnp.int32).reshape(2, 1, half, 1)
    unit_steps = jnp.broadcast_to(unit_steps, (2, count, half, local_slots)).reshape(units)
    positions = prompt_len + lax.dynamic_index_in_dim(by_unit(starts), beam, 0, False) + unit_steps
    frequency = rope_base ** (-(jnp.arange(64, dtype=f32) * 2.0 / 128))
    angles = positions.astype(f32)[:, None] * frequency
    cosine, sine = jnp.cos(angles), jnp.sin(angles)
    cosine = jnp.concatenate([cosine, cosine], axis=1)
    sine = jnp.concatenate([-sine, sine], axis=1)
    slot_ids = beam * local_slots + jnp.arange(local_slots, dtype=jnp.int32)
    owned = unit_roots[:, None, :] == slot_ids[:, None]
    upto = jnp.arange(units)[:, None] <= jnp.arange(units)[None, :]
    ranks = jnp.einsum(
        "pwu,uv->pwv", owned.astype(f32), upto.astype(f32), preferred_element_type=f32
    ).astype(jnp.int32)
    code = jnp.where(owned, ranks - 1, -1)
    tiles = (jnp.max(ranks[:, :, -1], axis=1) + tile_units - 1) // tile_units
    lens = lax.dynamic_slice_in_dim(lengths, beam * local_slots, local_slots, 0)
    places = (place + jnp.arange(count, dtype=jnp.int32)) % count
    ids = ring_member(places, count)
    own_chain = lax.dynamic_index_in_dim(chain, beam, 3, False)
    linked = own_chain[..., None] == jnp.arange(width, dtype=jnp.int32)
    linked = linked.reshape(2, half, 2, half, count, local_slots, count, local_slots)
    linked = jnp.transpose(linked, (0, 4, 1, 5, 2, 6, 3, 7)).reshape(units, units)
    fresh_bias = jnp.where(linked, 0.0, masked_score).astype(f32)

    info = jnp.concatenate([core.reshape(1), ids])
    sums = []
    for n in range(local):
        blocks = project(info, mine, other, w_qkv, n, local, prompts)
        front, back, mark = scatter_ring(blocks, count)
        sums.append((blocks[0], front, back))
    block = fetch_first(prompt_keys, prompt_values, mark)
    queries, fresh_keys, fresh_values = rotate(
        sums, qkv_bias.reshape(1, -1), cosine, sine, (block[0], fresh_bias, code)
    )

    def attend(state, block, piece):
        outs = prompt_piece(
            queries,
            (fresh_keys, fresh_values, fresh_bias),
            state,
            block,
            prompt_keys,
            prompt_values,
            piece,
            ids,
            (suffix_keys, suffix_values),
        )
        return outs[:2], outs[2:]

    state = None
    for piece in range(pieces - 1):
        state, block = attend(state, block, piece)
    gathered = gather_ring(queries, count, state[1])

    middle = count // 2
    held = [block]

    def members(step):
        return (step,) if step in (0, middle) else (step, count - step)

    def produce(step, after):
        made, held[0] = suffix_attention(
            (tiles, lens, ids, code),
            gathered,
            members(step),
            members(step - 1) if step > 1 else members(middle) if step == 0 else (),
            step == middle,
            held[0],
            (prompt_keys, prompt_values) if step == 1 else (suffix_keys, suffix_values),
            after,
        )
        return made

    (own,) = produce(0, ())
    front, back = return_ring(produce, (), count)
    state, _ = attend(state, held[0], pieces - 1)
    sums = (own, front, back)
    contexts = merge(state, sums, local)

    per = prompts // heads
    chips = heads // 2
    targets = ids // per
    away = (targets % 2) ^ core
    turn = (targets // 2 - head // 2) % chips
    info = jnp.stack([away, turn * per + ids % per]).astype(jnp.int32)
    late = (middle - 1, middle, middle + 1)
    early = tuple(j for j in range(count) if j not in late)
    contexts = [gather_ring(context, count) for context in contexts]
    *held, w_held = output(info, contexts, early, (0, 1), w_out, chips * per, None)
    rows = per * units
    terms = []
    for h in range(2):
        keep, send = output(
            info, contexts, late, (h,), w_held, chips * per, held[2 * h : 2 * h + 2]
        )
        came = lax.ppermute(send, "head", partner)
        terms += [keep, came]
        for i in range(1, chips):
            at = slice(i * rows, (i + 1) * rows)
            far = (keep[at].astype(f32) + came[at].astype(f32)).astype(bf16)
            pairs = [(j, (j + 2 * i) % heads) for j in range(heads)]
            terms.append(lax.ppermute(far, "head", pairs))
    result = finish(terms, rows, steps, local_slots, count)
    return result.reshape(steps, width, per, result.shape[1])


def solution(mesh):
    return jax.shard_map(
        shards,
        mesh=mesh,
        in_specs=(
            P(None, "beam", None, None),
            P("beam", "head"),
            P("head"),
            P("beam", "head", None, None),
            P("beam", "head", None, None),
            P("beam", None, "head", None, None),
            P("beam", None, "head", None, None),
            P("head", "beam"),
            P(),
            P(),
        ),
        out_specs=P(None, None, "head", "beam"),
        check_vma=False,
    )
```

```python
import functools

import jax
import jax.numpy as jnp
from jax import lax
from jax.experimental import pallas as pl
from jax.experimental.pallas import tpu as pltpu
from jax.sharding import PartitionSpec as P

rope_base = 1000000.0
masked_score = -1e30
log2e = 1.4426950408889634
group = 8
bf16 = jnp.bfloat16
f32 = jnp.float32
key_block = 2048
pieces = 4
tile_units = 32
lift_limit = 64.0
prompt_vmem = 46
output_vmem = 45
suffix_vmem = 48


def params(vmem_mib=24):
    return pltpu.CompilerParams(vmem_limit_bytes=vmem_mib << 20)


def whole(_):
    return pl.BlockSpec(memory_space=pltpu.VMEM)


def ring_order(count):
    return list(range(0, count, 2)) + list(range(count - 1, 0, -2))


def ring_pairs(count):
    order = ring_order(count)
    forward = [(order[i], order[(i + 1) % count]) for i in range(count)]
    return forward, [(b, a) for a, b in forward]


def ring_place(index, count):
    return jnp.where(index % 2 == 0, index // 2, count - 1 - index // 2)


def ring_member(place, count):
    return jnp.where(place < count // 2, 2 * place, 2 * (count - 1 - place) + 1)


def relay_kernel(ahead_ref, behind_ref, _, front_ref, back_ref):
    half = front_ref.shape[0]
    front_ref[...] = ahead_ref[:half]
    back_ref[...] = behind_ref[half:]


def relay(ahead, behind, after):
    rows, columns = ahead.shape
    return pl.pallas_call(
        relay_kernel,
        in_specs=[whole(None)] * 2 + [pl.BlockSpec(memory_space=pl.ANY)],
        out_specs=[whole(None)] * 2,
        out_shape=[jax.ShapeDtypeStruct((rows // 2, columns), bf16)] * 2,
        compiler_params=params(8),
        name="relay",
    )(ahead, behind, after)


def gather_ring(block, count, after=None):
    forward, backward = ring_pairs(count)
    middle = count // 2
    half = block.shape[0] // 2
    found = [None] * count
    found[0] = block
    ahead = behind = block
    for step in range(1, middle):
        ahead = lax.ppermute(ahead, "beam", forward)
        behind = lax.ppermute(behind, "beam", backward)
        found[count - step] = ahead
        found[step] = behind
    if after is None:
        ahead, behind = ahead[:half], behind[half:]
    else:
        ahead, behind = relay(ahead, behind, after)
    found[middle] = (
        lax.ppermute(ahead, "beam", forward),
        lax.ppermute(behind, "beam", backward),
    )
    return found


def scatter_ring(blocks, count):
    forward, backward = ring_pairs(count)
    middle = count // 2
    ahead, behind = blocks[middle]
    half = ahead.shape[0]
    for step in range(middle - 1, -1, -1):
        ahead = lax.ppermute(ahead, "beam", forward)
        behind = lax.ppermute(behind, "beam", backward)
        if step == 0:
            break
        front = blocks[step].astype(f32)
        back = blocks[count - step].astype(f32)
        ahead = ahead.astype(f32)
        behind = behind.astype(f32)
        if step == middle - 1:
            ahead = jnp.concatenate([ahead + front[:half], front[half:]])
            behind = jnp.concatenate([back[:half], behind + back[half:]])
        else:
            ahead = ahead + front
            behind = behind + back
        ahead = ahead.astype(bf16)
        behind = behind.astype(bf16)
        mark = ahead if step == middle - 1 else mark
    return ahead, behind, mark


def return_ring(produce, after, count):
    forward, backward = ring_pairs(count)
    middle = count // 2
    ((ahead, behind),) = produce(middle, after)
    half = ahead.shape[0]
    for step in range(middle - 1, -1, -1):
        marker = (ahead, behind)
        ahead = lax.ppermute(ahead, "beam", forward)
        behind = lax.ppermute(behind, "beam", backward)
        if step == 0:
            return ahead, behind
        made = produce(step, marker)
        front, back = (block.astype(f32) for block in made)
        one, two = ahead.astype(f32), behind.astype(f32)
        if step == middle - 1:
            one = jnp.concatenate([one + front[:half], front[half:]])
            two = jnp.concatenate([back[:half], two + back[half:]])
        else:
            one, two = one + front, two + back
        ahead, behind = one.astype(bf16), two.astype(bf16)


def flat(found):
    listed = []
    for block in found:
        listed.extend(block if isinstance(block, tuple) else (block,))
    return listed


def lineage_kernel(parents_ref, lengths_ref, roots_ref, starts_ref, chain_ref):
    steps, width, prompts = parents_ref.shape

    def take(table, chosen):
        out = jnp.zeros_like(chosen)
        for j in range(width):
            out = jnp.where(chosen == j, table[j : j + 1, :], out)
        return out

    own = lax.broadcasted_iota(jnp.int32, (width, prompts), 0)
    lengths = lengths_ref[...]
    for s in range(steps):
        current = own
        for t in range(steps - 1, s, -1):
            chain_ref[s, t] = own - width
        chain_ref[s, s] = own
        for t in range(s, 0, -1):
            current = take(parents_ref[t], current)
            chain_ref[s, t - 1] = current
        root = take(parents_ref[0], current)
        roots_ref[s] = root
        starts_ref[s] = take(lengths, root)


def lineage_tables(parents, lengths):
    steps, width, prompts = parents.shape
    return pl.pallas_call(
        lineage_kernel,
        in_specs=[whole(None)] * 2,
        out_specs=[whole(None)] * 3,
        out_shape=(
            jax.ShapeDtypeStruct((steps, width, prompts), jnp.int32),
            jax.ShapeDtypeStruct((steps, width, prompts), jnp.int32),
            jax.ShapeDtypeStruct((steps, steps, width, prompts), jnp.int32),
        ),
        compiler_params=params(8),
        name="lineage",
    )(parents, lengths)


def split_kernel(core_ref, x_ref, o_ref, sem):
    count, half, part = o_ref.shape
    rows = pl.ds(pl.multiple_of(core_ref[0] * half, half), half)
    copies = [
        pltpu.make_async_copy(x_ref.at[rows, b * part : (b + 1) * part], o_ref.at[b], sem.at[b])
        for b in range(count)
    ]
    for copy in copies:
        copy.start()
    for copy in copies:
        copy.wait()


def split_hidden(hidden, core, count):
    rows, width = hidden.shape
    half, part = rows // 2, width // count
    return pl.pallas_call(
        split_kernel,
        in_specs=[pl.BlockSpec(memory_space=pltpu.SMEM), pl.BlockSpec(memory_space=pltpu.HBM)],
        out_specs=whole(None),
        out_shape=jax.ShapeDtypeStruct((count, half, part), bf16),
        scratch_shapes=[pltpu.SemaphoreType.DMA((count,))],
        compiler_params=params(62),
        name="split_hidden",
    )(core, hidden)


def project_kernel(count, prompts, head, info_ref, mine_ref, other_ref, w_ref, *refs):
    outs, y_ref = refs[:-1], refs[-1]
    half, part = mine_ref.shape[1:]
    units = 2 * half * count // prompts
    rows = half * count
    core = info_ref[0]
    columns = y_ref.shape[0] * 128
    w = w_ref[:, head * columns : (head + 1) * columns]
    lower = pl.ds(pl.multiple_of(core * rows, rows), rows)
    upper = pl.ds(pl.multiple_of((1 - core) * rows, rows), rows)
    for at, ref in ((lower, mine_ref), (upper, other_ref)):
        y = jnp.dot(ref[...].reshape(rows, part), w, preferred_element_type=f32)
        for c in range(y_ref.shape[0]):
            y_ref[c, at] = y[:, c * 128 : (c + 1) * 128]
    at = 0
    for j in range(count):
        block = jnp.concatenate(
            [
                y_ref[c, pl.ds(info_ref[1 + j], units, stride=prompts)]
                for c in range(y_ref.shape[0])
            ],
            axis=1,
        )
        if j == count // 2:
            outs[at][...] = block[: units // 2].astype(bf16)
            outs[at + 1][...] = block[units // 2 :].astype(bf16)
            at += 2
        else:
            outs[at][...] = block
            at += 1


def project(info, mine, other, w, head, local, prompts):
    count, half, part = mine.shape
    columns = w.shape[1] // local
    units = 2 * half * count // prompts
    middle = count // 2
    shapes = []
    for j in range(count):
        if j == middle:
            shapes += [jax.ShapeDtypeStruct((units // 2, columns), bf16)] * 2
        else:
            shapes.append(jax.ShapeDtypeStruct((units, columns), f32))
    outs = pl.pallas_call(
        functools.partial(project_kernel, count, prompts, head),
        in_specs=[pl.BlockSpec(memory_space=pltpu.SMEM)]
        + [whole(None)] * 3,
        out_specs=[whole(None)] * len(shapes),
        scratch_shapes=[pltpu.VMEM((columns // 128, 2 * half * count, 128), f32)],
        out_shape=shapes,
        compiler_params=params(44),
        cost_estimate=pl.CostEstimate(
            flops=2 * units * count * part * columns, bytes_accessed=6 << 20, transcendentals=0
        ),
        name="project",
    )(info, mine, other, w)
    return list(outs[:middle]) + [(outs[middle], outs[middle + 1])] + list(outs[middle + 2 :])


def fetch_kernel(k_hbm, v_hbm, _, k_next, v_next, sem):
    size = k_next.shape[1] // 4
    fetches = [
        pltpu.make_async_copy(
            source.at[0, n, i * size : (i + 1) * size],
            target.at[n, i * size : (i + 1) * size],
            sem.at[h, n, i],
        )
        for n in range(k_next.shape[0])
        for i in range(4)
        for h, (source, target) in enumerate(((k_hbm, k_next), (v_hbm, v_next)))
    ]
    for fetch in fetches:
        fetch.start()
    for fetch in fetches:
        fetch.wait()


def fetch_first(keys, values, after):
    local = keys.shape[1]
    return pl.pallas_call(
        fetch_kernel,
        in_specs=[pl.BlockSpec(memory_space=pl.ANY)] * 3,
        out_specs=[whole(None)] * 2,
        out_shape=[jax.ShapeDtypeStruct((local, key_block, 128), bf16)] * 2,
        scratch_shapes=[pltpu.SemaphoreType.DMA((2, local, 4))],
        compiler_params=params(48),
        cost_estimate=pl.CostEstimate(flops=0, bytes_accessed=8 << 20, transcendentals=0),
        name="fetch_first",
    )(keys, values, after)


def rotate_kernel(local, *refs):
    sums, (bias_ref, cos_ref, sin_ref) = refs[: 3 * local], refs[3 * local : 3 * local + 3]
    q_ref, k_ref, v_ref = refs[-3:]
    cosine, sine = cos_ref[...], sin_ref[...]
    scale = log2e * 128**-0.5
    for n in range(local):
        own_ref, front_ref, back_ref = sums[3 * n : 3 * n + 3]
        columns = own_ref.shape[1]
        x = own_ref[...] + front_ref[...].astype(f32) + back_ref[...].astype(f32)
        x = x + bias_ref[:, n * columns : (n + 1) * columns]
        for g in range(group + 1):
            part = x[:, g * 128 : (g + 1) * 128]
            turned = part * cosine + pltpu.roll(part, 64, 1) * sine
            if g < group:
                at = (n * group + g) * 128
                q_ref[:, at : at + 128] = (turned * scale).astype(bf16)
            else:
                k_ref[:, n * 128 : (n + 1) * 128] = turned.astype(bf16)
        v_ref[:, n * 128 : (n + 1) * 128] = x[:, (group + 1) * 128 :].astype(bf16)


def rotate(sums, bias, cosine, sine, after):
    local = len(sums)
    units = cosine.shape[0]
    given = [part for three in sums for part in three] + [bias, cosine, sine]
    return pl.pallas_call(
        functools.partial(rotate_kernel, local),
        in_specs=[whole(None)] * len(given) + [pl.BlockSpec(memory_space=pl.ANY)] * len(after),
        out_specs=[whole(None)] * 3,
        out_shape=(
            jax.ShapeDtypeStruct((units, local * group * 128), bf16),
            jax.ShapeDtypeStruct((units, local * 128), bf16),
            jax.ShapeDtypeStruct((units, local * 128), bf16),
        ),
        compiler_params=params(),
        name="rotate",
    )(*given, *after)


def dot_nt(a, b):
    return lax.dot_general(a, b, (((1,), (1,)), ((), ())), preferred_element_type=f32)


def prompt_kernel(local, first, piece, last, q_ref, *refs):
    if first:
        kf_ref, vf_ref, bias_ref = refs[:3]
        refs = refs[3:]
    else:
        refs = refs[2:]
    k_first, v_first, k_hbm, v_hbm = refs[:4]
    rows_ref, fresh_sum, k_held, v_held, sem = refs[-5:]
    outs = refs[-9:-5] if last < 2 else refs[-7:-5]
    acc, peak = outs[:2]
    units = q_ref.shape[0]
    rows = group * units
    block = k_first.shape[1]
    steps = k_held.shape[0] + 1
    rest = []
    for i in range(1, steps):
        keys = pl.ds((piece * steps + i) * block, block)
        rest.append(
            (
                pltpu.make_async_copy(k_hbm.at[0, :, keys], k_held.at[i - 1], sem.at[i, 0]),
                pltpu.make_async_copy(v_hbm.at[0, :, keys], v_held.at[i - 1], sem.at[i, 1]),
            )
        )
    if last == 0:
        keys = pl.ds((piece + 1) * steps * block, block)
        sources = [k_hbm.at[0, :, keys], v_hbm.at[0, :, keys]]
        targets = outs[2:]
    elif last == 1:
        ids_ref, ks_hbm, vs_hbm = refs[4:7]
        prompt = ids_ref[0]
        sources = [ks_hbm.at[:, prompt], vs_hbm.at[:, prompt]]
        targets = [ref.at[0] for ref in outs[2:]]
    if last < 2:
        rest.append(
            [pltpu.make_async_copy(sources[h], targets[h], sem.at[0, h]) for h in range(2)]
        )
    for pair in rest:
        for copy in pair:
            copy.start()

    for n in range(local):
        for g in range(group):
            at = (n * group + g) * 128
            rows_ref[n, g * units : (g + 1) * units] = q_ref[:, at : at + 128]
        if first:
            head = slice(n * 128, (n + 1) * 128)
            bias = jnp.concatenate([bias_ref[...]] * group)
            s = dot_nt(rows_ref[n], kf_ref[:, head]) + bias
            top = jnp.max(s, axis=1, keepdims=True)
            p = jnp.exp2(s - top).astype(bf16)
            v = jnp.concatenate([vf_ref[:, head], jnp.ones((units, 128), bf16)], axis=1)
            acc[n] = jnp.dot(p, v, preferred_element_type=f32)
            peak[n] = jnp.broadcast_to(top, (rows, 128))

    ones = jnp.ones((block, 128), bf16)
    cut = rows // 4
    spots = [(n, slice(r * cut, (r + 1) * cut)) for n in range(local) for r in range(4)]
    for i in range(steps):
        k_ref, v_ref = (k_first, v_first) if i == 0 else (k_held.at[i - 1], v_held.at[i - 1])
        if i > 0:
            for copy in rest[i - 1]:
                copy.wait()
        over = None
        for n, at in spots:
            s = dot_nt(rows_ref[n, at], k_ref[n])
            level = peak[n, at]
            lifted = [s[:, c : c + 128] - level for c in range(0, block, 128)]
            most = functools.reduce(jnp.maximum, lifted)
            over = most if over is None else jnp.maximum(over, most)
            p = jnp.concatenate([jnp.exp2(x).astype(bf16) for x in lifted], axis=1)
            values = jnp.concatenate([v_ref[n], ones], axis=1)
            fresh_sum[n, at] = jnp.dot(p, values, preferred_element_type=f32)
        worst = jnp.max(over)

        @pl.when(worst < lift_limit)
        def _():
            acc[...] += fresh_sum[...]

        @pl.when(worst >= lift_limit)
        def _(k_ref=k_ref, v_ref=v_ref):
            for n, at in spots:
                s = dot_nt(rows_ref[n, at], k_ref[n])
                before = peak[n, at]
                now = jnp.maximum(before, jnp.max(s, axis=1, keepdims=True))
                peak[n, at] = now
                p = jnp.exp2(s - jnp.concatenate([now] * (block // 128), axis=1)).astype(bf16)
                fade = jnp.exp2(before - now)
                values = jnp.concatenate([v_ref[n], ones], axis=1)
                acc[n, at] = acc[n, at] * jnp.concatenate([fade, fade], axis=1) + jnp.dot(
                    p, values, preferred_element_type=f32
                )

    if last < 2:
        for copy in rest[-1]:
            copy.wait()


def prompt_piece(queries, fresh, state, block, keys, values, piece, ids, suffix):
    units = queries.shape[0]
    local = keys.shape[1]
    rows = group * units
    first = state is None
    last = max(piece + 3 - pieces, 0)
    steps = keys.shape[2] // pieces // key_block
    length = steps * key_block
    acc_shape, peak_shape = (local, rows, 256), (local, rows, 128)
    given = [queries, *(fresh if first else state), *block]
    hbm = [keys, values]
    following = block[0].shape
    if last == 1:
        slots, _, _, span, _ = suffix[0].shape
        following = (1, slots, local, span, 128)
    anywhere = pl.BlockSpec(memory_space=pl.ANY)
    outs = pl.pallas_call(
        functools.partial(prompt_kernel, local, first, piece, last),
        in_specs=[whole(None)] * len(given)
        + [anywhere] * 2
        + ([pl.BlockSpec(memory_space=pltpu.SMEM), anywhere, anywhere] if last == 1 else []),
        out_specs=[whole(None)] * (4 if last < 2 else 2),
        out_shape=(
            jax.ShapeDtypeStruct(acc_shape, f32),
            jax.ShapeDtypeStruct(peak_shape, f32),
            *([jax.ShapeDtypeStruct(following, bf16)] * (2 if last < 2 else 0)),
        ),
        input_output_aliases={} if first else {1: 0, 2: 1},
        scratch_shapes=[
            pltpu.VMEM((local, rows, 128), bf16),
            pltpu.VMEM(acc_shape, f32),
            pltpu.VMEM((steps - 1, local, key_block, 128), bf16),
            pltpu.VMEM((steps - 1, local, key_block, 128), bf16),
            pltpu.SemaphoreType.DMA((steps, 2)),
        ],
        compiler_params=params(prompt_vmem),
        cost_estimate=pl.CostEstimate(
            flops=local * rows * length * 1536,
            bytes_accessed=local * length * 512,
            transcendentals=local * rows * length,
        ),
        name="prompt_attention",
    )(*given, *hbm, *((ids, *suffix) if last == 1 else ()))
    return outs


def suffix_kernel(local, members, following, split, tiles_ref, lens_ref, ids_ref, *refs):
    parts = 2 if split else 1
    listed = parts * len(members)
    q_refs = refs[:listed]
    code_ref, k_ref, v_ref = refs[listed : listed + 3]
    hbm = refs[listed + 3 : listed + 5]
    fetched = 2
    tail = refs[-listed - fetched - 2 :]
    outs, nexts, (acc, sem) = tail[:listed], tail[listed : listed + fetched], tail[-2:]
    units = parts * q_refs[0].shape[0]
    slots = k_ref.shape[1]
    keys = k_ref.shape[3]
    tile = tile_units
    wide = group * 128
    span = local * group
    fetches = []
    if following:
        for c, j in enumerate(following):
            prompt = ids_ref[j]
            for h in range(2):
                fetches.append(
                    pltpu.make_async_copy(hbm[h].at[:, prompt], nexts[h].at[c], sem.at[c, h])
                )
    else:
        block = nexts[0].shape[1]
        keys_at = pl.ds(hbm[0].shape[2] // pieces * (pieces - 1), block)
        for h in range(2):
            fetches.append(
                pltpu.make_async_copy(hbm[h].at[0, :, keys_at], nexts[h], sem.at[0, h])
            )
    for fetch in fetches:
        fetch.start()

    prompts = [ids_ref[j] for j in members]
    acc[...] = jnp.zeros_like(acc)
    key = lax.broadcasted_iota(jnp.int32, (1, keys), 1)
    ones = jnp.ones((keys, 128), bf16)
    lane = lax.broadcasted_iota(jnp.int32, (slots * tile, 128), 1)
    chains = [(n, w) for n in range(local) for w in range(slots)]

    def body(t, _):
        spot = lax.broadcasted_iota(jnp.int32, (tile, units), 0) + t * tile
        picks, rows = [], {}
        for c, prompt in enumerate(prompts):
            pick = jnp.concatenate(
                [
                    jnp.where(code_ref[prompt, w : w + 1, :] == spot, 1.0, 0.0)
                    for w in range(slots)
                ]
            ).astype(bf16)
            picks.append(pick)
            q = jnp.concatenate([ref[...] for ref in q_refs[c * parts : (c + 1) * parts]])
            chosen = jnp.dot(pick, q, preferred_element_type=f32).astype(bf16)
            for n, w in chains:
                rows[c, n, w] = jnp.concatenate(
                    [
                        chosen[w * tile : (w + 1) * tile, at : at + 128]
                        for at in range(n * wide, (n + 1) * wide, 128)
                    ],
                    axis=0,
                )

        def score(c, n, w):
            limit = jnp.where(key < lens_ref[w, prompts[c]], 0.0, masked_score)
            return dot_nt(rows[c, n, w], k_ref[c, w, n]) + limit

        def weigh(c, n, w, p):
            values = jnp.concatenate([v_ref[c, w, n], ones], axis=1)
            return jnp.dot(p.astype(bf16), values, preferred_element_type=f32)

        def by_lane(found, c):
            out = jnp.zeros((slots * tile, 128), f32)
            for n in range(local):
                for g in range(group):
                    at = slice(g * tile, (g + 1) * tile)
                    part = jnp.concatenate([found[c, n, w][at] for w in range(slots)])
                    out = jnp.where(lane % span == n * group + g, part, out)
            high = out.astype(bf16).astype(f32)
            rest = out - high
            mid = rest.astype(bf16).astype(f32)
            low = rest - mid
            third = lane // span % 3
            return jnp.where(third == 0, high, jnp.where(third == 1, mid, low))

        def add(sums, tops):
            for c in range(len(members)):
                packed = by_lane({k: x[:, 128:] for k, x in sums.items()}, c)
                packed = jnp.where(lane // span < 6, packed, 0.0)
                levels = 0.0 if tops is None else by_lane(tops, c)
                packed = jnp.where(lane // span < 3, levels, packed).astype(bf16)
                result = [
                    jnp.concatenate(
                        [
                            sums[c, n, w][g * tile : (g + 1) * tile, :128].astype(bf16)
                            for w in range(slots)
                        ]
                    )
                    for n in range(local)
                    for g in range(group)
                ]
                acc[c] += lax.dot_general(
                    picks[c],
                    jnp.concatenate([*result, packed], axis=1),
                    (((0,), (0,)), ((), ())),
                    preferred_element_type=f32,
                )

        sums, over, under = {}, None, None
        for c in range(len(members)):
            for n, w in chains:
                s = score(c, n, w)
                most = functools.reduce(
                    jnp.maximum, [s[:, i : i + 128] for i in range(0, keys, 128)]
                )
                over = most if over is None else jnp.maximum(over, most)
                o = weigh(c, n, w, jnp.exp2(s))
                under = o[:, 128:] if under is None else jnp.minimum(under, o[:, 128:])
                sums[c, n, w] = o
        plain = (jnp.max(over) < lift_limit) & (jnp.min(under) > 2.0**-lift_limit)

        @pl.when(plain)
        def _():
            add(sums, None)

        @pl.when(jnp.logical_not(plain))
        def _():
            sums, tops = {}, {}
            for c in range(len(members)):
                for n, w in chains:
                    s = score(c, n, w)
                    top = jnp.max(s, axis=1, keepdims=True)
                    sums[c, n, w] = weigh(c, n, w, jnp.exp2(s - top))
                    tops[c, n, w] = jnp.broadcast_to(top, (s.shape[0], 128))
            add(sums, tops)

        return 0

    count = tiles_ref[prompts[0]]
    for prompt in prompts[1:]:
        count = jnp.maximum(count, tiles_ref[prompt])
    lax.fori_loop(0, count, body, 0)
    size = units // parts
    for c in range(len(members)):
        for h in range(parts):
            outs[c * parts + h][...] = acc[c, h * size : (h + 1) * size].astype(bf16)
    for fetch in fetches:
        fetch.wait()


def suffix_attention(tables, found, members, following, split, block, hbm, after):
    tiles, lens, ids, code = tables
    _, slots, local, span, _ = block[0].shape
    listed = flat([found[j] for j in members])
    parts = 2 if split else 1
    units = parts * listed[0].shape[0]
    width = local * group * 128 + 128
    shapes = [jax.ShapeDtypeStruct((units // parts, width), bf16)] * len(listed)
    if following:
        shapes += [jax.ShapeDtypeStruct((len(following), slots, local, span, 128), bf16)] * 2
    else:
        shapes += [jax.ShapeDtypeStruct((local, key_block, 128), bf16)] * 2
    smem = pl.BlockSpec(memory_space=pltpu.SMEM)
    anywhere = pl.BlockSpec(memory_space=pl.ANY)
    result = pl.pallas_call(
        functools.partial(suffix_kernel, local, members, following, split),
        in_specs=[smem] * 3
        + [whole(None)] * (len(listed) + 3)
        + [anywhere] * (len(hbm) + len(after)),
        out_specs=[whole(None)] * len(shapes),
        out_shape=shapes,
        scratch_shapes=[
            pltpu.VMEM((len(members), units, width), f32),
            pltpu.SemaphoreType.DMA((max(len(following), 1), 2)),
        ],
        compiler_params=params(suffix_vmem),
        cost_estimate=pl.CostEstimate(
            flops=len(members) << 30, bytes_accessed=1 << 20, transcendentals=len(members) << 19
        ),
        name="suffix_attention",
    )(tiles, lens, ids, *listed, code, *block, *hbm, *after)
    sums, block = result[: len(listed)], result[len(listed) :]
    return [tuple(sums)] if split else list(sums), block


def merge_kernel(local, acc_ref, peak_ref, own_ref, front_ref, back_ref, *outs):
    units = outs[0].shape[0]
    span = local * group
    wide = local * group * 128
    part = own_ref[...].astype(f32) + front_ref[...].astype(f32) + back_ref[...].astype(f32)
    stats = part[:, wide:]
    for n in range(local):
        for g in range(group):
            at = slice(g * units, (g + 1) * units)
            lane = n * group + g
            level, total = (
                sum(stats[:, i * span + lane : i * span + lane + 1] for i in range(h, h + 3))
                for h in (0, 3)
            )
            peak = peak_ref[n, at]
            top = jnp.maximum(peak, level)
            one = jnp.exp2(peak - top)
            two = jnp.exp2(level - top)
            mixed = acc_ref[n, at, :128] * one + part[:, lane * 128 : (lane + 1) * 128] * two
            outs[n][:, g * 128 : (g + 1) * 128] = (
                mixed / (acc_ref[n, at, 128:] * one + total * two)
            ).astype(bf16)


def merge(state, sums, local):
    units = sums[0].shape[0]
    given = [*state, *sums]
    return pl.pallas_call(
        functools.partial(merge_kernel, local),
        in_specs=[whole(None)] * len(given),
        out_specs=[whole(None)] * local,
        out_shape=[jax.ShapeDtypeStruct((units, group * 128), bf16)] * local,
        compiler_params=params(8),
        name="merge",
    )(*given)


def output_kernel(local, members, middle, halves, info_ref, w_ref, *refs):
    early = len(halves) == 2
    if early:
        *refs, w_held, sem = refs
        size = w_held.shape[0] // sem.shape[0]
        fetches = [
            pltpu.make_async_copy(
                w_ref.at[i * size : (i + 1) * size], w_held.at[i * size : (i + 1) * size], sem.at[i]
            )
            for i in range(sem.shape[0])
        ]
        for fetch in fetches:
            fetch.start()
        w_ref = w_held
    outs = refs[-2 * len(halves) :]
    contexts = refs[: local * (len(members) + (middle in members))]
    per_head = len(contexts) // local
    units = sum(contexts[i].shape[0] for i in range(per_head)) // len(members)
    x = jnp.concatenate(
        [
            jnp.concatenate([ref[...] for ref in contexts[n * per_head : (n + 1) * per_head]])
            for n in range(local)
        ],
        axis=1,
    )
    width = outs[0].shape[1]
    depth = x.shape[1] // 2
    if early:
        for fetch in fetches[: len(fetches) // 2]:
            fetch.wait()
        started = [
            jnp.dot(
                x[:, :depth],
                w_ref[:depth, column * width : (column + 1) * width],
                preferred_element_type=f32,
            )
            for column in halves
        ]
        for fetch in fetches[len(fetches) // 2 :]:
            fetch.wait()
    for h, column in enumerate(halves):
        w = w_ref[:, column * width : (column + 1) * width]
        if early:
            y = jnp.dot(x[:, depth:], w[depth:], preferred_element_type=f32) + started[h]
        else:
            y = jnp.dot(x, w, preferred_element_type=f32)
        y = y.astype(bf16)
        for at, j in enumerate(members):
            rows = pl.ds(pl.multiple_of(info_ref[1, j] * units, units), units)
            for away in range(2):

                @pl.when(info_ref[0, j] == away)
                def _(at=at, away=away, rows=rows, h=h, y=y):
                    outs[2 * h + away][rows] = y[at * units : (at + 1) * units]


def output(info, contexts, members, halves, w, blocks, held):
    local = len(contexts)
    count = len(contexts[0])
    units = contexts[0][0].shape[0]
    listed = [block for found in contexts for block in flat([found[j] for j in members])]
    held = [] if held is None else list(held)
    outs = 2 * len(halves)
    given = 2 + len(listed)
    early = len(halves) == 2
    shapes = [jax.ShapeDtypeStruct((blocks * units, w.shape[1] // 2), bf16)] * outs
    return pl.pallas_call(
        functools.partial(output_kernel, local, members, count // 2, halves),
        in_specs=[pl.BlockSpec(memory_space=pltpu.SMEM)]
        + [pl.BlockSpec(memory_space=pl.ANY) if early else whole(None)]
        + [whole(None)] * (len(listed) + len(held)),
        out_specs=[whole(None)] * (outs + early),
        out_shape=shapes + ([jax.ShapeDtypeStruct(w.shape, w.dtype)] if early else []),
        scratch_shapes=[pltpu.SemaphoreType.DMA((16,))] if early else [],
        input_output_aliases={given + i: i for i in range(len(held))},
        compiler_params=params(output_vmem if early else 16),
        cost_estimate=pl.CostEstimate(
            flops=len(members) * units * w.shape[0] * w.shape[1] * len(halves),
            bytes_accessed=2 << 20,
            transcendentals=0,
        ),
        name="output_projection",
    )(info, w, *listed, *held)


def finish_kernel(steps, local, count, *refs):
    terms, o_ref = refs[:-1], refs[-1]
    rows, width_out = o_ref.shape
    per = rows // (steps * local * count)
    width = local * count
    total = jnp.concatenate(
        [
            sum(term[:rows].astype(f32) for term in terms[h * len(terms) // 2 : (h + 1) * len(terms) // 2])
            for h in range(2)
        ],
        axis=1,
    )
    i = lax.broadcasted_iota(jnp.int32, (rows, rows), 1)
    t = lax.broadcasted_iota(jnp.int32, (rows, rows), 0)
    slot = i // (steps * width)
    part = (i // (steps // 2 * width)) % 2
    source = (i // (steps // 2 * local)) % count
    step = part * (steps // 2) + (i // local) % (steps // 2)
    target = (step * width + source * local + i % local) * per + slot
    perm = jnp.where(t == target, 1.0, 0.0).astype(bf16)
    o_ref[...] = jnp.dot(perm, total.astype(bf16), preferred_element_type=f32).astype(bf16)


def finish(terms, rows, steps, local, count):
    return pl.pallas_call(
        functools.partial(finish_kernel, steps, local, count),
        in_specs=[whole(None)] * len(terms),
        out_specs=whole(None),
        out_shape=jax.ShapeDtypeStruct((rows, 2 * terms[0].shape[1]), bf16),
        compiler_params=params(8),
        name="finish",
    )(*terms)


def shards(
    hidden,
    w_qkv,
    qkv_bias,
    prompt_keys,
    prompt_values,
    suffix_keys,
    suffix_values,
    w_out,
    parents,
    lengths,
):
    count = lax.axis_size("beam")
    heads = lax.axis_size("head")
    beam = lax.axis_index("beam").astype(jnp.int32)
    head = lax.axis_index("head").astype(jnp.int32)
    steps, local_slots, prompts, _ = hidden.shape
    local = prompt_keys.shape[1]
    prompt_len = prompt_keys.shape[2]
    width = local_slots * count
    units = steps * width
    place = ring_place(beam, count)
    core = head % 2
    partner = [(j, j ^ 1) for j in range(heads)]

    rows = hidden.reshape(steps * local_slots * prompts, hidden.shape[3])
    mine = lax.all_to_all(
        split_hidden(rows, core.reshape(1), count), "beam", split_axis=0, concat_axis=0, tiled=True
    )
    other = lax.ppermute(mine, "head", partner)

    roots, starts, chain = lineage_tables(parents, lengths)
    half = steps // 2

    def by_unit(table):
        table = table.reshape(2, half, count, local_slots, prompts)
        return jnp.transpose(table, (4, 0, 2, 1, 3)).reshape(prompts, units)

    unit_roots = by_unit(roots)
    unit_steps = jnp.arange(steps, dtype=jnp.int32).reshape(2, 1, half, 1)
    unit_steps = jnp.broadcast_to(unit_steps, (2, count, half, local_slots)).reshape(units)
    positions = prompt_len + lax.dynamic_index_in_dim(by_unit(starts), beam, 0, False) + unit_steps
    frequency = rope_base ** (-(jnp.arange(64, dtype=f32) * 2.0 / 128))
    angles = positions.astype(f32)[:, None] * frequency
    cosine, sine = jnp.cos(angles), jnp.sin(angles)
    cosine = jnp.concatenate([cosine, cosine], axis=1)
    sine = jnp.concatenate([-sine, sine], axis=1)
    slot_ids = beam * local_slots + jnp.arange(local_slots, dtype=jnp.int32)
    owned = unit_roots[:, None, :] == slot_ids[:, None]
    upto = jnp.arange(units)[:, None] <= jnp.arange(units)[None, :]
    ranks = jnp.einsum(
        "pwu,uv->pwv", owned.astype(f32), upto.astype(f32), preferred_element_type=f32
    ).astype(jnp.int32)
    code = jnp.where(owned, ranks - 1, -1)
    tiles = (jnp.max(ranks[:, :, -1], axis=1) + tile_units - 1) // tile_units
    lens = lax.dynamic_slice_in_dim(lengths, beam * local_slots, local_slots, 0)
    places = (place + jnp.arange(count, dtype=jnp.int32)) % count
    ids = ring_member(places, count)
    own_chain = lax.dynamic_index_in_dim(chain, beam, 3, False)
    linked = own_chain[..., None] == jnp.arange(width, dtype=jnp.int32)
    linked = linked.reshape(2, half, 2, half, count, local_slots, count, local_slots)
    linked = jnp.transpose(linked, (0, 4, 1, 5, 2, 6, 3, 7)).reshape(units, units)
    fresh_bias = jnp.where(linked, 0.0, masked_score).astype(f32)

    info = jnp.concatenate([core.reshape(1), ids])
    sums = []
    for n in range(local):
        blocks = project(info, mine, other, w_qkv, n, local, prompts)
        front, back, mark = scatter_ring(blocks, count)
        sums.append((blocks[0], front, back))
    block = fetch_first(prompt_keys, prompt_values, mark)
    queries, fresh_keys, fresh_values = rotate(
        sums, qkv_bias.reshape(1, -1), cosine, sine, (block[0], fresh_bias, code)
    )

    def attend(state, block, piece):
        outs = prompt_piece(
            queries,
            (fresh_keys, fresh_values, fresh_bias),
            state,
            block,
            prompt_keys,
            prompt_values,
            piece,
            ids,
            (suffix_keys, suffix_values),
        )
        return outs[:2], outs[2:]

    state = None
    for piece in range(pieces - 1):
        state, block = attend(state, block, piece)
    gathered = gather_ring(queries, count, state[1])

    middle = count // 2
    held = [block]

    def members(step):
        return (step,) if step in (0, middle) else (step, count - step)

    def produce(step, after):
        made, held[0] = suffix_attention(
            (tiles, lens, ids, code),
            gathered,
            members(step),
            members(step - 1) if step > 1 else members(middle) if step == 0 else (),
            step == middle,
            held[0],
            (prompt_keys, prompt_values) if step == 1 else (suffix_keys, suffix_values),
            after,
        )
        return made

    (own,) = produce(0, ())
    front, back = return_ring(produce, (), count)
    state, _ = attend(state, held[0], pieces - 1)
    sums = (own, front, back)
    contexts = merge(state, sums, local)

    per = prompts // heads
    chips = heads // 2
    targets = ids // per
    away = (targets % 2) ^ core
    turn = (targets // 2 - head // 2) % chips
    info = jnp.stack([away, turn * per + ids % per]).astype(jnp.int32)
    late = (middle,)
    early = tuple(j for j in range(count) if j not in late)
    contexts = [gather_ring(context, count) for context in contexts]
    *held, w_held = output(info, contexts, early, (0, 1), w_out, chips * per, None)
    rows = per * units
    terms = []
    for h in range(2):
        keep, send = output(
            info, contexts, late, (h,), w_held, chips * per, held[2 * h : 2 * h + 2]
        )
        came = lax.ppermute(send, "head", partner)
        terms += [keep, came]
        for i in range(1, chips):
            at = slice(i * rows, (i + 1) * rows)
            far = (keep[at].astype(f32) + came[at].astype(f32)).astype(bf16)
            pairs = [(j, (j + 2 * i) % heads) for j in range(heads)]
            terms.append(lax.ppermute(far, "head", pairs))
    result = finish(terms, rows, steps, local_slots, count)
    return result.reshape(steps, width, per, result.shape[1])


def solution(mesh):
    return jax.shard_map(
        shards,
        mesh=mesh,
        in_specs=(
            P(None, "beam", None, None),
            P("beam", "head"),
            P("head"),
            P("beam", "head", None, None),
            P("beam", "head", None, None),
            P("beam", None, "head", None, None),
            P("beam", None, "head", None, None),
            P("head", "beam"),
            P(),
            P(),
        ),
        out_specs=P(None, None, "head", "beam"),
        check_vma=False,
    )
```
